32 devices in a mesh: seq: 4 (over y, x), batch: 8 (over z, core).
Axes of the slice: x: 2, y: 2, z: 4, core: 2. Of those that a mesh axis runs over, the one named last changes fastest.
Arguments:
- inputs: float32 [16, 1024, 768], P('batch', 'seq'), may hold values from -6 to 6
- gain_one: float32 [768], P(('seq', 'batch')), may hold values from 0.1 to 1.9
- w_in: float32 [768, 2304], P(('seq', 'batch')), may hold values from -0.21875 to 0.21875
- conv_weight: float32 [3, 2304], P(None, ('seq', 'batch')), may hold values from -3 to 3
- kernel: float32 [2, 2048, 768], P(None, 'batch', 'seq'), may hold values from -6 to 6
- w_out: float32 [768, 768], P(('seq', 'batch')), may hold values from -0.21875 to 0.21875
- gain_two: float32 [768], P(('seq', 'batch')), may hold values from 0.1 to 1.9
- w_gate: float32 [768, 3072], P(('seq', 'batch')), may hold values from -0.21875 to 0.21875
- w_up: float32 [768, 3072], P(('seq', 'batch')), may hold values from -0.21875 to 0.21875
- w_down: float32 [3072, 768], P(('seq', 'batch')), may hold values from -0.109375 to 0.109375
- mask_positions: int32 [16, 80], P('batch'), may hold values from 0 to 1023, as said below
- mask_counts: int32 [16], P('batch'), may hold values from 1 to 80, as said below
- grad_rows: float32 [16, 80, 768], P('batch'), may hold values from -6 to 6
Outputs:
- outputs: float32 [16, 1024, 768], P('batch', 'seq')
- input_grad: float32 [16, 1024, 768], P('batch', 'seq')
- gain_one_grad: float32 [768], P(('seq', 'batch'))
- w_in_grad: float32 [768, 2304], P(('seq', 'batch'))
- conv_weight_grad: float32 [3, 2304], P(None, ('seq', 'batch'))
- kernel_grad: float32 [2, 2048, 768], P(None, 'batch', 'seq')
- w_out_grad: float32 [768, 768], P(('seq', 'batch'))
- gain_two_grad: float32 [768], P(('seq', 'batch'))
- w_gate_grad: float32 [768, 3072], P(('seq', 'batch'))
- w_up_grad: float32 [768, 3072], P(('seq', 'batch'))
- w_down_grad: float32 [3072, 768], P(('seq', 'batch'))
The draws below stay inside these ranges and needn't reach their ends.
Inputs may be any that keep to these rules, and one draw needn't show every extreme that they name: `mask_positions`: the 80 entries of a row are distinct positions of that sequence; only the first mask_counts of them are live. `mask_counts`: in each aligned block of 2 sequences one row has 4 or more live positions; some row of the batch has 80.
All inputs are finite; a program needn't handle non-finite values.
Results may differ from the reference program's by a relative error of at most 0.0003.
Values sent between devices are 32-bit elements; how exact they have to be, the bound alone decides.
No kernel may reach another device: no remote copies, remote signals or barrier semaphores. Data moves between devices by JAX's collectives and lax.ppermute only.
A program may use at most 256 MiB of HBM per device.

```python
import math
import jax
import jax.numpy as jnp
from jax import lax

D = 768
FF = 3072
SEQ_LEN = 1024
SEQS_DEV = 2
MASKED = 80
BATCH = 16
FREQS = 2048
N_SEQ = 4


def chosen_rows(key):
    owners = jax.random.randint(key, (BATCH // SEQS_DEV,), 0, SEQS_DEV)
    within = jnp.arange(BATCH, dtype=jnp.int32) % SEQS_DEV
    return within == jnp.repeat(owners, SEQS_DEV, total_repeat_length=BATCH)


def draw_mask_counts(key, part):
    chosen = chosen_rows(key)
    key = jax.random.fold_in(key, 11)
    drawn_key, strong_key, top_key = jax.random.split(key, 3)
    counts = jax.random.randint(drawn_key, (BATCH,), 1, MASKED + 1)
    strong = jax.random.randint(strong_key, (BATCH,), N_SEQ, MASKED + 1)
    counts = jnp.where(chosen, strong, counts)
    top_row = jax.random.randint(top_key, (), 0, BATCH)
    row_index = jnp.arange(BATCH, dtype=jnp.int32)
    return jnp.where(row_index == top_row, MASKED, counts).astype(jnp.int32)


def full_order(single_key):
    return jax.random.permutation(single_key, SEQ_LEN)[:MASKED]


def shard_order(single_key):
    return jax.random.permutation(single_key, SEQ_LEN // N_SEQ)


def draw_mask_positions(key, part):
    chosen = chosen_rows(key)
    key = jax.random.fold_in(key, 12)
    free_key, strat_key = jax.random.split(key)
    shuffled = jax.vmap(full_order)(jax.random.split(free_key, BATCH))
    inner_order = jax.vmap(shard_order)(jax.random.split(strat_key, BATCH))
    slot_index = jnp.arange(MASKED, dtype=jnp.int32)
    spread_rows = slot_index % N_SEQ * (SEQ_LEN // N_SEQ) + inner_order[:, slot_index // N_SEQ]
    return jnp.where(chosen[:, None], spread_rows, shuffled).astype(jnp.int32)


def steps_of(rng, extent, cuts, smallest, high):
    gain, own = 1.0, jax.random.fold_in(rng, 6)
    for position, shards_of in cuts:
        draws = jnp.exp(jax.random.uniform(jax.random.fold_in(own, position), (shards_of,), jnp.float32, smallest / len(cuts), high / len(cuts)))
        gain = gain * jnp.repeat(draws, extent[position] // shards_of).reshape([-1 if axis == position else 1 for axis in range(len(extent))])
    return gain


def bell_draw(key, extent, width, limit, shards=(), held_as=jnp.bfloat16):
    entries = width * jax.random.normal(key, extent, jnp.float32)
    if shards:
        entries = entries * steps_of(key, extent, shards, -0.22, 0.18)
    return jnp.clip(entries, -limit, limit).astype(held_as)


def setup_inputs(seed: int = 0) -> dict:
    splits = jax.random.split(jax.random.key(seed), 14)
    return {
        "inputs": bell_draw(splits[0], (BATCH, SEQ_LEN, D), 1.0, 6.0, ((0, 8), (1, 4)), jnp.float32),
        "gain_one": jnp.clip(1.0 + 0.18 * jax.random.normal(splits[1], (D,), jnp.float32), 0.1, 1.9),
        "w_in": bell_draw(splits[2], (D, 3 * D), D ** -0.5, 0.21875, ((0, 32),), jnp.float32),
        "conv_weight": bell_draw(splits[3], (3, 3 * D), 0.6, 3.0, ((1, 32),), jnp.float32),
        "kernel": bell_draw(splits[4], (2, FREQS, D), 1.0, 6.0, ((1, 8), (2, 4)), jnp.float32),
        "w_out": bell_draw(splits[5], (D, D), D ** -0.5, 0.21875, ((0, 32),), jnp.float32),
        "gain_two": jnp.clip(1.0 + 0.18 * jax.random.normal(splits[6], (D,), jnp.float32), 0.1, 1.9),
        "w_gate": bell_draw(splits[7], (D, FF), D ** -0.5, 0.21875, ((0, 32),), jnp.float32),
        "w_up": bell_draw(splits[8], (D, FF), D ** -0.5, 0.21875, ((0, 32),), jnp.float32),
        "w_down": bell_draw(splits[9], (FF, D), FF ** -0.5, 0.109375, ((0, 32),), jnp.float32),
        "mask_positions": draw_mask_positions(jax.random.fold_in(splits[13], 71), 0),
        "mask_counts": draw_mask_counts(jax.random.fold_in(splits[13], 71), 0),
        "grad_rows": bell_draw(splits[12], (BATCH, MASKED, D), 1.0, 6.0, ((0, 8),), jnp.float32),
    }


eps = 1e-05

@jax.custom_vjp
def low(v):
    return lax.optimization_barrier(v.astype(jnp.bfloat16)).astype(jnp.float32)

@jax.custom_vjp
def low_back(v):
    return v

def low_keep(v):
    return (low(v), None)

def low_pass(kept, grad):
    return (grad,)

def back_keep(v):
    return (v, None)

def back_low(kept, grad):
    return (low(grad),)
low.defvjp(low_keep, low_pass)
low_back.defvjp(back_keep, back_low)

def layer_norm(values, norm_gain):
    centered = values - lax.optimization_barrier(jnp.mean(values, axis=-1, keepdims=True))
    spread = lax.optimization_barrier(jnp.mean(centered * centered, axis=-1, keepdims=True))
    return centered * lax.rsqrt(spread + eps) * norm_gain

def matmul(left_side, right_side):
    return jnp.einsum('td,de->te', left_side, right_side, precision=lax.Precision.HIGHEST)

def forward(sequence, gain_one, w_in, conv_weight, kernel, w_out, gain_two, w_gate, w_up, w_down):
    projected = matmul(layer_norm(sequence, gain_one), w_in)
    padded = jnp.pad(projected, ((1, 1), (0, 0)))
    mixed = conv_weight[0] * padded[:-2] + conv_weight[1] * padded[1:-1] + conv_weight[2] * padded[2:]
    signal, gating, values = jnp.split(mixed, 3, axis=-1)
    signal_hat = jnp.fft.fft(signal, n=FREQS, axis=0)
    values_hat = jnp.fft.fft(values, n=FREQS, axis=0)
    spectrum = kernel[0] + 1j * kernel[1] + signal_hat / math.sqrt(SEQ_LEN)
    long_conv = jnp.real(jnp.fft.ifft(spectrum * values_hat, axis=0))[:SEQ_LEN]
    residual = sequence + matmul(gating * long_conv, w_out)
    normed_two = layer_norm(residual, gain_two)
    hidden = jax.nn.gelu(matmul(normed_two, w_gate), approximate=True) * matmul(normed_two, w_up)
    return residual + matmul(hidden, w_down)

def reference(inputs, gain_one, w_in, conv_weight, kernel, w_out, gain_two, w_gate, w_up, w_down, mask_positions, mask_counts, grad_rows):
    weights = (gain_one, w_in, conv_weight, kernel, w_out, gain_two, w_gate, w_up, w_down)

    def one_sequence(totals, pieces):
        sequence, positions, live_count, row_values = pieces
        result, pullback = jax.vjp(forward, sequence, *weights)
        slot_index = jnp.arange(MASKED, dtype=jnp.int32)
        live = (slot_index < live_count).astype(row_values.dtype)
        cotangent = jnp.zeros((SEQ_LEN, row_values.shape[1]), row_values.dtype).at[positions].add(row_values * live[:, None])
        gradients = pullback(cotangent)
        totals = jax.tree.map(jnp.add, totals, tuple(gradients[1:]))
        return (totals, (result, gradients[0]))
    starting = jax.tree.map(jnp.zeros_like, weights)
    totals, (outputs, input_grad) = lax.scan(one_sequence, starting, (inputs, mask_positions, mask_counts, grad_rows))
    return (outputs, input_grad, totals[0], totals[1], totals[2], totals[3], totals[4], totals[5], totals[6], totals[7], totals[8])
```

```python
import math

import jax
import jax.numpy as jnp
import numpy as np
from jax import lax
from jax.sharding import PartitionSpec as P

EPS = 1e-05
HIGH = lax.Precision.HIGH
RADIX = 8
FOLDED = 5


def contract(pattern, left_side, right_side):
    return jnp.einsum(pattern, left_side, right_side, precision=HIGH)


def swap(value, axis, distance):
    devices = lax.axis_size(axis)
    return lax.ppermute(value, axis, [(i, i ^ distance) for i in range(devices)])


def gather_pieces(value, axis, dim):
    half = value.shape[dim] // 2
    first = lax.slice_in_dim(value, 0, half, axis=dim)
    second = lax.slice_in_dim(value, half, 2 * half, axis=dim)
    first_one = swap(first, axis, 1)
    second_two = swap(second, axis, 2)
    first_two = swap(first, axis, 2)
    second_one = swap(second, axis, 1)
    first_three = swap(first_one, axis, 2)
    second_three = swap(second_two, axis, 1)
    return (
        value,
        jnp.concatenate([first_one, second_one], axis=dim),
        jnp.concatenate([first_two, second_two], axis=dim),
        jnp.concatenate([first_three, second_three], axis=dim),
    )


def scatter_pieces(pieces, axis, dim):
    half = pieces[0].shape[dim] // 2
    first = [lax.slice_in_dim(p, 0, half, axis=dim) for p in pieces]
    second = [lax.slice_in_dim(p, half, 2 * half, axis=dim) for p in pieces]
    first_three = swap(first[3], axis, 2)
    second_three = swap(second[3], axis, 1)
    first_two = swap(first[2], axis, 2)
    second_one = swap(second[1], axis, 1)
    first_one = swap(first[1] + first_three, axis, 1)
    second_two = swap(second[2] + second_three, axis, 2)
    return jnp.concatenate(
        [first[0] + first_two + first_one, second[0] + second_one + second_two], axis=dim
    )


def normalize(values):
    centered = values - jnp.mean(values, axis=-1, keepdims=True)
    inverse = lax.rsqrt(jnp.mean(centered * centered, axis=-1, keepdims=True) + EPS)
    return centered * inverse, inverse


def norm_pull(normed, inverse, grad):
    along = jnp.mean(grad * normed, axis=-1, keepdims=True)
    return (grad - jnp.mean(grad, axis=-1, keepdims=True) - normed * along) * inverse


def phase_tables(length):
    block = length // RADIX
    place = np.arange(block)[:, None]
    turn = np.arange(block)[None, :]
    forward, backward = [], []
    for phase in range(FOLDED):
        angle = 2.0 * np.pi * ((RADIX * turn + phase) * place % length) / length
        cos, sin = np.cos(angle), np.sin(angle)
        forward.append(np.block([[cos, -sin], [sin, cos]]))
        backward.append(np.block([[cos.T, sin.T], [-sin.T, cos.T]]))
    as_f32 = lambda t: jnp.asarray(np.stack(t).astype(np.float32))
    return as_f32(forward), as_f32(backward)


def dft(value, tables):
    block = tables.shape[1] // 2
    x0, x1, x2, x3 = [value[..., i * block : (i + 1) * block] for i in range(4)]
    root = math.sqrt(0.5)
    even, odd = x0 + x2, x1 + x3
    diff, tail = x0 - x2, (x1 - x3)
    slant, lean = tail * root, odd * root
    parts = [
        (even + odd, None),
        (x0 + slant, -x2 - lean),
        (diff, -tail),
        (x0 - slant, x2 - lean),
        (even - odd, None),
    ]
    out = []
    for phase, (real, imag) in enumerate(parts):
        if imag is None:
            out.append(contract("bck,kf->bcf", real, tables[phase, :block]))
        else:
            both = jnp.concatenate([real, imag], axis=-1)
            out.append(contract("bck,kf->bcf", both, tables[phase]))
    return out


def inverse_dft(spectra, tables):
    block = tables.shape[1] // 2
    root = math.sqrt(0.5)
    v0 = contract("bcf,fk->bck", spectra[0], tables[0, :, :block])
    v4 = contract("bcf,fk->bck", spectra[4], tables[4, :, :block])
    reals, imags = [None], [None]
    for phase in (1, 2, 3):
        both = contract("bcf,fk->bck", spectra[phase], tables[phase])
        reals.append(both[..., :block])
        imags.append(both[..., block:])
    _, r1, r2, r3 = reals
    _, i1, i2, i3 = imags
    plus, minus = v0 + v4, v0 - v4
    return jnp.concatenate(
        [
            plus + r1 + r2 + r3,
            minus - i2 + root * ((r1 - i1) - (r3 + i3)),
            plus - r2 - i1 + i3,
            minus + i2 + root * ((r3 - i3) - (r1 + i1)),
        ],
        axis=-1,
    )


def split_complex(value):
    block = value.shape[-1] // 2
    return value[..., :block], value[..., block:]


def times(left_side, right_side, conj=False):
    a, b = split_complex(left_side)
    c, d = split_complex(right_side)
    if conj:
        d = -d
    return jnp.concatenate([a * c - b * d, a * d + b * c], axis=-1)


def shift(value, step):
    zero = jnp.zeros_like(value[..., :1])
    if step < 0:
        return jnp.concatenate([zero, value[..., :-1]], axis=-1)
    return jnp.concatenate([value[..., 1:], zero], axis=-1)


def body(
    inputs,
    gain_one,
    w_in,
    conv_weight,
    kernel,
    w_out,
    gain_two,
    w_gate,
    w_up,
    w_down,
    mask_positions,
    mask_counts,
    grad_rows,
):
    shards = lax.axis_size("seq")
    groups = lax.axis_size("batch")
    s = lax.axis_index("seq")
    seqs, tokens, width = inputs.shape
    length = tokens * shards
    freqs = 2 * length
    block = freqs // RADIX
    own = width // shards
    rows = w_in.shape[0]
    hidden_own = w_gate.shape[1] // shards
    scale = 1.0 / math.sqrt(length)
    forward, backward = phase_tables(freqs)

    def columns(shard, blocks):
        wide = shard.reshape(rows, blocks, shards, -1)
        wide = lax.all_to_all(wide, "seq", split_axis=2, concat_axis=0, tiled=True)
        wide = wide.reshape(1, shards, rows, -1)
        full = lax.all_gather(wide, "batch", axis=0, tiled=True)
        return full.transpose(1, 0, 2, 3).reshape(width, -1)

    def columns_back(grad, blocks):
        parts = grad.reshape(shards, groups, rows, -1).transpose(1, 0, 2, 3)
        mine = lax.psum_scatter(parts, "batch", scatter_dimension=0, tiled=True)
        mine = mine.reshape(shards * rows, blocks, 1, -1)
        mine = lax.all_to_all(mine, "seq", split_axis=0, concat_axis=2, tiled=True)
        return mine.reshape(rows, -1)

    x_pieces = gather_pieces(inputs, "seq", 1)
    w_pre = columns(gain_one[:, None] * w_in, 3)
    taps_all = lax.all_gather(conv_weight, ("seq", "batch"), axis=1, tiled=True)
    taps = lax.dynamic_slice_in_dim(taps_all.reshape(3, 3, shards, own), s, 1, axis=2).reshape(3, 3 * own)

    wide = kernel.reshape(2, -1, RADIX, own)
    mirror = [(i, groups - 1 - i) for i in range(groups)]
    folded = lax.ppermute(wide[:, ::-1, :4:-1], "batch", mirror)
    folded = jnp.stack([wide[0, :, 1:4] + folded[0], wide[1, :, 1:4] - folded[1]])
    folded = jnp.concatenate([wide[:, :, :1], folded, wide[:, :, 4:5]], axis=2)
    folded = folded.transpose(2, 3, 0, 1)
    base = lax.all_gather(folded, "batch", axis=3, tiled=True).reshape(FOLDED, own, 2 * block)

    w_out_rows = lax.all_gather(w_out, "batch", axis=0, tiled=True)
    w_out_rel = jnp.concatenate(gather_pieces(w_out_rows, "seq", 0), axis=0)
    w_gate_own = columns(gain_two[:, None] * w_gate, 1)
    w_up_own = columns(gain_two[:, None] * w_up, 1)
    w_down_own = lax.all_gather(w_down, "batch", axis=0, tiled=True)

    x = jnp.zeros((seqs, length, width), jnp.float32)
    for d, piece in enumerate(x_pieces):
        x = lax.dynamic_update_slice(x, piece, (0, (s ^ d) * tokens, 0))
    n_one, _ = normalize(x)
    projected = contract("btd,dc->bct", n_one, w_pre)
    tap = taps[:, None, :, None]
    mixed = tap[0] * shift(projected, -1) + tap[1] * projected + tap[2] * shift(projected, 1)
    signal, gating, values = mixed[:, :own], mixed[:, own : 2 * own], mixed[:, 2 * own :]

    signal_hat = dft(signal, forward)
    values_hat = dft(values, forward)
    spectrum = []
    for phase in range(FOLDED):
        weight = scale if phase in (0, 4) else 2.0 * scale
        spectrum.append(base[phase] + weight * signal_hat[phase])
    products = [times(a, b) for a, b in zip(spectrum, values_hat)]
    long_conv = inverse_dft(products, backward) / freqs

    gated = gating * long_conv
    gated_rel = jnp.concatenate(gather_pieces(gated, "seq", 2), axis=1)
    residual = x + contract("bct,cd->btd", gated_rel, w_out_rel)

    slot = jnp.arange(mask_positions.shape[1], dtype=jnp.int32)
    live = slot[None, :] < mask_counts[:, None]
    places = jnp.arange(length, dtype=jnp.int32)
    select = ((mask_positions[:, :, None] == places) & live[:, :, None]).astype(jnp.float32)
    d_out = jnp.where(live[:, :, None], grad_rows, 0.0)

    n_two, _ = normalize(residual)
    gate = contract("btd,df->btf", n_two, w_gate_own)
    up = contract("btd,df->btf", n_two, w_up_own)
    hidden = jax.nn.gelu(gate, approximate=True) * up
    down = contract("btf,fd->btd", hidden, w_down_own)
    down_pieces = [
        lax.dynamic_slice_in_dim(down, (s ^ d) * tokens, tokens, axis=1) for d in range(4)
    ]
    outputs = scatter_pieces(down_pieces, "seq", 1)
    outputs = outputs + lax.dynamic_slice_in_dim(residual, s * tokens, tokens, axis=1)

    n_live, inverse_live = normalize(contract("bmt,btd->bmd", select, residual))

    def gated_unit(g, u):
        return jax.nn.gelu(g, approximate=True) * u

    hidden_live, unit_pull = jax.vjp(
        gated_unit,
        contract("bmd,df->bmf", n_live, w_gate_own),
        contract("bmd,df->bmf", n_live, w_up_own),
    )
    d_hidden = contract("bmd,fd->bmf", d_out, w_down_own)
    d_gate, d_up = unit_pull(d_hidden)
    w_down_part = contract("bmf,bmd->fd", hidden_live, d_out)
    w_gate_part = contract("bmd,bmf->df", n_live, d_gate)
    w_up_part = contract("bmd,bmf->df", n_live, d_up)
    e_two = contract("bmf,df->bmd", d_gate, w_gate_own) + contract("bmf,df->bmd", d_up, w_up_own)
    e_two = e_two + swap(e_two, "seq", 1)
    e_two = e_two + swap(e_two, "seq", 2)
    d_residual = d_out + norm_pull(n_live, inverse_live, e_two)
    w_out_own = w_out_rows
    d_gated = contract("bmd,cd->bmc", d_residual, w_out_own)
    gating_live = contract("bmt,bct->bmc", select, gating)
    long_live = contract("bmt,bct->bmc", select, long_conv)
    w_out_part = contract("bmc,bmd->cd", gating_live * long_live, d_residual)
    d_gating = contract("bmt,bmc->bct", select, d_gated * long_live)
    d_long = contract("bmt,bmc->bct", select, d_gated * gating_live)

    grad_hat = [g / freqs for g in dft(d_long, forward)]
    kernel_hat = [times(g, v, conj=True) for g, v in zip(grad_hat, values_hat)]
    kernel_part = jnp.stack([jnp.sum(k, axis=0) for k in kernel_hat])
    d_signal_hat = [
        k * (scale if phase in (0, 4) else 2.0 * scale) for phase, k in enumerate(kernel_hat)
    ]
    d_values_hat = [times(g, k, conj=True) for g, k in zip(grad_hat, spectrum)]
    d_signal = inverse_dft(d_signal_hat, backward)
    d_values = inverse_dft(d_values_hat, backward)
    d_mixed = jnp.concatenate([d_signal, d_gating, d_values], axis=1)
    taps_part = jnp.stack(
        [
            jnp.sum(shift(projected, -1) * d_mixed, axis=(0, 2)),
            jnp.sum(projected * d_mixed, axis=(0, 2)),
            jnp.sum(shift(projected, 1) * d_mixed, axis=(0, 2)),
        ]
    )
    d_projected = tap[0] * shift(d_mixed, 1) + tap[1] * d_mixed + tap[2] * shift(d_mixed, -1)
    w_in_part = contract("btd,bct->dc", n_one, d_projected)
    e_one = contract("bct,dc->btd", d_projected, w_pre)
    e_pieces = [
        lax.dynamic_slice_in_dim(e_one, (s ^ d) * tokens, tokens, axis=1) for d in range(4)
    ]
    e_own = scatter_pieces(e_pieces, "seq", 1)
    n_own, inverse_own = normalize(inputs)
    select_own = lax.dynamic_slice_in_dim(select, s * tokens, tokens, axis=2)
    input_grad = norm_pull(n_own, inverse_own, e_own) + contract("bmt,bmd->btd", select_own, d_residual)

    w_down_sum = lax.psum_scatter(w_down_part, "batch", scatter_dimension=0, tiled=True)
    w_gate_sum = columns_back(w_gate_part, 1)
    w_up_sum = columns_back(w_up_part, 1)
    w_out_sum = lax.psum_scatter(w_out_part, "batch", scatter_dimension=0, tiled=True)
    w_in_sum = columns_back(w_in_part, 3)
    gain_one_sum = jnp.sum(w_in * w_in_sum, axis=1)
    gain_two_sum = jnp.sum(w_gate * w_gate_sum, axis=1) + jnp.sum(w_up * w_up_sum, axis=1)

    placed = jnp.zeros((3, 3, shards, own), jnp.float32)
    placed = lax.dynamic_update_slice(placed, taps_part.reshape(3, 3, 1, own), (0, 0, s, 0))
    taps_sum = lax.psum_scatter(
        placed.reshape(3, 3 * width), ("seq", "batch"), scatter_dimension=1, tiled=True
    )

    kernel_part = kernel_part.reshape(FOLDED, own, 2, block)
    kernel_sum = lax.psum_scatter(kernel_part, "batch", scatter_dimension=3, tiled=True)
    kernel_sum = kernel_sum.transpose(2, 3, 0, 1)
    mirrored = lax.ppermute(kernel_sum[:, ::-1, 3:0:-1], "batch", mirror)
    mirrored = jnp.stack([mirrored[0], -mirrored[1]])
    kernel_grad = jnp.concatenate([kernel_sum, mirrored], axis=2).reshape(kernel.shape)

    return (
        outputs,
        input_grad,
        gain_one_sum,
        gain_one[:, None] * w_in_sum,
        taps_sum,
        kernel_grad,
        w_out_sum,
        gain_two_sum,
        gain_two[:, None] * w_gate_sum,
        gain_two[:, None] * w_up_sum,
        w_down_sum,
    )


def solution(mesh):
    split = ("seq", "batch")
    placed = (
        P("batch", "seq", None),
        P(split),
        P(split, None),
        P(None, split),
        P(None, "batch", "seq"),
        P(split, None),
        P(split),
        P(split, None),
        P(split, None),
        P(split, None),
        P("batch", None),
        P("batch"),
        P("batch", None, None),
    )
    return jax.shard_map(
        body,
        mesh=mesh,
        in_specs=placed,
        out_specs=(
            P("batch", "seq", None),
            P("batch", "seq", None),
            P(split),
            P(split, None),
            P(None, split),
            P(None, "batch", "seq"),
            P(split, None),
            P(split),
            P(split, None),
            P(split, None),
            P(split, None),
        ),
        check_vma=False,
    )
```

```python
import math

import jax
import jax.numpy as jnp
import numpy as np
from jax import lax
from jax.experimental import pallas as pl
from jax.experimental.pallas import tpu as pltpu
from jax.sharding import PartitionSpec as P

EPS = 1e-05
HIGH = lax.Precision.HIGH
RADIX = 8
FOLDED = 5
ROOT = math.sqrt(0.5)
VMEM = 56 * 1024 * 1024
COST = 20
NN = ((1,), (0,))
NT = ((1,), (1,))
TN = ((0,), (0,))
F32 = jnp.float32
BF16 = jnp.bfloat16


def contract(pattern, left_side, right_side):
    return jnp.einsum(pattern, left_side, right_side, precision=HIGH)


def swap(value, axis, distance):
    devices = lax.axis_size(axis)
    return lax.ppermute(value, axis, [(i, i ^ distance) for i in range(devices)])


def from_others(value):
    return [swap(value, "seq", d) for d in (1, 2, 3)]


def to_others(blocks):
    return [blocks[0]] + [swap(blocks[d], "seq", d) for d in (1, 2, 3)]


def to_all(value):
    return [value] + from_others(value)


def added(terms):
    return (terms[0] + terms[1]) + (terms[2] + terms[3])


def by_xor(pieces, index):
    count = len(pieces)
    out = []
    for k in range(count):
        chosen = pieces[k]
        for i in range(1, count):
            chosen = jnp.where(index == i, pieces[k ^ i], chosen)
        out.append(chosen)
    return out


def columns_out(shard, s):
    pieces = []
    for d in range(4):
        block = lax.dynamic_index_in_dim(shard, s ^ d, axis=1, keepdims=False)
        pieces.append(block if d == 0 else swap(block, "seq", d))
    return jnp.stack(by_xor(pieces, s))


def columns_there(own, s):
    pieces = []
    for d in range(4):
        block = lax.dynamic_index_in_dim(own, s ^ d, axis=0, keepdims=False)
        pieces.append(block if d == 0 else swap(block, "seq", d))
    return pieces


def over_batch(value):
    full = lax.all_gather(value, "batch", axis=0, tiled=True)
    return full.reshape((-1,) + value.shape)


def sum_over_batch(parts):
    flat = parts.reshape(-1, parts.shape[2])
    return lax.psum_scatter(flat, "batch", scatter_dimension=0, tiled=True)


def halves(value):
    high = value.astype(BF16)
    return high, (value - high.astype(F32)).astype(BF16)


def dot(left_side, right_side, dims):
    (a, b), (c, d) = left_side, right_side

    def product(x, y):
        return lax.dot_general(x, y, (dims, ((), ())), preferred_element_type=F32)

    return product(a, c) + (product(a, d) + product(b, c))


def chosen_rows(chosen, both, dims):
    high, low = both

    def product(x):
        return lax.dot_general(chosen, x, (dims, ((), ())), preferred_element_type=F32)

    return product(high) + product(low)


def normed(x):
    centered = x - jnp.mean(x, axis=-1, keepdims=True)
    inverse = lax.rsqrt(jnp.mean(centered * centered, axis=-1, keepdims=True) + EPS)
    return centered * inverse, inverse


def call(kernel, name, flops, moved, inputs, in_specs, outs, out_specs, grid=(1,), scratch=(), scalars=(), after=()):
    taken = len(scalars) + len(inputs)

    def run(*refs):
        kernel(*refs[:taken], *refs[taken + len(after) :])

    return pl.pallas_call(
        run,
        name=name,
        out_shape=tuple(outs),
        grid_spec=pltpu.PrefetchScalarGridSpec(
            num_scalar_prefetch=len(scalars),
            grid=grid,
            in_specs=list(in_specs) + [pl.BlockSpec(memory_space=pl.ANY)] * len(after),
            out_specs=tuple(out_specs),
            scratch_shapes=list(scratch),
        ),
        compiler_params=pltpu.CompilerParams(vmem_limit_bytes=VMEM),
        cost_estimate=pl.CostEstimate(flops=int(flops) // COST, bytes_accessed=int(moved) // COST, transcendentals=0),
    )(*scalars, *inputs, *after)


def shaped(*shape, dtype=F32):
    return jax.ShapeDtypeStruct(shape, dtype)


def whole(*shape):
    return pl.BlockSpec(shape, lambda *_: (0,) * len(shape))


def first(work):
    pl.when(pl.program_id(0) == 0)(work)


def fold_base(kernel, mirrored, w_out, after=()):
    _, turns, kept, own = mirrored.shape
    rows, width = w_out.shape
    wide = 2 * own

    def run(k_ref, m_ref, w_ref, out_ref):
        for phase in range(FOLDED):
            for part in range(2):
                value = k_ref[part, :, phase]
                if 0 < phase <= kept:
                    other = m_ref[part, :, phase - 1]
                    value = value + other if part == 0 else value - other
                out_ref[phase * turns : (phase + 1) * turns, part * own : (part + 1) * own] = value
        for k in range(width // wide):
            at = FOLDED * turns + k * rows
            out_ref[at : at + rows] = w_ref[:, k * wide : (k + 1) * wide]

    count = FOLDED * turns + width // wide * rows
    (out,) = call(
        run, "fold_base", 0, 12 * count * wide, [kernel, mirrored, w_out],
        [whole(*kernel.shape), whole(*mirrored.shape), whole(rows, width)],
        [shaped(count, wide)], [whole(count, wide)], after=after,
    )
    return out


def turn_in(gathered, channels):
    groups, shards, rows, columns = gathered.shape
    width = groups * shards * rows
    wide = -(-columns // 128) * 128

    def kernel(w_ref, high_ref, low_ref, flat_ref):
        flat_ref[:, channels // 128 * 128 :] = jnp.zeros((width, wide - channels // 128 * 128), F32)
        for k in range(shards):
            for j in range(groups):
                at = (k * groups + j) * rows
                flat_ref[at : at + rows, :channels] = w_ref[j, k, :, :channels]
        turned = flat_ref[...].T
        high_ref[...], low_ref[...] = halves(turned[:channels])

    return call(
        kernel, "turn_in", 0, 4 * 2 * width * wide, [gathered], [whole(*gathered.shape)],
        [shaped(channels, width, dtype=BF16)] * 2, [whole(channels, width)] * 2,
        scratch=[pltpu.VMEM((width, wide), F32)],
    )


def split_units(gathered, w_down, after=()):
    groups, shards, rows, columns = gathered.shape
    width = groups * shards * rows
    units = w_down.shape[0]

    def kernel(w_ref, d_ref, high_ref, low_ref, dh_ref, dl_ref, flat_ref):
        k = pl.program_id(0)
        for j in range(groups):
            flat_ref[j * rows : (j + 1) * rows] = w_ref[j, 0]

        high_ref[...], low_ref[...] = halves(flat_ref[...])
        dh_ref[...], dl_ref[...] = halves(d_ref[...])

    part = pl.BlockSpec((groups * rows, columns), lambda i: (i, 0))
    down = pl.BlockSpec((units // shards, width), lambda i: (i, 0))
    return call(
        kernel, "split_units", 0, 8 * width * (columns + units), [gathered, w_down],
        [pl.BlockSpec((groups, 1, rows, columns), lambda i: (0, i, 0, 0)), down],
        [shaped(width, columns, dtype=BF16)] * 2 + [shaped(units, width, dtype=BF16)] * 2,
        [part, part, down, down], grid=(shards,),
        scratch=[pltpu.VMEM((groups * rows, columns), F32)], after=after,
    )


def arrange(pieces, s, after=()):
    tokens, width = pieces[0].shape
    length = 4 * tokens

    def kernel(s_ref, p0, p1, p2, p3, x_ref, high_ref, low_ref):
        for d, piece in enumerate((p0, p1, p2, p3)):

            @pl.when(pl.program_id(0) == d)
            def _(piece=piece):
                x = piece[...]
                x_ref[...] = x
                high_ref[...], low_ref[...] = halves(normed(x)[0])

    rows = pl.BlockSpec((tokens, width), lambda i, s_ref: (s_ref[0] ^ i, 0))
    return call(
        kernel, "arrange", 0, 12 * length * width, pieces, [whole(tokens, width)] * 4,
        [shaped(length, width), shaped(length, width, dtype=BF16), shaped(length, width, dtype=BF16)],
        [rows] * 3, grid=(4,), scalars=[s.reshape(1)], after=after,
    )


def project(w_turned, n_both, after=()):
    channels, width = w_turned[0].shape
    length = n_both[0].shape[0]
    tokens = length // 2

    def kernel(wh, wl, nh, nl, out_ref):
        out_ref[...] = dot((wh[...], wl[...]), (nh[...], nl[...]), NT)

    rows = pl.BlockSpec((tokens, width), lambda i: (i, 0))
    (out,) = call(
        kernel, "project", 6 * length * width * channels, 4 * (length * width + channels * (length + width)),
        [*w_turned, *n_both], [whole(channels, width)] * 2 + [rows] * 2,
        [shaped(channels, length)], [pl.BlockSpec((channels, tokens), lambda i: (0, i))], grid=(2,), after=after,
    )
    return out


def phase_tables(length):
    block = length // RADIX
    place = np.arange(block)[:, None]
    turn = np.arange(block)[None, :]
    tables = []
    for phase in range(FOLDED):
        angle = 2.0 * np.pi * ((RADIX * turn + phase) * place % length) / length
        cos, sin = np.cos(angle), np.sin(angle)
        tables.append(np.block([[cos, -sin], [sin, cos]]))
    table = np.stack(tables).astype(np.float32)
    high = table.astype(BF16)
    low = (table - high.astype(np.float32)).astype(BF16)
    return jnp.asarray(high), jnp.asarray(low)


def shift(value, step):
    length = value.shape[1]
    lane = lax.broadcasted_iota(jnp.int32, value.shape, 1)
    if step < 0:
        return jnp.where(lane == 0, 0.0, pltpu.roll(value, 1, 1))
    return jnp.where(lane == length - 1, 0.0, pltpu.roll(value, length - 1, 1))


def fold(value, phase, block):
    x0, x1, x2, x3 = [value[:, i * block : (i + 1) * block] for i in range(4)]
    if phase == 0:
        return (x0 + x2) + (x1 + x3)
    if phase == 4:
        return (x0 + x2) - (x1 + x3)
    if phase == 2:
        return jnp.concatenate([x0 - x2, x3 - x1], axis=1)
    slant, lean = (x1 - x3) * ROOT, (x1 + x3) * ROOT
    if phase == 1:
        return jnp.concatenate([x0 + slant, -x2 - lean], axis=1)
    return jnp.concatenate([x0 - slant, x2 - lean], axis=1)


def unfold(total_ref, value, phase, block):
    if phase == 0:
        terms = (value,) * 4
    elif phase == 4:
        terms = (value, -value, value, -value)
    else:
        real, imag = value[:, :block], value[:, block:]
        if phase == 2:
            terms = (real, -imag, -real, imag)
        elif phase == 1:
            terms = (real, ROOT * (real - imag), -imag, -ROOT * (real + imag))
        else:
            terms = (real, -ROOT * (real + imag), imag, ROOT * (real - imag))
    for i, term in enumerate(terms):
        cols = slice(i * block, (i + 1) * block)
        total_ref[:, cols] = term if phase == 0 else total_ref[:, cols] + term


def times(left_side, right_side, block, conj=False):
    a, b = left_side[:, :block], left_side[:, block:]
    c, d = right_side[:, :block], right_side[:, block:]
    if conj:
        d = -d
    return jnp.concatenate([a * c - b * d, a * d + b * c], axis=1)


def pair(phase):
    return 1.0 if phase in (0, 4) else 2.0


def depth(phase, block):
    return block if phase in (0, 4) else 2 * block


def mix(projected, taps, base, tables, after=()):
    own, length = projected.shape[1:]
    block = 2 * length // RADIX
    groups = base.shape[0]
    turns = block // groups
    if turns % 8:
        base = base[:, : FOLDED * turns].reshape(groups, FOLDED, turns, 2 * own)
        spectrum = pl.BlockSpec((groups, 1, turns, 2 * own), lambda i: (0, i, 0, 0))
    else:
        spectrum = pl.BlockSpec((groups, turns, 2 * own), lambda i: (0, i, 0))
    scale = 1.0 / math.sqrt(length)

    def kernel(p_ref, tap_ref, base_ref, th_ref, tl_ref, gated_ref, gating_ref, long_ref, vals_ref, spec_ref,
               mixed_ref, acc_ref, base_t):
        step = pl.program_id(0)

        @pl.when(step == 0)
        def _():
            for k in range(3):

                p = p_ref[k]
                tap = tap_ref[k]
                mixed = tap[:, 0:1] * shift(p, -1) + tap[:, 1:2] * p + tap[:, 2:3] * shift(p, 1)
                if k == 1:
                    gating_ref[...] = mixed
                else:
                    mixed_ref[k // 2 * own : (k // 2 + 1) * own] = mixed

        turned = base_ref[...].reshape(block, 2 * own).T
        base_t[:, :block] = turned[:own]
        base_t[:, block:] = turned[own:]

        for phase in range(FOLDED):

            @pl.when(step == phase)
            def _(phase=phase):
                deep = depth(phase, block)
                table = (th_ref[0, :deep], tl_ref[0, :deep])
                hats = dot(halves(fold(mixed_ref[...], phase, block)), table, NN)
                spec = base_t[...] + (pair(phase) * scale) * hats[:own]
                vals = hats[own:]
                spec_ref[0] = spec
                vals_ref[0] = vals
                unfold(acc_ref, dot(halves(times(spec, vals, block)), table, NT), phase, block)

        @pl.when(step == FOLDED - 1)
        def _():
            long_conv = acc_ref[...] * (0.5 / length)
            long_ref[...] = long_conv
            gated_ref[...] = gating_ref[...] * long_conv

    flat, hat = shaped(own, length), shaped(FOLDED, own, 2 * block)
    by_phase = lambda *shape: pl.BlockSpec((1,) + shape, lambda i, *_: (i,) + (0,) * len(shape))
    return call(
        kernel, "mix", 3 * 6 * own * 4 * length * length, 4 * own * length * 22,
        [projected, taps, base, *tables],
        [whole(3, own, length), whole(3, own, 3)]
        + [spectrum]
        + [by_phase(2 * block, 2 * block), by_phase(2 * block, 2 * block)],
        [flat, flat, flat, hat, hat],
        [whole(own, length)] * 3 + [by_phase(own, 2 * block)] * 2,
        grid=(FOLDED,),
        scratch=[
            pltpu.VMEM((2 * own, length), F32),
            pltpu.VMEM((own, length), F32),
            pltpu.VMEM((own, 2 * block), F32),
        ],
        after=after,
    )


def mix_back(which, places, d_gating, d_long, projected, taps, vals, spec, kernel_sum, tables, after=()):
    own, length = projected.shape[1:]
    block = vals.shape[2] // 2
    groups = lax.axis_size("batch")
    turns = block // groups
    slots = places.shape[1]
    scale = 1.0 / math.sqrt(length)

    def kernel(at_ref, dg_ref, dl_ref, p_ref, tap_ref, vals_ref, spec_ref, th_ref, tl_ref, *refs):
        sum_refs, (out_ref, ker_ref, dtap_ref, long_ref, gating_ref, acc_ref) = refs[:-6], refs[-6:]
        step = pl.program_id(0)

        @pl.when(step == 0)
        def _():
            at = lax.broadcasted_iota(jnp.int32, (slots, length), 1)
            chosen = jnp.where(at == at_ref[0], 1.0, 0.0).astype(BF16)
            for source, target in ((dg_ref, gating_ref), (dl_ref, long_ref)):
                high, low = halves(source[0])
                target[...] = lax.dot_general(high, chosen, (NN, ((), ())), preferred_element_type=F32) + (
                    lax.dot_general(low, chosen, (NN, ((), ())), preferred_element_type=F32)
                )

        for phase in range(FOLDED):

            @pl.when(step == phase)
            def _(phase=phase):
                deep = depth(phase, block)
                table = (th_ref[0, :deep], tl_ref[0, :deep])
                hat = dot(halves(fold(long_ref[...], phase, block)), table, NN) * (0.5 / length)
                ker = times(hat, vals_ref[0], block, conj=True)
                spread = jnp.concatenate([ker[:, :block], ker[:, block:]], axis=0).T.reshape(groups, turns, 2 * own)
                ker_ref[:, 0] = sum_refs[0][:, 0] + spread if sum_refs else spread
                both = jnp.concatenate(
                    [ker * (pair(phase) * scale), times(hat, spec_ref[0], block, conj=True)], axis=0
                )
                unfold(acc_ref, dot(halves(both), table, NT), phase, block)

        @pl.when(step == FOLDED - 1)
        def _():
            lane = lax.broadcasted_iota(jnp.int32, (own, 128), 1)
            for k in range(3):
                grad = gating_ref[...] if k == 1 else acc_ref[k // 2 * own : (k // 2 + 1) * own]
                p = p_ref[k]
                tap = tap_ref[k]
                out_ref[k] = tap[:, 0:1] * shift(grad, 1) + tap[:, 1:2] * grad + tap[:, 2:3] * shift(grad, -1)
                sums = jnp.zeros((own, 128), F32)
                for j, moved in enumerate((shift(p, -1), p, shift(p, 1))):
                    sums = jnp.where(lane == j, jnp.sum(moved * grad, axis=1, keepdims=True), sums)
                dtap_ref[k] = sums

    by_phase = lambda *shape: pl.BlockSpec((1,) + shape, lambda i, *_: (i,) + (0,) * len(shape))
    spectrum = pl.BlockSpec((groups, 1, turns, 2 * own), lambda i, *_: (0, i, 0, 0))
    return call(
        kernel, "mix_back", 3 * 6 * own * 4 * length * length, 4 * own * length * 22,
        [places, d_gating, d_long, projected, taps, vals, spec, *tables, *kernel_sum],
        [
            pl.BlockSpec((1, slots, 1), lambda i: (which, 0, 0)),
            pl.BlockSpec((1, own, slots), lambda i: (which, 0, 0)),
            pl.BlockSpec((1, own, slots), lambda i: (which, 0, 0)),
            whole(3, own, length),
            whole(3, own, 3),
            by_phase(own, 2 * block),
            by_phase(own, 2 * block),
            by_phase(2 * block, 2 * block),
            by_phase(2 * block, 2 * block),
        ] + [spectrum] * len(kernel_sum),
        [shaped(3, own, length), shaped(groups, FOLDED, turns, 2 * own), shaped(3, own, 128)],
        [whole(3, own, length), spectrum, whole(3, own, 128)],
        grid=(FOLDED,),
        scratch=[
            pltpu.VMEM((own, length), F32),
            pltpu.VMEM((own, length), F32),
            pltpu.VMEM((2 * own, length), F32),
        ],
        after=after,
    )


def add_mixer(x, gated, w_out, after=()):
    length, width = x.shape
    own = gated[0].shape[0]
    tokens = length // 2

    def kernel(x_ref, g0, g1, g2, g3, w0, w1, w2, w3, out_ref, wh, wl, gh, gl):
        @first
        def _():
            for d, ref in enumerate((w0, w1, w2, w3)):
                wh[d * own : (d + 1) * own], wl[d * own : (d + 1) * own] = halves(ref[...])

        for d, ref in enumerate((g0, g1, g2, g3)):
            gh[d * own : (d + 1) * own], gl[d * own : (d + 1) * own] = halves(ref[...])
        out_ref[...] = x_ref[...] + dot((gh[...], gl[...]), (wh[...], wl[...]), TN)

    rows = pl.BlockSpec((tokens, width), lambda i: (i, 0))
    (out,) = call(
        kernel, "add_mixer", 6 * length * width * width, 4 * (3 * length * width + width * width),
        [x, *gated, *w_out],
        [rows] + [pl.BlockSpec((own, tokens), lambda i: (0, i))] * 4 + [whole(own, width)] * 4,
        [shaped(length, width)], [rows], grid=(2,),
        scratch=[pltpu.VMEM((width, width), BF16)] * 2 + [pltpu.VMEM((width, tokens), BF16)] * 2,
        after=after,
    )
    return out


def gelu_parts(u):
    inner = math.sqrt(2.0 / math.pi) * (u + 0.044715 * (u * u * u))
    return 0.5 * (1.0 + jnp.tanh(inner))


def deal(low, value, out_refs):
    tokens = value.shape[0] // 2
    for step in range(2):
        for crossed in range(2):

            @pl.when((pl.program_id(0) == step) & (low == crossed))
            def _(step=step, crossed=crossed):
                out_refs[2 * step + crossed][...] = value[:tokens]
                out_refs[2 * step + 1 - crossed][...] = value[tokens:]


def feed_forward(residual, w_units, w_down, s, after=()):
    length, width = residual.shape
    units = w_down[0].shape[0]
    tokens = length // 4

    def kernel(s_ref, r_ref, wh, wl, dh, dl, *out_refs):
        both = halves(normed(r_ref[...])[0])
        gate_up = dot(both, (wh[...], wl[...]), NN)
        gate, up = gate_up[:, :units], gate_up[:, units:]
        out = dot(halves(gate * gelu_parts(gate) * up), (dh[...], dl[...]), NN)
        deal(s_ref[0] & 1, out, out_refs)

    return call(
        kernel, "feed_forward", 18 * length * width * units, 4 * (2 * length * width + 3 * width * units),
        [residual, *w_units, *w_down],
        [pl.BlockSpec((2 * tokens, width), lambda i, s_ref: ((s_ref[0] >> 1) ^ i, 0))]
        + [whole(width, 2 * units)] * 2 + [whole(units, width)] * 2,
        [shaped(tokens, width)] * 4, [whole(tokens, width)] * 4,
        grid=(2,), scalars=[s.reshape(1)], after=after,
    )


def chosen(at_ref, slots, length):
    lane = lax.broadcasted_iota(jnp.int32, (slots, length), 1)
    return jnp.where(lane == at_ref[...], 1.0, 0.0).astype(BF16)


def live_back(residual, places, d_out, w_units, w_down, used, after=()):
    seqs = len(residual)
    length, width = residual[0].shape
    slots = places.shape[1]
    units = w_down[0].shape[0]
    rows = seqs * slots

    def kernel(r_refs, at_ref, o_ref, wh, wl, dh, dl, live_ref, n_ref, hid_ref, du_ref, e_ref):
        for i, ref in enumerate(r_refs):
            pick = chosen(at_ref.at[i], slots, length)
            live_ref[i * slots : (i + 1) * slots] = chosen_rows(pick, halves(ref[...]), NN)
        n = normed(live_ref[...])[0]
        n_ref[...] = n
        gate_up = dot(halves(n), (wh[...], wl[...]), NN)
        d_hidden = dot(halves(o_ref[...]), (dh[...], dl[...]), NT)
        gate, up = gate_up[:, :units], gate_up[:, units:]
        half = gelu_parts(gate)
        slope = half + gate * 2.0 * half * (1.0 - half) * math.sqrt(2.0 / math.pi) * (1.0 + 0.134145 * (gate * gate))
        hid_ref[...] = gate * half * up
        d_units = jnp.concatenate([d_hidden * up * slope, d_hidden * (gate * half)], axis=1)
        du_ref[...] = d_units
        e = dot(halves(d_units), (wh[...], wl[...]), NT)
        for i in range(seqs):
            e_ref[i * used : (i + 1) * used] = e[i * slots : i * slots + used]

    def spread(*refs):
        kernel(refs[:seqs], *refs[seqs:])

    return call(
        spread, "live_back", 30 * rows * width * units, 4 * (2 * length * width + 4 * width * units),
        [*residual, places, d_out, *w_units, *w_down],
        [whole(length, width)] * seqs + [whole(seqs, slots, 1), whole(rows, width)]
        + [whole(width, 2 * units)] * 2 + [whole(units, width)] * 2,
        [shaped(rows, width), shaped(rows, width), shaped(rows, units), shaped(rows, 2 * units), shaped(seqs * used, width)],
        [whole(rows, width), whole(rows, width), whole(rows, units), whole(rows, 2 * units), whole(seqs * used, width)],
        after=after,
    )


def unit_grads(normed_live, d_units, hidden, d_out, shards, after=()):
    slots, width = normed_live.shape
    units = hidden.shape[1]
    groups = lax.axis_size("batch")
    rows = width // groups // shards
    down = units // groups

    def kernel(n_ref, u_ref, h_ref, o_ref, out_ref):
        @pl.when(pl.program_id(0) < 2)
        def _():
            part = dot(halves(n_ref[...]), halves(u_ref[...]), TN)
            for j in range(groups):
                for k in range(shards):
                    at = (k * groups + j) * rows
                    out_ref[j, k * rows : (k + 1) * rows] = part[at : at + rows]

        @pl.when(pl.program_id(0) == 2)
        def _():
            part = dot(halves(h_ref[...]), halves(o_ref[...]), TN)
            for j in range(groups):
                out_ref[j] = part[j * down : (j + 1) * down]

    (out,) = call(
        kernel, "unit_grads", 18 * slots * width * units, 4 * 3 * width * units,
        [normed_live, d_units, hidden, d_out],
        [
            whole(slots, width),
            pl.BlockSpec((slots, units), lambda i: (0, jnp.minimum(i, 1))),
            whole(slots, units),
            whole(slots, width),
        ],
        [shaped(groups, shards * rows, 2 * units + width)],
        [pl.BlockSpec((groups, shards * rows, width), lambda i: (0, 0, i))],
        grid=(3,), after=after,
    )
    return out


def live_mix(live, d_out, e_terms, w_out, gating, long_conv, places, after=()):
    seqs = len(gating)
    own, length = gating[0].shape
    rows, width = live.shape
    slots = rows // seqs
    used = e_terms[0].shape[0]

    def kernel(live_ref, o_ref, *refs):
        e_refs, w_ref, refs = refs[: 2 * seqs], refs[2 * seqs], refs[2 * seqs + 1 :]
        g_refs, l_refs, refs = refs[:seqs], refs[seqs : 2 * seqs], refs[2 * seqs :]
        at_ref, res_ref, dw_ref, dg_ref, dl_ref, e_all, pick_ref = refs
        e_all[...] = jnp.zeros((rows, width), F32)
        for i in range(seqs):
            e_all[i * slots : i * slots + used] = e_refs[i][...] + e_refs[seqs + i][...]
        n, inverse = normed(live_ref[...])
        e = e_all[...]
        along = jnp.mean(e * n, axis=-1, keepdims=True)
        res_ref[...] = o_ref[...] + (e - jnp.mean(e, axis=-1, keepdims=True) - n * along) * inverse
        d_res = halves(res_ref[...])
        d_gated = dot(halves(w_ref[...]), d_res, NT)
        for i in range(seqs):
            pick = chosen(at_ref.at[i], slots, length)
            at = slice(i * slots, (i + 1) * slots)
            gate = [lax.dot_general(v, pick, (NT, ((), ())), preferred_element_type=F32) for v in halves(g_refs[i][...])]
            lng = [lax.dot_general(v, pick, (NT, ((), ())), preferred_element_type=F32) for v in halves(l_refs[i][...])]
            gate, lng = gate[0] + gate[1], lng[0] + lng[1]
            dg_ref[i] = d_gated[:, at] * lng
            dl_ref[i] = d_gated[:, at] * gate
            pick_ref[:, at] = gate * lng
        dw_ref[...] = dot(halves(pick_ref[...]), d_res, NN)

    return call(
        kernel, "live_mix", 20 * rows * width * own, 4 * (4 * own * length + 4 * rows * width),
        [live, d_out, *e_terms, w_out, *gating, *long_conv, places],
        [whole(rows, width)] * 2 + [whole(used, width)] * (2 * seqs) + [whole(own, width)]
        + [whole(own, length)] * (2 * seqs) + [whole(seqs, slots, 1)],
        [shaped(rows, width), shaped(own, width), shaped(seqs, own, slots), shaped(seqs, own, slots)],
        [whole(rows, width), whole(own, width), whole(seqs, own, slots), whole(seqs, own, slots)],
        scratch=[pltpu.VMEM((rows, width), F32), pltpu.VMEM((own, rows), F32)],
        after=after,
    )


def project_back(d_projected, n_both, w_turned, w_sum, s, after=()):
    channels, length = d_projected.shape
    width = n_both[0].shape[1]
    tokens = length // 4

    def kernel(s_ref, d_ref, nh, nl, wh, wl, *refs):
        sum_refs, e_refs, dw_ref = refs[:-5], refs[-5:-1], refs[-1]
        both = halves(d_ref[...])
        deal(s_ref[0] & 1, dot(both, (wh[...], wl[...]), TN), e_refs)
        part = dot(both, (nh[...], nl[...]), NN)

        @pl.when(pl.program_id(0) == 0)
        def _():
            dw_ref[...] = sum_refs[0][...] + part if sum_refs else part

        @pl.when(pl.program_id(0) == 1)
        def _():
            dw_ref[...] += part

    at = lambda i, s_ref: ((s_ref[0] >> 1) ^ i, 0)
    return call(
        kernel, "project_back", 12 * length * width * channels,
        4 * (2 * length * width + channels * (length + 3 * width)),
        [d_projected, *n_both, *w_turned, *w_sum],
        [pl.BlockSpec((channels, 2 * tokens), lambda i, s_ref: (0, (s_ref[0] >> 1) ^ i))]
        + [pl.BlockSpec((2 * tokens, width), at)] * 2 + [whole(channels, width)] * (2 + len(w_sum)),
        [shaped(tokens, width)] * 4 + [shaped(channels, width)],
        [whole(tokens, width)] * 4 + [whole(channels, width)],
        grid=(2,), scalars=[s.reshape(1)], after=after,
    )


def turn_back(turned, placed, w_out_part, after=()):
    channels, width = turned.shape
    own = w_out_part.shape[0]
    groups = lax.axis_size("batch")
    shards = width // own
    rows = own // groups
    wide = -(-(channels + 1) // 128) * 128

    def kernel(w_ref, p_ref, o_ref, out_ref, flat_ref):
        flat_ref[:channels] = w_ref[...]
        flat_ref[channels:] = jnp.zeros((wide - channels, width), F32)
        back = flat_ref[...].T
        for j in range(groups):
            for k in range(shards):
                at = (k * groups + j) * rows
                to = slice(k * rows, (k + 1) * rows)
                out_ref[j, to, : wide - 128] = back[at : at + rows, : wide - 128]
                out_ref[j, to, wide - 128 : wide] = back[at : at + rows, wide - 128 :] + p_ref[at : at + rows]
                out_ref[j, to, wide:] = o_ref[j * rows : (j + 1) * rows, k * own : (k + 1) * own]

    shape = (groups, shards * rows, wide + own)
    (out,) = call(
        kernel, "turn_back", 0, 8 * width * wide, [turned, placed, w_out_part],
        [whole(channels, width), whole(width, 128), whole(own, width)], [shaped(*shape)], [whole(*shape)],
        scratch=[pltpu.VMEM((wide, width), F32)], after=after,
    )
    return out


def norm_pull(n, inverse, grad):
    along = jnp.mean(grad * n, axis=-1, keepdims=True)
    return (grad - jnp.mean(grad, axis=-1, keepdims=True) - n * along) * inverse


def together(*values):
    return lax.optimization_barrier(values)


def body(
    inputs,
    gain_one,
    w_in,
    conv_weight,
    kernel,
    w_out,
    gain_two,
    w_gate,
    w_up,
    w_down,
    mask_positions,
    mask_counts,
    grad_rows,
):
    shards = lax.axis_size("seq")
    groups = lax.axis_size("batch")
    s = lax.axis_index("seq")
    seqs, tokens, width = inputs.shape
    length = tokens * shards
    freqs = 2 * length
    own = width // shards
    rows = w_in.shape[0]
    units = w_gate.shape[1] // shards
    count = conv_weight.shape[1]
    extra = 3 * count // rows
    tables = phase_tables(freqs)

    w_pre = (gain_one[:, None] * w_in).reshape(rows, 3, shards, own).transpose(0, 2, 1, 3)
    w_pre = w_pre.reshape(rows, shards, 3 * own)
    carried = jnp.broadcast_to(conv_weight.reshape(rows, 1, extra), (rows, shards, extra))
    split = 3 * own + extra
    sent = columns_out(jnp.concatenate([w_pre, carried], axis=2), s)
    wide = kernel.reshape(2, -1, RADIX, own)
    mirror = [(i, groups - 1 - i) for i in range(groups)]
    folded = lax.ppermute(wide[:, ::-1, :4:-1], "batch", mirror)
    sent, folded, inputs_now = together(sent, folded, inputs)
    w_pre = over_batch(sent.reshape(shards * rows, split)).reshape(groups, shards, rows, split)

    folded = fold_base(wide, folded, w_out)
    spectra = folded.shape[0] - rows * shards // 2
    near = [(swap(inputs_now[i], "seq", 1), swap(inputs_now[i], "seq", 2)) for i in range(seqs)]
    near, folded, w_pre, w_gate_now, w_up_now = together(near, folded, w_pre, w_gate, w_up)
    base = over_batch(folded)

    far = [swap(near[i][i % 2], "seq", 2 - i % 2) for i in range(seqs)]
    w_units = jnp.stack([gain_two[:, None] * w_gate_now, gain_two[:, None] * w_up_now], axis=1)
    w_units = w_units.reshape(rows, 2, shards, units).transpose(0, 2, 1, 3).reshape(rows, shards, 2 * units)
    w_turned = turn_in(w_pre, 3 * own)
    taps = w_pre[..., 3 * own :].reshape(groups, shards, 3, count).transpose(2, 1, 0, 3)
    taps = lax.dynamic_index_in_dim(taps.reshape(3, 3, shards, own), s, axis=2, keepdims=False)
    taps = taps.transpose(1, 2, 0)
    far, w_units, w_down_now, w_turned, taps = together(far, columns_out(w_units, s), w_down, w_turned, taps)
    x_pieces = [(inputs[i], *near[i], far[i]) for i in range(seqs)]
    w_units = over_batch(w_units.reshape(shards * rows, 2 * units))
    w_down_own = over_batch(w_down_now).reshape(units, width)

    slots = mask_positions.shape[1]
    pad = -slots % 128
    live = jnp.arange(slots, dtype=jnp.int32) < mask_counts[:, None]
    places = jnp.pad(jnp.where(live, mask_positions, -1), ((0, 0), (0, pad)), constant_values=-1)
    d_out = jnp.pad(jnp.where(live[:, :, None], grad_rows, 0.0), ((0, 0), (0, pad), (0, 0)))
    d_out = d_out.reshape(-1, width)
    places = places[:, :, None]

    def first_half(i, after):
        x_i, *n_i = arrange(x_pieces[i], s, after=after)
        return x_i, n_i, project(w_turned, n_i).reshape(3, own, length)

    first_0 = first_half(0, ())
    (x_0, n_0, p_0), base = together(first_0, base)

    w_out_own = base[:, spectra:].reshape(groups, shards // 2, rows, 2 * own).transpose(0, 2, 1, 3).reshape(own, width)
    w_out_there, (gated_0, *mixed_0) = together(from_others(w_out_own), mix(p_0, taps, base, tables))

    first_1 = first_half(1, (gated_0,))
    there_0, first_1, (gated_1, *mixed_1) = together(
        from_others(gated_0), first_1, mix(first_1[2], taps, base, tables, after=(gated_0,))
    )
    x_1, n_1, p_1 = first_1
    n_one, projected = (n_0, n_1), (p_0, p_1)
    gating, long_conv, vals, spec = zip(mixed_0, mixed_1)
    w_out_pieces = (w_out_own, *w_out_there)

    residual_0 = add_mixer(x_0, (gated_0, *there_0), w_out_pieces, after=(gated_1,))
    w_units = split_units(w_units.reshape(groups, shards, rows, 2 * units), w_down_own, after=(residual_0,))
    w_units, w_down_own = w_units[:2], w_units[2:]
    down_0 = feed_forward(residual_0, w_units, w_down_own, s)
    there_1, down_0, residual_0, w_units, w_down_own = together(
        from_others(gated_1), down_0, residual_0, w_units, w_down_own
    )

    residual_1 = add_mixer(x_1, (gated_1, *there_1), w_out_pieces, after=(down_0[0],))
    lived = live_back((residual_0, residual_1), places, d_out, w_units, w_down_own, slots)
    out_0 = [down_0[0], swap(down_0[1], "seq", 1), swap(down_0[2], "seq", 2)]
    lived, residual_1, out_0 = together(lived, residual_1, out_0)
    live_rows, n_live, hidden, d_units, e_two = lived
    residual = (residual_0, residual_1)

    e_two = [e_two[:slots], e_two[slots:]]
    unit_part = unit_grads(n_live, d_units, hidden, d_out, shards)
    e_there, unit_part = together([swap(e, "seq", 1 + i) for i, e in enumerate(e_two)], unit_part)
    unit_sums = sum_over_batch(unit_part)

    e_two = [e + there for e, there in zip(e_two, e_there)]
    down_1 = feed_forward(residual_1, w_units, w_down_own, s, after=(unit_part,))
    e_there, down_1 = together([swap(e, "seq", 2 - i) for i, e in enumerate(e_two)], down_1)
    e_terms = [*e_two, *e_there]

    d_residual, w_out_part, d_gating, d_long = live_mix(live_rows, d_out, e_terms, w_out_own, gating, long_conv, places)
    kernel_part, taps_part, d_projected = (), 0.0, []
    for i in range(seqs):
        d_p, *kernel_part, d_taps = mix_back(
            i, places, d_gating, d_long, projected[i], taps, vals[i], spec[i], kernel_part, tables,
            after=d_projected[-1:],
        )
        taps_part = taps_part + d_taps[:, :, :3]
        d_projected.append(d_p)
    out_0 += [swap(down_0[3], "seq", 3)]
    out_1 = [down_1[0], swap(down_1[1], "seq", 1), swap(down_1[2], "seq", 2)]
    d_projected, (kernel_part,), taps_part, d_residual, w_out_part, out_0, out_1 = together(
        d_projected, kernel_part, taps_part, d_residual, w_out_part, out_0, out_1
    )

    e_0 = project_back(d_projected[0].reshape(3 * own, length), n_0, w_turned, (), s)
    out_1 += [swap(down_1[3], "seq", 3)]
    (*e_0, w_in_part), out_1, unit_sums, kernel_part = together(e_0, out_1, unit_sums, kernel_part)
    kernel_sum = sum_over_batch(kernel_part.reshape(groups, -1, 2 * own))

    e_1 = project_back(d_projected[1].reshape(3 * own, length), n_1, w_turned, (w_in_part,), s)
    placed = jnp.zeros((3, 3, shards, own), F32)
    taps_part = taps_part.transpose(2, 0, 1)[:, :, None]
    placed = lax.dynamic_update_slice(placed, taps_part, (0, 0, s, 0))
    placed = placed.reshape(3, shards, groups, count).transpose(1, 2, 0, 3).reshape(width, extra)
    free = 3 * own % 128
    placed = jnp.pad(placed, ((0, 0), (free, 128 - free - extra)))
    w_in_part = turn_back(e_1[4], placed, w_out_part)
    e_there = [swap(e_0[1], "seq", 1), swap(e_0[2], "seq", 2)]
    outputs = [
        added(out) + lax.dynamic_slice_in_dim(residual[i], s * tokens, tokens, axis=0)
        for i, out in enumerate((out_0, out_1))
    ]
    e_there, e_1, w_in_part = together(e_there, e_1[:4], w_in_part)
    w_in_sum = sum_over_batch(w_in_part)

    e_one = ([e_0[0], *e_there, swap(e_0[3], "seq", 3)], to_others(e_1))
    outputs = jnp.stack(
        [
            added(out) + lax.dynamic_slice_in_dim(residual[i], s * tokens, tokens, axis=0)
            for i, out in enumerate((out_0, out_1))
        ]
    )
    e_one, w_in_sum, kernel_sum, outputs = together(e_one, w_in_sum, kernel_sum, outputs)

    kernel_sum = kernel_sum.reshape(FOLDED, -1, 2, own).transpose(2, 1, 0, 3)
    mirrored = lax.ppermute(kernel_sum[:, ::-1, 3:0:-1], "batch", mirror)
    w_back = jnp.concatenate([w_in_sum[:, :-own], unit_sums[:, : 2 * units]], axis=1)
    w_back = columns_there(w_back.reshape(shards, rows, -1), s)

    e_own = jnp.stack([added(e) for e in e_one])
    n_own, inverse_own = normed(inputs)
    here = s * tokens + jnp.arange(tokens, dtype=jnp.int32)
    select_own = (places == here).astype(F32)
    direct = contract("bmt,bmd->btd", select_own, d_residual.reshape(seqs, slots + pad, width))
    input_grad = norm_pull(n_own, inverse_own, e_own) + direct
    mirrored = jnp.stack([mirrored[0], -mirrored[1]])
    kernel_grad = jnp.concatenate([kernel_sum, mirrored], axis=2).reshape(kernel.shape)
    w_out_sum = w_in_sum[:, -own:].reshape(shards, rows, own).transpose(1, 0, 2).reshape(w_out.shape)
    w_back = by_xor(w_back, s)
    w_in_sum = w_back
    taps_sum = sum(p[:, 3 * own : split] for p in w_in_sum).reshape(conv_weight.shape)
    w_in_sum = jnp.stack([p[:, : 3 * own].reshape(rows, 3, own) for p in w_in_sum], axis=2)
    w_in_sum = w_in_sum.reshape(w_in.shape)
    w_down_sum = unit_sums[:, 2 * units :].reshape(w_down.shape)
    w_units_sum = [p[:, -2 * units :] for p in w_back]
    w_gate_sum = jnp.concatenate([p[:, :units] for p in w_units_sum], axis=1)
    w_up_sum = jnp.concatenate([p[:, units:] for p in w_units_sum], axis=1)
    gain_one_sum = jnp.sum(w_in * w_in_sum, axis=1)
    gain_two_sum = jnp.sum(w_gate * w_gate_sum, axis=1) + jnp.sum(w_up * w_up_sum, axis=1)

    return (
        outputs,
        input_grad,
        gain_one_sum,
        gain_one[:, None] * w_in_sum,
        taps_sum,
        kernel_grad,
        w_out_sum,
        gain_two_sum,
        gain_two[:, None] * w_gate_sum,
        gain_two[:, None] * w_up_sum,
        w_down_sum,
    )


def solution(mesh):
    split = ("seq", "batch")
    placed = (
        P("batch", "seq", None),
        P(split),
        P(split, None),
        P(None, split),
        P(None, "batch", "seq"),
        P(split, None),
        P(split),
        P(split, None),
        P(split, None),
        P(split, None),
        P("batch", None),
        P("batch"),
        P("batch", None, None),
    )
    return jax.shard_map(
        body,
        mesh=mesh,
        in_specs=placed,
        out_specs=(
            P("batch", "seq", None),
            P("batch", "seq", None),
            P(split),
            P(split, None),
            P(None, split),
            P(None, "batch", "seq"),
            P(split, None),
            P(split),
            P(split, None),
            P(split, None),
            P(split, None),
        ),
        check_vma=False,
    )
```

```python
import math

import jax
import jax.numpy as jnp
import numpy as np
from jax import lax
from jax.experimental import pallas as pl
from jax.experimental.pallas import tpu as pltpu
from jax.sharding import PartitionSpec as P

EPS = 1e-05
HIGH = lax.Precision.HIGH
RADIX = 8
FOLDED = 5
ROOT = math.sqrt(0.5)
VMEM = 56 * 1024 * 1024
COST = 20
NN = ((1,), (0,))
NT = ((1,), (1,))
TN = ((0,), (0,))
F32 = jnp.float32
BF16 = jnp.bfloat16


def contract(pattern, left_side, right_side):
    return jnp.einsum(pattern, left_side, right_side, precision=HIGH)


def swap(value, axis, distance):
    devices = lax.axis_size(axis)
    return lax.ppermute(value, axis, [(i, i ^ distance) for i in range(devices)])


def from_others(value):
    return [swap(value, "seq", d) for d in (1, 2, 3)]


def to_others(blocks):
    return [blocks[0]] + [swap(blocks[d], "seq", d) for d in (1, 2, 3)]


def to_all(value):
    return [value] + from_others(value)


def added(terms):
    return (terms[0] + terms[1]) + (terms[2] + terms[3])


def by_xor(pieces, index):
    count = len(pieces)
    out = []
    for k in range(count):
        chosen = pieces[k]
        for i in range(1, count):
            chosen = jnp.where(index == i, pieces[k ^ i], chosen)
        out.append(chosen)
    return out


def columns_out(shard, s):
    pieces = []
    for d in range(4):
        block = lax.dynamic_index_in_dim(shard, s ^ d, axis=1, keepdims=False)
        pieces.append(block if d == 0 else swap(block, "seq", d))
    return jnp.stack(by_xor(pieces, s))


def columns_there(own, s):
    pieces = []
    for d in range(4):
        block = lax.dynamic_index_in_dim(own, s ^ d, axis=0, keepdims=False)
        pieces.append(block if d == 0 else swap(block, "seq", d))
    return pieces


def over_batch(value):
    full = lax.all_gather(value, "batch", axis=0, tiled=True)
    return full.reshape((-1,) + value.shape)


def sum_over_batch(parts):
    flat = parts.reshape(-1, parts.shape[2])
    return lax.psum_scatter(flat, "batch", scatter_dimension=0, tiled=True)


def halves(value):
    high = value.astype(BF16)
    return high, (value - high.astype(F32)).astype(BF16)


def dot(left_side, right_side, dims):
    (a, b), (c, d) = left_side, right_side

    def product(x, y):
        return lax.dot_general(x, y, (dims, ((), ())), preferred_element_type=F32)

    return product(a, c) + (product(a, d) + product(b, c))


def chosen_rows(chosen, both, dims):
    high, low = both

    def product(x):
        return lax.dot_general(chosen, x, (dims, ((), ())), preferred_element_type=F32)

    return product(high) + product(low)


def normed(x):
    centered = x - jnp.mean(x, axis=-1, keepdims=True)
    inverse = lax.rsqrt(jnp.mean(centered * centered, axis=-1, keepdims=True) + EPS)
    return centered * inverse, inverse


def call(kernel, name, flops, moved, inputs, in_specs, outs, out_specs, grid=(1,), scratch=(), scalars=(), after=()):
    taken = len(scalars) + len(inputs)

    def run(*refs):
        kernel(*refs[:taken], *refs[taken + len(after) :])

    return pl.pallas_call(
        run,
        name=name,
        out_shape=tuple(outs),
        grid_spec=pltpu.PrefetchScalarGridSpec(
            num_scalar_prefetch=len(scalars),
            grid=grid,
            in_specs=list(in_specs) + [pl.BlockSpec(memory_space=pl.ANY)] * len(after),
            out_specs=tuple(out_specs),
            scratch_shapes=list(scratch),
        ),
        compiler_params=pltpu.CompilerParams(vmem_limit_bytes=VMEM),
        cost_estimate=pl.CostEstimate(flops=int(flops) // COST, bytes_accessed=int(moved) // COST, transcendentals=0),
    )(*scalars, *inputs, *after)


def shaped(*shape, dtype=F32):
    return jax.ShapeDtypeStruct(shape, dtype)


def whole(*shape):
    return pl.BlockSpec(shape, lambda *_: (0,) * len(shape))


def first(work):
    pl.when(pl.program_id(0) == 0)(work)


def fold_base(kernel, mirrored, after=()):
    _, turns, kept, own = mirrored.shape

    def run(k_ref, m_ref, out_ref):
        for phase in range(FOLDED):
            for part in range(2):
                value = k_ref[part, :, phase]
                if 0 < phase <= kept:
                    other = m_ref[part, :, phase - 1]
                    value = value + other if part == 0 else value - other
                out_ref[phase * turns : (phase + 1) * turns, part * own : (part + 1) * own] = value

    shape = (FOLDED * turns, 2 * own)
    (out,) = call(
        run, "fold_base", 0, 12 * shape[0] * shape[1], [kernel, mirrored],
        [whole(*kernel.shape), whole(*mirrored.shape)], [shaped(*shape)], [whole(*shape)], after=after,
    )
    return out


def turn_in(gathered, channels):
    groups, shards, rows, _ = gathered.shape
    width = groups * shards * rows
    wide = -(-channels // 128) * 128

    def kernel(w_ref, high_ref, low_ref, flat_ref):
        flat_ref[:, channels // 128 * 128 :] = jnp.zeros((width, wide - channels // 128 * 128), F32)
        for k in range(shards):
            for j in range(groups):
                at = (k * groups + j) * rows
                flat_ref[at : at + rows, :channels] = w_ref[j, k, :, :channels]
        turned = flat_ref[...].T
        high_ref[...], low_ref[...] = halves(turned[:channels])

    return call(
        kernel, "turn_in", 0, 4 * 2 * width * wide, [gathered], [whole(*gathered.shape)],
        [shaped(channels, width, dtype=BF16)] * 2, [whole(channels, width)] * 2,
        scratch=[pltpu.VMEM((width, wide), F32)],
    )


def split_units(gathered, w_down, after=()):
    groups, shards, rows, columns = gathered.shape
    width = groups * shards * rows
    units = w_down.shape[0]

    def kernel(w_ref, d_ref, high_ref, low_ref, dh_ref, dl_ref, flat_ref):
        k = pl.program_id(0)
        for j in range(groups):
            flat_ref[j * rows : (j + 1) * rows] = w_ref[j, 0]

        high_ref[...], low_ref[...] = halves(flat_ref[...])
        dh_ref[...], dl_ref[...] = halves(d_ref[...])

    part = pl.BlockSpec((groups * rows, columns), lambda i: (i, 0))
    down = pl.BlockSpec((units // shards, width), lambda i: (i, 0))
    return call(
        kernel, "split_units", 0, 8 * width * (columns + units), [gathered, w_down],
        [pl.BlockSpec((groups, 1, rows, columns), lambda i: (0, i, 0, 0)), down],
        [shaped(width, columns, dtype=BF16)] * 2 + [shaped(units, width, dtype=BF16)] * 2,
        [part, part, down, down], grid=(shards,),
        scratch=[pltpu.VMEM((groups * rows, columns), F32)], after=after,
    )


def arrange(pieces, s, after=()):
    tokens, width = pieces[0].shape
    length = 4 * tokens

    def kernel(s_ref, p0, p1, p2, p3, x_ref, high_ref, low_ref):
        for d, piece in enumerate((p0, p1, p2, p3)):

            @pl.when(pl.program_id(0) == d)
            def _(piece=piece):
                x = piece[...]
                x_ref[...] = x
                high_ref[...], low_ref[...] = halves(normed(x)[0])

    rows = pl.BlockSpec((tokens, width), lambda i, s_ref: (s_ref[0] ^ i, 0))
    return call(
        kernel, "arrange", 0, 12 * length * width, pieces, [whole(tokens, width)] * 4,
        [shaped(length, width), shaped(length, width, dtype=BF16), shaped(length, width, dtype=BF16)],
        [rows] * 3, grid=(4,), scalars=[s.reshape(1)], after=after,
    )


def project(w_turned, n_both, after=()):
    channels, width = w_turned[0].shape
    length = n_both[0].shape[0]
    tokens = length // 2

    def kernel(wh, wl, nh, nl, out_ref):
        out_ref[...] = dot((wh[...], wl[...]), (nh[...], nl[...]), NT)

    rows = pl.BlockSpec((tokens, width), lambda i: (i, 0))
    (out,) = call(
        kernel, "project", 6 * length * width * channels, 4 * (length * width + channels * (length + width)),
        [*w_turned, *n_both], [whole(channels, width)] * 2 + [rows] * 2,
        [shaped(channels, length)], [pl.BlockSpec((channels, tokens), lambda i: (0, i))], grid=(2,), after=after,
    )
    return out


def phase_tables(length):
    block = length // RADIX
    place = np.arange(block)[:, None]
    turn = np.arange(block)[None, :]
    tables = []
    for phase in range(FOLDED):
        angle = 2.0 * np.pi * ((RADIX * turn + phase) * place % length) / length
        cos, sin = np.cos(angle), np.sin(angle)
        tables.append(np.block([[cos, -sin], [sin, cos]]))
    table = np.stack(tables).astype(np.float32)
    high = table.astype(BF16)
    low = (table - high.astype(np.float32)).astype(BF16)
    return jnp.asarray(high), jnp.asarray(low)


def shift(value, step):
    length = value.shape[1]
    lane = lax.broadcasted_iota(jnp.int32, value.shape, 1)
    if step < 0:
        return jnp.where(lane == 0, 0.0, pltpu.roll(value, 1, 1))
    return jnp.where(lane == length - 1, 0.0, pltpu.roll(value, length - 1, 1))


def fold(value, phase, block):
    x0, x1, x2, x3 = [value[:, i * block : (i + 1) * block] for i in range(4)]
    if phase == 0:
        return (x0 + x2) + (x1 + x3)
    if phase == 4:
        return (x0 + x2) - (x1 + x3)
    if phase == 2:
        return jnp.concatenate([x0 - x2, x3 - x1], axis=1)
    slant, lean = (x1 - x3) * ROOT, (x1 + x3) * ROOT
    if phase == 1:
        return jnp.concatenate([x0 + slant, -x2 - lean], axis=1)
    return jnp.concatenate([x0 - slant, x2 - lean], axis=1)


def unfold(total_ref, value, phase, block):
    if phase == 0:
        terms = (value,) * 4
    elif phase == 4:
        terms = (value, -value, value, -value)
    else:
        real, imag = value[:, :block], value[:, block:]
        if phase == 2:
            terms = (real, -imag, -real, imag)
        elif phase == 1:
            terms = (real, ROOT * (real - imag), -imag, -ROOT * (real + imag))
        else:
            terms = (real, -ROOT * (real + imag), imag, ROOT * (real - imag))
    for i, term in enumerate(terms):
        cols = slice(i * block, (i + 1) * block)
        total_ref[:, cols] = term if phase == 0 else total_ref[:, cols] + term


def times(left_side, right_side, block, conj=False):
    a, b = left_side[:, :block], left_side[:, block:]
    c, d = right_side[:, :block], right_side[:, block:]
    if conj:
        d = -d
    return jnp.concatenate([a * c - b * d, a * d + b * c], axis=1)


def pair(phase):
    return 1.0 if phase in (0, 4) else 2.0


def depth(phase, block):
    return block if phase in (0, 4) else 2 * block


def mix(projected, taps, base, tables, after=()):
    own, length = projected.shape[1:]
    block = 2 * length // RADIX
    groups = base.shape[0]
    turns = block // groups
    if turns % 8:
        base = base.reshape(groups, FOLDED, turns, 2 * own)
        spectrum = pl.BlockSpec((groups, 1, turns, 2 * own), lambda i: (0, i, 0, 0))
    else:
        spectrum = pl.BlockSpec((groups, turns, 2 * own), lambda i: (0, i, 0))
    scale = 1.0 / math.sqrt(length)

    def kernel(p_ref, tap_ref, base_ref, th_ref, tl_ref, gated_ref, gating_ref, long_ref, vals_ref, spec_ref,
               mixed_ref, acc_ref, base_t):
        step = pl.program_id(0)

        @pl.when(step == 0)
        def _():
            for k in range(3):

                p = p_ref[k]
                tap = tap_ref[k]
                mixed = tap[:, 0:1] * shift(p, -1) + tap[:, 1:2] * p + tap[:, 2:3] * shift(p, 1)
                if k == 1:
                    gating_ref[...] = mixed
                else:
                    mixed_ref[k // 2 * own : (k // 2 + 1) * own] = mixed

        turned = base_ref[...].reshape(block, 2 * own).T
        base_t[:, :block] = turned[:own]
        base_t[:, block:] = turned[own:]

        for phase in range(FOLDED):

            @pl.when(step == phase)
            def _(phase=phase):
                deep = depth(phase, block)
                table = (th_ref[0, :deep], tl_ref[0, :deep])
                hats = dot(halves(fold(mixed_ref[...], phase, block)), table, NN)
                spec = base_t[...] + (pair(phase) * scale) * hats[:own]
                vals = hats[own:]
                spec_ref[0] = spec
                vals_ref[0] = vals
                unfold(acc_ref, dot(halves(times(spec, vals, block)), table, NT), phase, block)

        @pl.when(step == FOLDED - 1)
        def _():
            long_conv = acc_ref[...] * (0.5 / length)
            long_ref[...] = long_conv
            gated_ref[...] = gating_ref[...] * long_conv

    flat, hat = shaped(own, length), shaped(FOLDED, own, 2 * block)
    by_phase = lambda *shape: pl.BlockSpec((1,) + shape, lambda i, *_: (i,) + (0,) * len(shape))
    return call(
        kernel, "mix", 3 * 6 * own * 4 * length * length, 4 * own * length * 22,
        [projected, taps, base, *tables],
        [whole(3, own, length), whole(3, own, 3)]
        + [spectrum]
        + [by_phase(2 * block, 2 * block), by_phase(2 * block, 2 * block)],
        [flat, flat, flat, hat, hat],
        [whole(own, length)] * 3 + [by_phase(own, 2 * block)] * 2,
        grid=(FOLDED,),
        scratch=[
            pltpu.VMEM((2 * own, length), F32),
            pltpu.VMEM((own, length), F32),
            pltpu.VMEM((own, 2 * block), F32),
        ],
        after=after,
    )


def mix_back(which, places, d_gating, d_long, projected, taps, vals, spec, kernel_sum, tables, after=()):
    own, length = projected.shape[1:]
    block = vals.shape[2] // 2
    groups = lax.axis_size("batch")
    turns = block // groups
    slots = places.shape[1]
    scale = 1.0 / math.sqrt(length)

    def kernel(at_ref, dg_ref, dl_ref, p_ref, tap_ref, vals_ref, spec_ref, th_ref, tl_ref, *refs):
        sum_refs, (out_ref, ker_ref, dtap_ref, long_ref, gating_ref, acc_ref) = refs[:-6], refs[-6:]
        step = pl.program_id(0)

        @pl.when(step == 0)
        def _():
            at = lax.broadcasted_iota(jnp.int32, (slots, length), 1)
            chosen = jnp.where(at == at_ref[0], 1.0, 0.0).astype(BF16)
            for source, target in ((dg_ref, gating_ref), (dl_ref, long_ref)):
                high, low = halves(source[0])
                target[...] = lax.dot_general(high, chosen, (NN, ((), ())), preferred_element_type=F32) + (
                    lax.dot_general(low, chosen, (NN, ((), ())), preferred_element_type=F32)
                )

        for phase in range(FOLDED):

            @pl.when(step == phase)
            def _(phase=phase):
                deep = depth(phase, block)
                table = (th_ref[0, :deep], tl_ref[0, :deep])
                hat = dot(halves(fold(long_ref[...], phase, block)), table, NN) * (0.5 / length)
                ker = times(hat, vals_ref[0], block, conj=True)
                spread = jnp.concatenate([ker[:, :block], ker[:, block:]], axis=0).T.reshape(groups, turns, 2 * own)
                ker_ref[:, 0] = sum_refs[0][:, 0] + spread if sum_refs else spread
                both = jnp.concatenate(
                    [ker * (pair(phase) * scale), times(hat, spec_ref[0], block, conj=True)], axis=0
                )
                unfold(acc_ref, dot(halves(both), table, NT), phase, block)

        @pl.when(step == FOLDED - 1)
        def _():
            lane = lax.broadcasted_iota(jnp.int32, (own, 128), 1)
            for k in range(3):
                grad = gating_ref[...] if k == 1 else acc_ref[k // 2 * own : (k // 2 + 1) * own]
                p = p_ref[k]
                tap = tap_ref[k]
                out_ref[k] = tap[:, 0:1] * shift(grad, 1) + tap[:, 1:2] * grad + tap[:, 2:3] * shift(grad, -1)
                sums = jnp.zeros((own, 128), F32)
                for j, moved in enumerate((shift(p, -1), p, shift(p, 1))):
                    sums = jnp.where(lane == j, jnp.sum(moved * grad, axis=1, keepdims=True), sums)
                dtap_ref[k] = sums

    by_phase = lambda *shape: pl.BlockSpec((1,) + shape, lambda i, *_: (i,) + (0,) * len(shape))
    spectrum = pl.BlockSpec((groups, 1, turns, 2 * own), lambda i, *_: (0, i, 0, 0))
    return call(
        kernel, "mix_back", 3 * 6 * own * 4 * length * length, 4 * own * length * 22,
        [places, d_gating, d_long, projected, taps, vals, spec, *tables, *kernel_sum],
        [
            pl.BlockSpec((1, slots, 1), lambda i: (which, 0, 0)),
            pl.BlockSpec((1, own, slots), lambda i: (which, 0, 0)),
            pl.BlockSpec((1, own, slots), lambda i: (which, 0, 0)),
            whole(3, own, length),
            whole(3, own, 3),
            by_phase(own, 2 * block),
            by_phase(own, 2 * block),
            by_phase(2 * block, 2 * block),
            by_phase(2 * block, 2 * block),
        ] + [spectrum] * len(kernel_sum),
        [shaped(3, own, length), shaped(groups, FOLDED, turns, 2 * own), shaped(3, own, 128)],
        [whole(3, own, length), spectrum, whole(3, own, 128)],
        grid=(FOLDED,),
        scratch=[
            pltpu.VMEM((own, length), F32),
            pltpu.VMEM((own, length), F32),
            pltpu.VMEM((2 * own, length), F32),
        ],
        after=after,
    )


def add_mixer(x, gated, w_out, after=()):
    length, width = x.shape
    own = gated[0].shape[0]
    tokens = length // 2

    def kernel(x_ref, g0, g1, g2, g3, w0, w1, w2, w3, out_ref, wh, wl, gh, gl):
        @first
        def _():
            for d, ref in enumerate((w0, w1, w2, w3)):
                wh[d * own : (d + 1) * own], wl[d * own : (d + 1) * own] = halves(ref[...])

        for d, ref in enumerate((g0, g1, g2, g3)):
            gh[d * own : (d + 1) * own], gl[d * own : (d + 1) * own] = halves(ref[...])
        out_ref[...] = x_ref[...] + dot((gh[...], gl[...]), (wh[...], wl[...]), TN)

    rows = pl.BlockSpec((tokens, width), lambda i: (i, 0))
    (out,) = call(
        kernel, "add_mixer", 6 * length * width * width, 4 * (3 * length * width + width * width),
        [x, *gated, *w_out],
        [rows] + [pl.BlockSpec((own, tokens), lambda i: (0, i))] * 4 + [whole(own, width)] * 4,
        [shaped(length, width)], [rows], grid=(2,),
        scratch=[pltpu.VMEM((width, width), BF16)] * 2 + [pltpu.VMEM((width, tokens), BF16)] * 2,
        after=after,
    )
    return out


def gelu_parts(u):
    inner = math.sqrt(2.0 / math.pi) * (u + 0.044715 * (u * u * u))
    return 0.5 * (1.0 + jnp.tanh(inner))


def deal(low, value, out_refs):
    tokens = value.shape[0] // 2
    for step in range(2):
        for crossed in range(2):

            @pl.when((pl.program_id(0) == step) & (low == crossed))
            def _(step=step, crossed=crossed):
                out_refs[2 * step + crossed][...] = value[:tokens]
                out_refs[2 * step + 1 - crossed][...] = value[tokens:]


def feed_forward(residual, w_units, w_down, s, after=()):
    length, width = residual.shape
    units = w_down[0].shape[0]
    tokens = length // 4

    def kernel(s_ref, r_ref, wh, wl, dh, dl, *out_refs):
        both = halves(normed(r_ref[...])[0])
        gate_up = dot(both, (wh[...], wl[...]), NN)
        gate, up = gate_up[:, :units], gate_up[:, units:]
        out = dot(halves(gate * gelu_parts(gate) * up), (dh[...], dl[...]), NN)
        deal(s_ref[0] & 1, out, out_refs)

    return call(
        kernel, "feed_forward", 18 * length * width * units, 4 * (2 * length * width + 3 * width * units),
        [residual, *w_units, *w_down],
        [pl.BlockSpec((2 * tokens, width), lambda i, s_ref: ((s_ref[0] >> 1) ^ i, 0))]
        + [whole(width, 2 * units)] * 2 + [whole(units, width)] * 2,
        [shaped(tokens, width)] * 4, [whole(tokens, width)] * 4,
        grid=(2,), scalars=[s.reshape(1)], after=after,
    )


def chosen(at_ref, slots, length):
    lane = lax.broadcasted_iota(jnp.int32, (slots, length), 1)
    return jnp.where(lane == at_ref[...], 1.0, 0.0).astype(BF16)


def live_back(residual, places, d_out, w_units, w_down, used, after=()):
    seqs = len(residual)
    length, width = residual[0].shape
    slots = places.shape[1]
    units = w_down[0].shape[0]
    rows = seqs * slots

    def kernel(r_refs, at_ref, o_ref, wh, wl, dh, dl, live_ref, n_ref, hid_ref, du_ref, e_ref):
        for i, ref in enumerate(r_refs):
            pick = chosen(at_ref.at[i], slots, length)
            live_ref[i * slots : (i + 1) * slots] = chosen_rows(pick, halves(ref[...]), NN)
        n = normed(live_ref[...])[0]
        n_ref[...] = n
        gate_up = dot(halves(n), (wh[...], wl[...]), NN)
        d_hidden = dot(halves(o_ref[...]), (dh[...], dl[...]), NT)
        gate, up = gate_up[:, :units], gate_up[:, units:]
        half = gelu_parts(gate)
        slope = half + gate * 2.0 * half * (1.0 - half) * math.sqrt(2.0 / math.pi) * (1.0 + 0.134145 * (gate * gate))
        hid_ref[...] = gate * half * up
        d_units = jnp.concatenate([d_hidden * up * slope, d_hidden * (gate * half)], axis=1)
        du_ref[...] = d_units
        e = dot(halves(d_units), (wh[...], wl[...]), NT)
        for i in range(seqs):
            e_ref[i * used : (i + 1) * used] = e[i * slots : i * slots + used]

    def spread(*refs):
        kernel(refs[:seqs], *refs[seqs:])

    return call(
        spread, "live_back", 30 * rows * width * units, 4 * (2 * length * width + 4 * width * units),
        [*residual, places, d_out, *w_units, *w_down],
        [whole(length, width)] * seqs + [whole(seqs, slots, 1), whole(rows, width)]
        + [whole(width, 2 * units)] * 2 + [whole(units, width)] * 2,
        [shaped(rows, width), shaped(rows, width), shaped(rows, units), shaped(rows, 2 * units), shaped(seqs * used, width)],
        [whole(rows, width), whole(rows, width), whole(rows, units), whole(rows, 2 * units), whole(seqs * used, width)],
        after=after,
    )


def unit_grads(normed_live, d_units, hidden, d_out, shards, after=()):
    slots, width = normed_live.shape
    units = hidden.shape[1]
    groups = lax.axis_size("batch")
    rows = width // groups // shards
    down = units // groups

    def kernel(n_ref, u_ref, h_ref, o_ref, out_ref):
        @pl.when(pl.program_id(0) < 2)
        def _():
            part = dot(halves(n_ref[...]), halves(u_ref[...]), TN)
            for j in range(groups):
                for k in range(shards):
                    at = (k * groups + j) * rows
                    out_ref[j, k * rows : (k + 1) * rows] = part[at : at + rows]

        @pl.when(pl.program_id(0) == 2)
        def _():
            part = dot(halves(h_ref[...]), halves(o_ref[...]), TN)
            for j in range(groups):
                out_ref[j] = part[j * down : (j + 1) * down]

    (out,) = call(
        kernel, "unit_grads", 18 * slots * width * units, 4 * 3 * width * units,
        [normed_live, d_units, hidden, d_out],
        [
            whole(slots, width),
            pl.BlockSpec((slots, units), lambda i: (0, jnp.minimum(i, 1))),
            whole(slots, units),
            whole(slots, width),
        ],
        [shaped(groups, shards * rows, 2 * units + width)],
        [pl.BlockSpec((groups, shards * rows, width), lambda i: (0, 0, i))],
        grid=(3,), after=after,
    )
    return out


def live_mix(live, d_out, e_terms, w_out, gating, long_conv, places, after=()):
    seqs = len(gating)
    own, length = gating[0].shape
    rows, width = live.shape
    slots = rows // seqs
    used = e_terms[0].shape[0]

    def kernel(live_ref, o_ref, *refs):
        e_refs, w_ref, refs = refs[: 2 * seqs], refs[2 * seqs], refs[2 * seqs + 1 :]
        g_refs, l_refs, refs = refs[:seqs], refs[seqs : 2 * seqs], refs[2 * seqs :]
        at_ref, res_ref, dw_ref, dg_ref, dl_ref, e_all, pick_ref = refs
        e_all[...] = jnp.zeros((rows, width), F32)
        for i in range(seqs):
            e_all[i * slots : i * slots + used] = e_refs[i][...] + e_refs[seqs + i][...]
        n, inverse = normed(live_ref[...])
        e = e_all[...]
        along = jnp.mean(e * n, axis=-1, keepdims=True)
        res_ref[...] = o_ref[...] + (e - jnp.mean(e, axis=-1, keepdims=True) - n * along) * inverse
        d_res = halves(res_ref[...])
        d_gated = dot(halves(w_ref[...]), d_res, NT)
        for i in range(seqs):
            pick = chosen(at_ref.at[i], slots, length)
            at = slice(i * slots, (i + 1) * slots)
            gate = [lax.dot_general(v, pick, (NT, ((), ())), preferred_element_type=F32) for v in halves(g_refs[i][...])]
            lng = [lax.dot_general(v, pick, (NT, ((), ())), preferred_element_type=F32) for v in halves(l_refs[i][...])]
            gate, lng = gate[0] + gate[1], lng[0] + lng[1]
            dg_ref[i] = d_gated[:, at] * lng
            dl_ref[i] = d_gated[:, at] * gate
            pick_ref[:, at] = gate * lng
        dw_ref[...] = dot(halves(pick_ref[...]), d_res, NN)

    return call(
        kernel, "live_mix", 20 * rows * width * own, 4 * (4 * own * length + 4 * rows * width),
        [live, d_out, *e_terms, w_out, *gating, *long_conv, places],
        [whole(rows, width)] * 2 + [whole(used, width)] * (2 * seqs) + [whole(own, width)]
        + [whole(own, length)] * (2 * seqs) + [whole(seqs, slots, 1)],
        [shaped(rows, width), shaped(own, width), shaped(seqs, own, slots), shaped(seqs, own, slots)],
        [whole(rows, width), whole(own, width), whole(seqs, own, slots), whole(seqs, own, slots)],
        scratch=[pltpu.VMEM((rows, width), F32), pltpu.VMEM((own, rows), F32)],
        after=after,
    )


def project_back(d_projected, n_both, w_turned, w_sum, s, after=()):
    channels, length = d_projected.shape
    width = n_both[0].shape[1]
    tokens = length // 4

    def kernel(s_ref, d_ref, nh, nl, wh, wl, *refs):
        sum_refs, e_refs, dw_ref = refs[:-5], refs[-5:-1], refs[-1]
        both = halves(d_ref[...])
        deal(s_ref[0] & 1, dot(both, (wh[...], wl[...]), TN), e_refs)
        part = dot(both, (nh[...], nl[...]), NN)

        @pl.when(pl.program_id(0) == 0)
        def _():
            dw_ref[...] = sum_refs[0][...] + part if sum_refs else part

        @pl.when(pl.program_id(0) == 1)
        def _():
            dw_ref[...] += part

    at = lambda i, s_ref: ((s_ref[0] >> 1) ^ i, 0)
    return call(
        kernel, "project_back", 12 * length * width * channels,
        4 * (2 * length * width + channels * (length + 3 * width)),
        [d_projected, *n_both, *w_turned, *w_sum],
        [pl.BlockSpec((channels, 2 * tokens), lambda i, s_ref: (0, (s_ref[0] >> 1) ^ i))]
        + [pl.BlockSpec((2 * tokens, width), at)] * 2 + [whole(channels, width)] * (2 + len(w_sum)),
        [shaped(tokens, width)] * 4 + [shaped(channels, width)],
        [whole(tokens, width)] * 4 + [whole(channels, width)],
        grid=(2,), scalars=[s.reshape(1)], after=after,
    )


def turn_back(turned, placed, w_out_part, after=()):
    channels, width = turned.shape
    own = w_out_part.shape[0]
    groups = lax.axis_size("batch")
    shards = width // own
    rows = own // groups
    wide = -(-(channels + 1) // 128) * 128

    def kernel(w_ref, p_ref, o_ref, out_ref, flat_ref):
        flat_ref[:channels] = w_ref[...]
        flat_ref[channels:] = jnp.zeros((wide - channels, width), F32)
        back = flat_ref[...].T
        for j in range(groups):
            for k in range(shards):
                at = (k * groups + j) * rows
                to = slice(k * rows, (k + 1) * rows)
                out_ref[j, to, : wide - 128] = back[at : at + rows, : wide - 128]
                out_ref[j, to, wide - 128 : wide] = back[at : at + rows, wide - 128 :] + p_ref[at : at + rows]
                out_ref[j, to, wide:] = o_ref[j * rows : (j + 1) * rows, k * own : (k + 1) * own]

    shape = (groups, shards * rows, wide + own)
    (out,) = call(
        kernel, "turn_back", 0, 8 * width * wide, [turned, placed, w_out_part],
        [whole(channels, width), whole(width, 128), whole(own, width)], [shaped(*shape)], [whole(*shape)],
        scratch=[pltpu.VMEM((wide, width), F32)], after=after,
    )
    return out


def finish(which, e_terms, x, d_residual, places, s, held, after=()):
    tokens, width = e_terms[0].shape
    seqs, slots, _ = places.shape

    def kernel(s_ref, e0, e1, e2, e3, x_ref, d_ref, at_ref, *refs):
        out_ref = refs[-1]
        e = (e0[...] + e1[...]) + (e2[...] + e3[...])
        n, inverse = normed(x_ref[0])
        along = jnp.mean(e * n, axis=-1, keepdims=True)
        here = lax.broadcasted_iota(jnp.int32, (slots, tokens), 1) + s_ref[0] * tokens
        pick = jnp.where(here == at_ref[0], 1.0, 0.0).astype(BF16)
        direct = chosen_rows(pick, halves(d_ref[...]), TN)
        out_ref[0] = (e - jnp.mean(e, axis=-1, keepdims=True) - n * along) * inverse + direct

    inputs = [*e_terms, x, d_residual, places, *held]
    one = pl.BlockSpec((1, tokens, width), lambda i, *_: (which, 0, 0))
    return pl.pallas_call(
        kernel,
        name="finish",
        out_shape=shaped(seqs, tokens, width),
        grid_spec=pltpu.PrefetchScalarGridSpec(
            num_scalar_prefetch=1,
            grid=(1,),
            in_specs=[whole(tokens, width)] * 4
            + [one, pl.BlockSpec((slots, width), lambda i, *_: (which, 0))]
            + [pl.BlockSpec((1, slots, 1), lambda i, *_: (which, 0, 0))]
            + [pl.BlockSpec(memory_space=pl.ANY)] * len(held),
            out_specs=one,
        ),
        input_output_aliases={len(inputs): 0} if held else {},
        compiler_params=pltpu.CompilerParams(vmem_limit_bytes=VMEM),
        cost_estimate=pl.CostEstimate(flops=10**6, bytes_accessed=10**6, transcendentals=0),
    )(s.reshape(1), *inputs)


def weight_grads(pieces, s, gain_one, gain_two, w_in, w_gate, w_up, own, units):
    rows, columns = pieces[0].shape
    start = columns - 2 * units
    shards = len(pieces)

    def kernel(s_ref, *refs):
        p_refs, refs = refs[:shards], refs[shards:]
        one_ref, two_ref, wi_ref, wg_ref, wu_ref, di_ref, dg_ref, du_ref, g1_ref, g2_ref, tap_ref = refs
        one, two = one_ref[...], two_ref[...]
        lane = 3 * own // 128 * 128
        tap_ref[...] = (p_refs[0][:, lane:start] + p_refs[1][:, lane:start]) + (
            p_refs[2][:, lane:start] + p_refs[3][:, lane:start]
        )
        for index in range(shards):

            @pl.when(s_ref[0] == index)
            def _(index=index):
                sum_one = jnp.zeros((rows, 1), F32)
                sum_two = jnp.zeros((rows, 1), F32)
                for d, p_ref in enumerate(p_refs):
                    k = index ^ d
                    for j in range(3):
                        at = slice((j * shards + k) * own, (j * shards + k + 1) * own)
                        part = p_ref[:, j * own : (j + 1) * own]
                        sum_one += jnp.sum(wi_ref[:, at] * part, axis=1, keepdims=True)
                        di_ref[:, at] = one * part
                    at = slice(k * units, (k + 1) * units)
                    for j, (w_ref, d_ref) in enumerate(((wg_ref, dg_ref), (wu_ref, du_ref))):
                        part = p_ref[:, start + j * units : start + (j + 1) * units]
                        sum_two += jnp.sum(w_ref[:, at] * part, axis=1, keepdims=True)
                        d_ref[:, at] = two * part
                g1_ref[...] = sum_one
                g2_ref[...] = sum_two

    inputs = [*pieces, gain_one[:, None], gain_two[:, None], w_in, w_gate, w_up]
    wide = start - 3 * own // 128 * 128
    outs = [w_in.shape, w_gate.shape, w_up.shape, (rows, 1), (rows, 1), (rows, wide)]
    return call(
        kernel, "weight_grads", 0, 0, inputs, [whole(*v.shape) for v in inputs],
        [shaped(*v) for v in outs], [whole(*v) for v in outs], scalars=[s.reshape(1)],
    )


def norm_pull(n, inverse, grad):
    along = jnp.mean(grad * n, axis=-1, keepdims=True)
    return (grad - jnp.mean(grad, axis=-1, keepdims=True) - n * along) * inverse


def together(*values):
    return lax.optimization_barrier(values)


def body(
    inputs,
    gain_one,
    w_in,
    conv_weight,
    kernel,
    w_out,
    gain_two,
    w_gate,
    w_up,
    w_down,
    mask_positions,
    mask_counts,
    grad_rows,
):
    shards = lax.axis_size("seq")
    groups = lax.axis_size("batch")
    s = lax.axis_index("seq")
    seqs, tokens, width = inputs.shape
    length = tokens * shards
    freqs = 2 * length
    own = width // shards
    rows = w_in.shape[0]
    units = w_gate.shape[1] // shards
    count = conv_weight.shape[1]
    extra = 3 * count // rows
    tables = phase_tables(freqs)

    slots = mask_positions.shape[1]
    pad = -slots % 128
    live = jnp.arange(slots, dtype=jnp.int32) < mask_counts[:, None]
    places = jnp.pad(jnp.where(live, mask_positions, -1), ((0, 0), (0, pad)), constant_values=-1)
    d_out = jnp.pad(jnp.where(live[:, :, None], grad_rows, 0.0), ((0, 0), (0, pad), (0, 0)))
    d_out = d_out.reshape(-1, width)
    places = places[:, :, None]

    w_pre = (gain_one[:, None] * w_in).reshape(rows, 3, shards, own).transpose(0, 2, 1, 3)
    w_pre = w_pre.reshape(rows, shards, 3 * own)
    carried = jnp.broadcast_to(conv_weight.reshape(rows, 1, extra), (rows, shards, extra))
    split = 3 * own + extra
    sent = columns_out(jnp.concatenate([w_pre, carried], axis=2), s)
    near_0 = (swap(inputs[0], "seq", 1), swap(inputs[0], "seq", 2))
    w_down_own = over_batch(w_down).reshape(units, width)
    sent, near_0, x_now, kernel_now, places, d_out = together(sent, near_0, inputs[1], kernel, places, d_out)
    w_out_turned = w_out.reshape(rows, shards, own).transpose(1, 0, 2).reshape(shards * rows, own)
    sent = jnp.concatenate([sent.reshape(shards * rows, split), w_out_turned], axis=1)

    wide = kernel_now.reshape(2, -1, RADIX, own)
    mirror = [(i, groups - 1 - i) for i in range(groups)]
    folded = lax.ppermute(wide[:, ::-1, :4:-1], "batch", mirror)
    near_1 = (swap(x_now, "seq", 1), swap(x_now, "seq", 2))
    near_1, near_0, folded, sent, w_down_own, w_gate_now, w_up_now = together(
        near_1, near_0, folded, sent, w_down_own, w_gate, w_up
    )
    w_pre = over_batch(sent).reshape(groups, shards, rows, split + own)
    base = over_batch(fold_base(wide, folded))

    far = (swap(near_0[0], "seq", 2), swap(near_1[1], "seq", 1))
    w_units = jnp.stack([gain_two[:, None] * w_gate_now, gain_two[:, None] * w_up_now], axis=1)
    w_units = w_units.reshape(rows, 2, shards, units).transpose(0, 2, 1, 3).reshape(rows, shards, 2 * units)
    far, w_units = together(far, columns_out(w_units, s))
    x_pieces = [(inputs[0], *near_0, far[0]), (inputs[1], *near_1, far[1])]
    arranged_0, w_pre = together(arrange(x_pieces[0], s), w_pre)
    w_units = over_batch(w_units.reshape(shards * rows, 2 * units))

    w_out_own = w_pre[..., split:].transpose(0, 2, 1, 3).reshape(own, width)
    w_turned = turn_in(w_pre, 3 * own)
    taps = w_pre[..., 3 * own : split].reshape(groups, shards, 3, count).transpose(2, 1, 0, 3)
    taps = lax.dynamic_index_in_dim(taps.reshape(3, 3, shards, own), s, axis=2, keepdims=False)
    taps = taps.transpose(1, 2, 0)

    def first_half(arranged):
        x_i, *n_i = arranged
        return x_i, n_i, project(w_turned, n_i).reshape(3, own, length)

    first_0 = first_half(arranged_0)
    first_1 = first_half(arrange(x_pieces[1], s, after=(first_0[2],)))
    w_out_there, (x_0, n_0, p_0), (x_1, n_1, p_1), w_turned, taps = together(
        from_others(w_out_own), first_0, first_1, w_turned, taps
    )
    gated_0, *mixed_0 = mix(p_0, taps, base, tables)
    there_0, (gated_1, *mixed_1) = together(from_others(gated_0), mix(p_1, taps, base, tables, after=(gated_0,)))
    n_one, projected = (n_0, n_1), (p_0, p_1)
    gating, long_conv, vals, spec = zip(mixed_0, mixed_1)
    w_out_pieces = (w_out_own, *w_out_there)

    residual_0 = add_mixer(x_0, (gated_0, *there_0), w_out_pieces, after=(gated_1,))
    w_units = split_units(w_units.reshape(groups, shards, rows, 2 * units), w_down_own, after=(residual_0,))
    w_units, w_down_own = w_units[:2], w_units[2:]
    down_0 = feed_forward(residual_0, w_units, w_down_own, s)
    there_1, down_0, residual_0, w_units, w_down_own = together(
        from_others(gated_1), down_0, residual_0, w_units, w_down_own
    )

    residual_1 = add_mixer(x_1, (gated_1, *there_1), w_out_pieces, after=(down_0[0],))
    lived = live_back((residual_0, residual_1), places, d_out, w_units, w_down_own, slots)
    out_0 = [down_0[0], swap(down_0[1], "seq", 1), swap(down_0[2], "seq", 2)]
    lived, residual_1, out_0 = together(lived, residual_1, out_0)
    live_rows, n_live, hidden, d_units, e_two = lived
    residual = (residual_0, residual_1)

    e_two = [e_two[:slots], e_two[slots:]]
    unit_part = unit_grads(n_live, d_units, hidden, d_out, shards)
    e_there, unit_part = together([swap(e, "seq", 1 + i) for i, e in enumerate(e_two)], unit_part)
    unit_sums = sum_over_batch(unit_part)

    e_two = [e + there for e, there in zip(e_two, e_there)]
    down_1 = feed_forward(residual_1, w_units, w_down_own, s, after=(unit_part,))
    e_there, down_1 = together([swap(e, "seq", 2 - i) for i, e in enumerate(e_two)], down_1)
    e_terms = [*e_two, *e_there]

    d_residual, w_out_part, d_gating, d_long = live_mix(live_rows, d_out, e_terms, w_out_own, gating, long_conv, places)
    kernel_part, taps_part, d_projected = (), 0.0, []
    for i in range(seqs):
        d_p, *kernel_part, d_taps = mix_back(
            i, places, d_gating, d_long, projected[i], taps, vals[i], spec[i], kernel_part, tables,
            after=d_projected[-1:],
        )
        taps_part = taps_part + d_taps[:, :, :3]
        d_projected.append(d_p)
    out_0 += [swap(down_0[3], "seq", 3)]
    out_1 = [down_1[0], swap(down_1[1], "seq", 1), swap(down_1[2], "seq", 2)]
    d_projected, (kernel_part,), taps_part, d_residual, w_out_part, out_0, out_1 = together(
        d_projected, kernel_part, taps_part, d_residual, w_out_part, out_0, out_1
    )

    e_0 = project_back(d_projected[0].reshape(3 * own, length), n_0, w_turned, (), s)
    out_1 += [swap(down_1[3], "seq", 3)]
    (*e_0, w_in_part), out_1, unit_sums, kernel_part = together(e_0, out_1, unit_sums, kernel_part)
    kernel_sum = sum_over_batch(kernel_part.reshape(groups, -1, 2 * own))

    e_1 = project_back(d_projected[1].reshape(3 * own, length), n_1, w_turned, (w_in_part,), s)
    placed = jnp.zeros((3, 3, shards, own), F32)
    taps_part = taps_part.transpose(2, 0, 1)[:, :, None]
    placed = lax.dynamic_update_slice(placed, taps_part, (0, 0, s, 0))
    placed = placed.reshape(3, shards, groups, count).transpose(1, 2, 0, 3).reshape(width, extra)
    free = 3 * own % 128
    placed = jnp.pad(placed, ((0, 0), (free, 128 - free - extra)))
    w_in_part = turn_back(e_1[4], placed, w_out_part)
    e_there = [swap(e_0[1], "seq", 1), swap(e_0[2], "seq", 2)]
    outputs = [
        added(out) + lax.dynamic_slice_in_dim(residual[i], s * tokens, tokens, axis=0)
        for i, out in enumerate((out_0, out_1))
    ]
    e_there, e_1, w_in_part = together(e_there, e_1[:4], w_in_part)
    w_in_sum = sum_over_batch(w_in_part)

    e_0 = [e_0[0], *e_there, swap(e_0[3], "seq", 3)]
    input_grad = finish(0, e_0, inputs, d_residual, places, s, ())
    outputs = jnp.stack(
        [
            added(out) + lax.dynamic_slice_in_dim(residual[i], s * tokens, tokens, axis=0)
            for i, out in enumerate((out_0, out_1))
        ]
    )
    kernel_sum = kernel_sum.reshape(FOLDED, -1, 2, own).transpose(2, 1, 0, 3)
    mirrored = lax.ppermute(kernel_sum[:, ::-1, 3:0:-1], "batch", mirror)
    e_1, w_in_sum, mirrored, outputs, input_grad = together(to_others(e_1), w_in_sum, mirrored, outputs, input_grad)

    w_back = jnp.concatenate([w_in_sum[:, :-own], unit_sums[:, : 2 * units]], axis=1)
    w_back = columns_there(w_back.reshape(shards, rows, -1), s)
    mirrored = jnp.stack([mirrored[0], -mirrored[1]])
    kernel_grad = jnp.concatenate([kernel_sum, mirrored], axis=2).reshape(kernel.shape)
    input_grad = finish(1, e_1, inputs, d_residual, places, s, (input_grad,))
    w_out_sum = w_in_sum[:, -own:].reshape(shards, rows, own).transpose(1, 0, 2).reshape(w_out.shape)
    w_down_sum = unit_sums[:, 2 * units :].reshape(w_down.shape)
    w_back, kernel_grad, input_grad, w_out_sum, w_down_sum = together(
        w_back, kernel_grad, input_grad, w_out_sum, w_down_sum
    )
    w_in_sum, w_gate_sum, w_up_sum, gain_one_sum, gain_two_sum, taps_sum = weight_grads(
        w_back, s, gain_one, gain_two, w_in, w_gate, w_up, own, units
    )
    taps_sum = taps_sum[:, free : free + extra].reshape(conv_weight.shape)

    return (
        outputs,
        input_grad,
        gain_one_sum[:, 0],
        w_in_sum,
        taps_sum,
        kernel_grad,
        w_out_sum,
        gain_two_sum[:, 0],
        w_gate_sum,
        w_up_sum,
        w_down_sum,
    )


def solution(mesh):
    split = ("seq", "batch")
    placed = (
        P("batch", "seq", None),
        P(split),
        P(split, None),
        P(None, split),
        P(None, "batch", "seq"),
        P(split, None),
        P(split),
        P(split, None),
        P(split, None),
        P(split, None),
        P("batch", None),
        P("batch"),
        P("batch", None, None),
    )
    return jax.shard_map(
        body,
        mesh=mesh,
        in_specs=placed,
        out_specs=(
            P("batch", "seq", None),
            P("batch", "seq", None),
            P(split),
            P(split, None),
            P(None, split),
            P(None, "batch", "seq"),
            P(split, None),
            P(split),
            P(split, None),
            P(split, None),
            P(split, None),
        ),
        check_vma=False,
    )
```

```python
import math

import jax
import jax.numpy as jnp
import numpy as np
from jax import lax
from jax.experimental import pallas as pl
from jax.experimental.pallas import tpu as pltpu
from jax.sharding import PartitionSpec as P

EPS = 1e-05
HIGH = lax.Precision.HIGH
RADIX = 8
FOLDED = 5
ROOT = math.sqrt(0.5)
VMEM = 56 * 1024 * 1024
COST = 20
NN = ((1,), (0,))
NT = ((1,), (1,))
TN = ((0,), (0,))
F32 = jnp.float32
BF16 = jnp.bfloat16


def contract(pattern, left_side, right_side):
    return jnp.einsum(pattern, left_side, right_side, precision=HIGH)


def swap(value, axis, distance):
    devices = lax.axis_size(axis)
    return lax.ppermute(value, axis, [(i, i ^ distance) for i in range(devices)])


def from_others(value):
    return [swap(value, "seq", d) for d in (1, 2, 3)]


def to_others(blocks):
    return [blocks[0]] + [swap(blocks[d], "seq", d) for d in (1, 2, 3)]


def to_all(value):
    return [value] + from_others(value)


def added(terms):
    return (terms[0] + terms[1]) + (terms[2] + terms[3])


def by_xor(pieces, index):
    count = len(pieces)
    out = []
    for k in range(count):
        chosen = pieces[k]
        for i in range(1, count):
            chosen = jnp.where(index == i, pieces[k ^ i], chosen)
        out.append(chosen)
    return out


def columns_out(shard, s):
    pieces = []
    for d in range(4):
        block = lax.dynamic_index_in_dim(shard, s ^ d, axis=1, keepdims=False)
        pieces.append(block if d == 0 else swap(block, "seq", d))
    return jnp.stack(by_xor(pieces, s))


def columns_there(own, s):
    pieces = []
    for d in range(4):
        block = lax.dynamic_index_in_dim(own, s ^ d, axis=0, keepdims=False)
        pieces.append(block if d == 0 else swap(block, "seq", d))
    return pieces


def over_batch(value):
    full = lax.all_gather(value, "batch", axis=0, tiled=True)
    return full.reshape((-1,) + value.shape)


def sum_over_batch(parts):
    flat = parts.reshape(-1, parts.shape[2])
    return lax.psum_scatter(flat, "batch", scatter_dimension=0, tiled=True)


def halves(value):
    high = value.astype(BF16)
    return high, (value - high.astype(F32)).astype(BF16)


def dot(left_side, right_side, dims):
    (a, b), (c, d) = left_side, right_side

    def product(x, y):
        return lax.dot_general(x, y, (dims, ((), ())), preferred_element_type=F32)

    return product(a, c) + (product(a, d) + product(b, c))


def chosen_rows(chosen, both, dims):
    high, low = both

    def product(x):
        return lax.dot_general(chosen, x, (dims, ((), ())), preferred_element_type=F32)

    return product(high) + product(low)


def normed(x):
    centered = x - jnp.mean(x, axis=-1, keepdims=True)
    inverse = lax.rsqrt(jnp.mean(centered * centered, axis=-1, keepdims=True) + EPS)
    return centered * inverse, inverse


def call(kernel, name, flops, moved, inputs, in_specs, outs, out_specs, grid=(1,), scratch=(), scalars=(), after=()):
    taken = len(scalars) + len(inputs)

    def run(*refs):
        kernel(*refs[:taken], *refs[taken + len(after) :])

    return pl.pallas_call(
        run,
        name=name,
        out_shape=tuple(outs),
        grid_spec=pltpu.PrefetchScalarGridSpec(
            num_scalar_prefetch=len(scalars),
            grid=grid,
            in_specs=list(in_specs) + [pl.BlockSpec(memory_space=pl.ANY)] * len(after),
            out_specs=tuple(out_specs),
            scratch_shapes=list(scratch),
        ),
        compiler_params=pltpu.CompilerParams(vmem_limit_bytes=VMEM),
        cost_estimate=pl.CostEstimate(flops=int(flops) // COST, bytes_accessed=int(moved) // COST, transcendentals=0),
    )(*scalars, *inputs, *after)


def shaped(*shape, dtype=F32):
    return jax.ShapeDtypeStruct(shape, dtype)


def whole(*shape):
    return pl.BlockSpec(shape, lambda *_: (0,) * len(shape))


def first(work):
    pl.when(pl.program_id(0) == 0)(work)


def fold_base(kernel, mirrored, after=()):
    _, turns, kept, own = mirrored.shape

    def run(k_ref, m_ref, out_ref):
        for phase in range(FOLDED):
            for part in range(2):
                value = k_ref[part, :, phase]
                if 0 < phase <= kept:
                    other = m_ref[part, :, phase - 1]
                    value = value + other if part == 0 else value - other
                out_ref[phase * turns : (phase + 1) * turns, part * own : (part + 1) * own] = value

    shape = (FOLDED * turns, 2 * own)
    (out,) = call(
        run, "fold_base", 0, 12 * shape[0] * shape[1], [kernel, mirrored],
        [whole(*kernel.shape), whole(*mirrored.shape)], [shaped(*shape)], [whole(*shape)], after=after,
    )
    return out


def turn_in(gathered, channels):
    groups, shards, rows, _ = gathered.shape
    width = groups * shards * rows
    wide = -(-channels // 128) * 128

    def kernel(w_ref, high_ref, low_ref, flat_ref):
        flat_ref[:, channels // 128 * 128 :] = jnp.zeros((width, wide - channels // 128 * 128), F32)
        for k in range(shards):
            for j in range(groups):
                at = (k * groups + j) * rows
                flat_ref[at : at + rows, :channels] = w_ref[j, k, :, :channels]
        turned = flat_ref[...].T
        high_ref[...], low_ref[...] = halves(turned[:channels])

    return call(
        kernel, "turn_in", 0, 4 * 2 * width * wide, [gathered], [whole(*gathered.shape)],
        [shaped(channels, width, dtype=BF16)] * 2, [whole(channels, width)] * 2,
        scratch=[pltpu.VMEM((width, wide), F32)],
    )


def split_units(gathered, after=()):
    groups, shards, rows, columns = gathered.shape
    width = groups * shards * rows

    def kernel(w_ref, high_ref, low_ref, flat_ref):
        for j in range(groups):
            flat_ref[j * rows : (j + 1) * rows] = w_ref[j, 0]
        high_ref[...], low_ref[...] = halves(flat_ref[...])

    part = pl.BlockSpec((groups * rows, columns), lambda i: (i, 0))
    return call(
        kernel, "split_units", 0, 8 * width * columns, [gathered],
        [pl.BlockSpec((groups, 1, rows, columns), lambda i: (0, i, 0, 0))],
        [shaped(width, columns, dtype=BF16)] * 2, [part, part], grid=(shards,),
        scratch=[pltpu.VMEM((groups * rows, columns), F32)], after=after,
    )


def split_down(weight, after=()):
    units, width = weight.shape

    def kernel(w_ref, high_ref, low_ref):
        high_ref[...], low_ref[...] = halves(w_ref[...])

    part = pl.BlockSpec((units // 2, width), lambda i: (i, 0))
    return call(
        kernel, "split_down", 0, 8 * units * width, [weight], [part],
        [shaped(units, width, dtype=BF16)] * 2, [part, part], grid=(2,), after=after,
    )


def arrange(which, near, far, s, after=()):
    _, tokens, width = near[0].shape
    length = 4 * tokens

    def kernel(s_ref, p0, p1, p2, p3, x_ref, high_ref, low_ref):
        for d, piece in enumerate((p0, p1, p2, p3)):

            @pl.when(pl.program_id(0) == d)
            def _(d=d, piece=piece):
                x = piece[...] if d == 3 else piece[0]
                x_ref[...] = x
                high_ref[...], low_ref[...] = halves(normed(x)[0])

    rows = pl.BlockSpec((tokens, width), lambda i, s_ref: (s_ref[0] ^ i, 0))
    return call(
        kernel, "arrange", 0, 12 * length * width, [*near, far],
        [pl.BlockSpec((1, tokens, width), lambda i, s_ref: (which, 0, 0))] * 3 + [whole(tokens, width)],
        [shaped(length, width), shaped(length, width, dtype=BF16), shaped(length, width, dtype=BF16)],
        [rows] * 3, grid=(4,), scalars=[s.reshape(1)], after=after,
    )


def project(w_turned, n_both, after=()):
    channels, width = w_turned[0].shape
    length = n_both[0].shape[0]
    tokens = length // 2

    def kernel(wh, wl, nh, nl, out_ref):
        out_ref[...] = dot((wh[...], wl[...]), (nh[...], nl[...]), NT)

    rows = pl.BlockSpec((tokens, width), lambda i: (i, 0))
    (out,) = call(
        kernel, "project", 6 * length * width * channels, 4 * (length * width + channels * (length + width)),
        [*w_turned, *n_both], [whole(channels, width)] * 2 + [rows] * 2,
        [shaped(channels, length)], [pl.BlockSpec((channels, tokens), lambda i: (0, i))], grid=(2,), after=after,
    )
    return out


def phase_tables(length):
    block = length // RADIX
    place = np.arange(block)[:, None]
    turn = np.arange(block)[None, :]
    tables = []
    for phase in range(FOLDED):
        angle = 2.0 * np.pi * ((RADIX * turn + phase) * place % length) / length
        cos, sin = np.cos(angle), np.sin(angle)
        tables.append(np.block([[cos, -sin], [sin, cos]]))
    table = np.stack(tables).astype(np.float32)
    high = table.astype(BF16)
    low = (table - high.astype(np.float32)).astype(BF16)
    return jnp.asarray(high), jnp.asarray(low)


def shift(value, step):
    length = value.shape[1]
    lane = lax.broadcasted_iota(jnp.int32, value.shape, 1)
    if step < 0:
        return jnp.where(lane == 0, 0.0, pltpu.roll(value, 1, 1))
    return jnp.where(lane == length - 1, 0.0, pltpu.roll(value, length - 1, 1))


def fold(value, phase, block):
    x0, x1, x2, x3 = [value[:, i * block : (i + 1) * block] for i in range(4)]
    if phase == 0:
        return (x0 + x2) + (x1 + x3)
    if phase == 4:
        return (x0 + x2) - (x1 + x3)
    if phase == 2:
        return jnp.concatenate([x0 - x2, x3 - x1], axis=1)
    slant, lean = (x1 - x3) * ROOT, (x1 + x3) * ROOT
    if phase == 1:
        return jnp.concatenate([x0 + slant, -x2 - lean], axis=1)
    return jnp.concatenate([x0 - slant, x2 - lean], axis=1)


def unfold(total_ref, value, phase, block):
    if phase == 0:
        terms = (value,) * 4
    elif phase == 4:
        terms = (value, -value, value, -value)
    else:
        real, imag = value[:, :block], value[:, block:]
        if phase == 2:
            terms = (real, -imag, -real, imag)
        elif phase == 1:
            terms = (real, ROOT * (real - imag), -imag, -ROOT * (real + imag))
        else:
            terms = (real, -ROOT * (real + imag), imag, ROOT * (real - imag))
    for i, term in enumerate(terms):
        cols = slice(i * block, (i + 1) * block)
        total_ref[:, cols] = term if phase == 0 else total_ref[:, cols] + term


def times(left_side, right_side, block, conj=False):
    a, b = left_side[:, :block], left_side[:, block:]
    c, d = right_side[:, :block], right_side[:, block:]
    if conj:
        d = -d
    return jnp.concatenate([a * c - b * d, a * d + b * c], axis=1)


def pair(phase):
    return 1.0 if phase in (0, 4) else 2.0


def depth(phase, block):
    return block if phase in (0, 4) else 2 * block


def mix(projected, taps, base, tables, after=()):
    own, length = projected.shape[1:]
    block = 2 * length // RADIX
    groups = base.shape[0]
    turns = block // groups
    if turns % 8:
        base = base.reshape(groups, FOLDED, turns, 2 * own)
        spectrum = pl.BlockSpec((groups, 1, turns, 2 * own), lambda i: (0, i, 0, 0))
    else:
        spectrum = pl.BlockSpec((groups, turns, 2 * own), lambda i: (0, i, 0))
    scale = 1.0 / math.sqrt(length)

    def kernel(p_ref, tap_ref, base_ref, th_ref, tl_ref, gated_ref, gating_ref, long_ref, vals_ref, spec_ref,
               mixed_ref, acc_ref, base_t):
        step = pl.program_id(0)

        @pl.when(step == 0)
        def _():
            for k in range(3):

                p = p_ref[k]
                tap = tap_ref[k]
                mixed = tap[:, 0:1] * shift(p, -1) + tap[:, 1:2] * p + tap[:, 2:3] * shift(p, 1)
                if k == 1:
                    gating_ref[...] = mixed
                else:
                    mixed_ref[k // 2 * own : (k // 2 + 1) * own] = mixed

        turned = base_ref[...].reshape(block, 2 * own).T
        base_t[:, :block] = turned[:own]
        base_t[:, block:] = turned[own:]

        for phase in range(FOLDED):

            @pl.when(step == phase)
            def _(phase=phase):
                deep = depth(phase, block)
                table = (th_ref[0, :deep], tl_ref[0, :deep])
                hats = dot(halves(fold(mixed_ref[...], phase, block)), table, NN)
                spec = base_t[...] + (pair(phase) * scale) * hats[:own]
                vals = hats[own:]
                spec_ref[0] = spec
                vals_ref[0] = vals
                unfold(acc_ref, dot(halves(times(spec, vals, block)), table, NT), phase, block)

        @pl.when(step == FOLDED - 1)
        def _():
            long_conv = acc_ref[...] * (0.5 / length)
            long_ref[...] = long_conv
            gated_ref[...] = gating_ref[...] * long_conv

    flat, hat = shaped(own, length), shaped(FOLDED, own, 2 * block)
    by_phase = lambda *shape: pl.BlockSpec((1,) + shape, lambda i, *_: (i,) + (0,) * len(shape))
    return call(
        kernel, "mix", 3 * 6 * own * 4 * length * length, 4 * own * length * 22,
        [projected, taps, base, *tables],
        [whole(3, own, length), whole(3, own, 3)]
        + [spectrum]
        + [by_phase(2 * block, 2 * block), by_phase(2 * block, 2 * block)],
        [flat, flat, flat, hat, hat],
        [whole(own, length)] * 3 + [by_phase(own, 2 * block)] * 2,
        grid=(FOLDED,),
        scratch=[
            pltpu.VMEM((2 * own, length), F32),
            pltpu.VMEM((own, length), F32),
            pltpu.VMEM((own, 2 * block), F32),
        ],
        after=after,
    )


def mix_back(places, d_gating, d_long, projected, taps, vals, spec, tables, after=()):
    seqs = len(projected)
    own, length = projected[0].shape[1:]
    block = vals[0].shape[2] // 2
    groups = lax.axis_size("batch")
    turns = block // groups
    slots = places.shape[1]
    scale = 1.0 / math.sqrt(length)

    def kernel(at_ref, dg_ref, dl_ref, tap_ref, *refs):
        p_refs, vals_refs, spec_refs, refs = refs[:seqs], refs[seqs : 2 * seqs], refs[2 * seqs : 3 * seqs], refs[3 * seqs :]
        th_ref, tl_ref, *refs = refs
        out_refs, (ker_ref, dtap_ref, long_ref, gating_ref, acc_ref) = refs[:seqs], refs[seqs:]
        step = pl.program_id(0)

        @pl.when(step == 0)
        def _():
            at = lax.broadcasted_iota(jnp.int32, (slots, length), 1)
            for i in range(seqs):
                pick = jnp.where(at == at_ref[i], 1.0, 0.0).astype(BF16)
                for source, target in ((dg_ref, gating_ref), (dl_ref, long_ref)):
                    high, low = halves(source[i])
                    target[i * own : (i + 1) * own] = lax.dot_general(
                        high, pick, (NN, ((), ())), preferred_element_type=F32
                    ) + lax.dot_general(low, pick, (NN, ((), ())), preferred_element_type=F32)

        for phase in range(FOLDED):

            @pl.when(step == phase)
            def _(phase=phase):
                deep = depth(phase, block)
                table = (th_ref[0, :deep], tl_ref[0, :deep])
                hats = dot(halves(fold(long_ref[...], phase, block)), table, NN) * (0.5 / length)
                both, kernel_sum = [], 0.0
                for i in range(seqs):
                    hat = hats[i * own : (i + 1) * own]
                    ker = times(hat, vals_refs[i][0], block, conj=True)
                    kernel_sum = kernel_sum + ker
                    both += [ker * (pair(phase) * scale), times(hat, spec_refs[i][0], block, conj=True)]
                turned = jnp.concatenate([kernel_sum[:, :block], kernel_sum[:, block:]], axis=0).T
                ker_ref[:, 0] = turned.reshape(groups, turns, 2 * own)
                unfold(acc_ref, dot(halves(jnp.concatenate(both, axis=0)), table, NT), phase, block)

        @pl.when(step == FOLDED - 1)
        def _():
            lane = lax.broadcasted_iota(jnp.int32, (own, 128), 1)
            for k in range(3):
                tap = tap_ref[k]
                sums = jnp.zeros((own, 128), F32)
                for i in range(seqs):
                    if k == 1:
                        grad = gating_ref[i * own : (i + 1) * own]
                    else:
                        at = 2 * i + k // 2
                        grad = acc_ref[at * own : (at + 1) * own]
                    p = p_refs[i][k]
                    out_refs[i][k] = tap[:, 0:1] * shift(grad, 1) + tap[:, 1:2] * grad + tap[:, 2:3] * shift(grad, -1)
                    for j, moved in enumerate((shift(p, -1), p, shift(p, 1))):
                        sums += jnp.where(lane == j, jnp.sum(moved * grad, axis=1, keepdims=True), 0.0)
                dtap_ref[k] = sums

    by_phase = lambda *shape: pl.BlockSpec((1,) + shape, lambda i: (i,) + (0,) * len(shape))
    flat = shaped(3, own, length)
    return call(
        kernel, "mix_back", seqs * 3 * 6 * own * 4 * length * length, seqs * 4 * own * length * 22,
        [places, d_gating, d_long, taps, *projected, *vals, *spec, *tables],
        [whole(seqs, slots, 1), whole(seqs, own, slots), whole(seqs, own, slots), whole(3, own, 3)]
        + [whole(3, own, length)] * seqs + [by_phase(own, 2 * block)] * (2 * seqs) + [by_phase(2 * block, 2 * block)] * 2,
        [flat] * seqs + [shaped(groups, FOLDED, turns, 2 * own), shaped(3, own, 128)],
        [whole(3, own, length)] * seqs
        + [pl.BlockSpec((groups, 1, turns, 2 * own), lambda i: (0, i, 0, 0)), whole(3, own, 128)],
        grid=(FOLDED,),
        scratch=[
            pltpu.VMEM((seqs * own, length), F32),
            pltpu.VMEM((seqs * own, length), F32),
            pltpu.VMEM((2 * seqs * own, length), F32),
        ],
        after=after,
    )


def add_mixer(x, gated, w_out, after=()):
    length, width = x.shape
    own = gated[0].shape[0]
    tokens = length // 2

    def kernel(x_ref, g0, g1, g2, g3, w0, w1, w2, w3, out_ref, wh, wl, gh, gl):
        @first
        def _():
            for d, ref in enumerate((w0, w1, w2, w3)):
                wh[d * own : (d + 1) * own], wl[d * own : (d + 1) * own] = halves(ref[...])

        for d, ref in enumerate((g0, g1, g2, g3)):
            gh[d * own : (d + 1) * own], gl[d * own : (d + 1) * own] = halves(ref[...])
        out_ref[...] = x_ref[...] + dot((gh[...], gl[...]), (wh[...], wl[...]), TN)

    rows = pl.BlockSpec((tokens, width), lambda i: (i, 0))
    (out,) = call(
        kernel, "add_mixer", 6 * length * width * width, 4 * (3 * length * width + width * width),
        [x, *gated, *w_out],
        [rows] + [pl.BlockSpec((own, tokens), lambda i: (0, i))] * 4 + [whole(own, width)] * 4,
        [shaped(length, width)], [rows], grid=(2,),
        scratch=[pltpu.VMEM((width, width), BF16)] * 2 + [pltpu.VMEM((width, tokens), BF16)] * 2,
        after=after,
    )
    return out


def gelu_parts(u):
    inner = math.sqrt(2.0 / math.pi) * (u + 0.044715 * (u * u * u))
    return 0.5 * (1.0 + jnp.tanh(inner))


def units_of(residual, w_units, after=()):
    length, width = residual.shape
    units = w_units[0].shape[1] // 2
    tokens = length // 4

    def kernel(r_ref, wh, wl, high_ref, low_ref):
        gate_up = []
        for i in range(2):
            rows = r_ref[i * tokens : (i + 1) * tokens]
            gate_up.append(dot(halves(normed(rows)[0]), (wh[...], wl[...]), NN))
        for i, v in enumerate(gate_up):
            at = slice(i * tokens, (i + 1) * tokens)
            high_ref[at], low_ref[at] = halves(v[:, :units] * gelu_parts(v[:, :units]) * v[:, units:])

    rows = lambda columns: pl.BlockSpec((2 * tokens, columns), lambda i: (i, 0))
    return call(
        kernel, "units_of", 12 * length * width * units, 4 * (2 * length * width + 2 * width * units),
        [residual, *w_units], [rows(width)] + [whole(width, 2 * units)] * 2,
        [shaped(length, units, dtype=BF16)] * 2, [rows(units)] * 2, grid=(2,), after=after,
    )


def down_of(hidden, w_down, s, after=()):
    length, units = hidden[0].shape
    width = w_down[0].shape[1]
    tokens = length // 4

    def kernel(s_ref, hh, hl, dh, dl, *out_refs):
        for i, out_ref in enumerate(out_refs):
            rows = pl.ds(pl.multiple_of((s_ref[0] ^ i) * tokens, tokens), tokens)
            out_ref[...] = dot((hh[rows], hl[rows]), (dh[...], dl[...]), NN)

    return call(
        kernel, "down_of", 6 * length * width * units, 4 * (2 * length * width + width * units),
        [*hidden, *w_down], [whole(length, units)] * 2 + [whole(units, width)] * 2,
        [shaped(tokens, width)] * 4, [whole(tokens, width)] * 4, scalars=[s.reshape(1)], after=after,
    )


def feed_forward(residual, w_units, w_down, s, after=()):
    length, width = residual.shape
    units = w_down[0].shape[0]
    tokens = length // 4

    def kernel(s_ref, r_ref, wh, wl, dh, dl, *out_refs):
        gate_up = []
        for i in range(4):
            rows = r_ref[pl.ds(pl.multiple_of((s_ref[0] ^ i) * tokens, tokens), tokens)]
            gate_up.append(dot(halves(normed(rows)[0]), (wh[...], wl[...]), NN))
        hidden = [halves(v[:, :units] * gelu_parts(v[:, :units]) * v[:, units:]) for v in gate_up]
        for both, out_ref in zip(hidden, out_refs):
            out_ref[...] = dot(both, (dh[...], dl[...]), NN)

    return call(
        kernel, "feed_forward", 18 * length * width * units, 4 * (2 * length * width + 3 * width * units),
        [residual, *w_units, *w_down],
        [whole(length, width)] + [whole(width, 2 * units)] * 2 + [whole(units, width)] * 2,
        [shaped(tokens, width)] * 4, [whole(tokens, width)] * 4,
        scalars=[s.reshape(1)], after=after,
    )


def chosen(at_ref, slots, length):
    lane = lax.broadcasted_iota(jnp.int32, (slots, length), 1)
    return jnp.where(lane == at_ref[...], 1.0, 0.0).astype(BF16)


def live_back(residual, x, gated, w_out, places, d_out, w_units, w_down, used, after=()):
    seqs = 1 + len(residual)
    length, width = x.shape
    own = gated[0].shape[0]
    slots = places.shape[1]
    units = w_down[0].shape[0]
    rows = seqs * slots

    def kernel(*refs):
        r_refs, refs = refs[: seqs - 1], refs[seqs - 1 :]
        x_ref, g_refs, w_refs, refs = refs[0], refs[1:5], refs[5:9], refs[9:]
        at_ref, o_ref, wh, wl, dh, dl, live_ref, n_ref, hid_ref, du_ref, e_ref = refs
        for i, ref in enumerate((*r_refs, x_ref)):
            pick = chosen(at_ref.at[i], slots, length)
            live_ref[i * slots : (i + 1) * slots] = chosen_rows(pick, halves(ref[...]), NN)
        mixed = jnp.concatenate([chosen_rows(pick, halves(ref[...]), NT) for ref in g_refs], axis=1)
        weight = jnp.concatenate([ref[...] for ref in w_refs], axis=0)
        live_ref[rows - slots :] += dot(halves(mixed), halves(weight), NN)
        n = normed(live_ref[...])[0]
        n_ref[...] = n
        gate_up = dot(halves(n), (wh[...], wl[...]), NN)
        d_hidden = dot(halves(o_ref[...]), (dh[...], dl[...]), NT)
        gate, up = gate_up[:, :units], gate_up[:, units:]
        half = gelu_parts(gate)
        slope = half + gate * 2.0 * half * (1.0 - half) * math.sqrt(2.0 / math.pi) * (1.0 + 0.134145 * (gate * gate))
        hid_ref[...] = gate * half * up
        d_units = jnp.concatenate([d_hidden * up * slope, d_hidden * (gate * half)], axis=1)
        du_ref[...] = d_units
        e = dot(halves(d_units), (wh[...], wl[...]), NT)
        for i in range(seqs):
            e_ref[i * used : (i + 1) * used] = e[i * slots : i * slots + used]

    return call(
        kernel, "live_back", 30 * rows * width * units, 4 * (2 * length * width + 4 * width * units),
        [*residual, x, *gated, *w_out, places, d_out, *w_units, *w_down],
        [whole(length, width)] * seqs + [whole(own, length)] * 4 + [whole(own, width)] * 4
        + [whole(seqs, slots, 1), whole(rows, width)] + [whole(width, 2 * units)] * 2 + [whole(units, width)] * 2,
        [shaped(rows, width), shaped(rows, width), shaped(rows, units), shaped(rows, 2 * units), shaped(seqs * used, width)],
        [whole(rows, width), whole(rows, width), whole(rows, units), whole(rows, 2 * units), whole(seqs * used, width)],
        after=after,
    )


def unit_grads(normed_live, d_units, hidden, d_out, shards, after=()):
    slots, width = normed_live.shape
    units = hidden.shape[1]
    groups = lax.axis_size("batch")
    rows = width // groups // shards
    down = units // groups

    def kernel(n_ref, u_ref, h_ref, o_ref, out_ref):
        @pl.when(pl.program_id(0) < 2)
        def _():
            part = dot(halves(n_ref[...]), halves(u_ref[...]), TN)
            for j in range(groups):
                for k in range(shards):
                    at = (k * groups + j) * rows
                    out_ref[j, k * rows : (k + 1) * rows] = part[at : at + rows]

        @pl.when(pl.program_id(0) == 2)
        def _():
            part = dot(halves(h_ref[...]), halves(o_ref[...]), TN)
            for j in range(groups):
                out_ref[j] = part[j * down : (j + 1) * down]

    (out,) = call(
        kernel, "unit_grads", 18 * slots * width * units, 4 * 3 * width * units,
        [normed_live, d_units, hidden, d_out],
        [
            whole(slots, width),
            pl.BlockSpec((slots, units), lambda i: (0, jnp.minimum(i, 1))),
            whole(slots, units),
            whole(slots, width),
        ],
        [shaped(groups, shards * rows, 2 * units + width)],
        [pl.BlockSpec((groups, shards * rows, width), lambda i: (0, 0, i))],
        grid=(3,), after=after,
    )
    return out


def live_mix(live, d_out, e_terms, w_out, gating, long_conv, places, after=()):
    seqs = len(gating)
    own, length = gating[0].shape
    rows, width = live.shape
    slots = rows // seqs
    used = e_terms[0].shape[0]

    def kernel(live_ref, o_ref, *refs):
        e_refs, w_ref, refs = refs[: 2 * seqs], refs[2 * seqs], refs[2 * seqs + 1 :]
        g_refs, l_refs, refs = refs[:seqs], refs[seqs : 2 * seqs], refs[2 * seqs :]
        at_ref, res_ref, dw_ref, dg_ref, dl_ref, e_all, pick_ref = refs
        e_all[...] = jnp.zeros((rows, width), F32)
        for i in range(seqs):
            e_all[i * slots : i * slots + used] = e_refs[i][...] + e_refs[seqs + i][...]
        n, inverse = normed(live_ref[...])
        e = e_all[...]
        along = jnp.mean(e * n, axis=-1, keepdims=True)
        res_ref[...] = o_ref[...] + (e - jnp.mean(e, axis=-1, keepdims=True) - n * along) * inverse
        d_res = halves(res_ref[...])
        d_gated = dot(halves(w_ref[...]), d_res, NT)
        for i in range(seqs):
            pick = chosen(at_ref.at[i], slots, length)
            at = slice(i * slots, (i + 1) * slots)
            gate = [lax.dot_general(v, pick, (NT, ((), ())), preferred_element_type=F32) for v in halves(g_refs[i][...])]
            lng = [lax.dot_general(v, pick, (NT, ((), ())), preferred_element_type=F32) for v in halves(l_refs[i][...])]
            gate, lng = gate[0] + gate[1], lng[0] + lng[1]
            dg_ref[i] = d_gated[:, at] * lng
            dl_ref[i] = d_gated[:, at] * gate
            pick_ref[:, at] = gate * lng
        dw_ref[...] = dot(halves(pick_ref[...]), d_res, NN)

    return call(
        kernel, "live_mix", 20 * rows * width * own, 4 * (4 * own * length + 4 * rows * width),
        [live, d_out, *e_terms, w_out, *gating, *long_conv, places],
        [whole(rows, width)] * 2 + [whole(used, width)] * (2 * seqs) + [whole(own, width)]
        + [whole(own, length)] * (2 * seqs) + [whole(seqs, slots, 1)],
        [shaped(rows, width), shaped(own, width), shaped(seqs, own, slots), shaped(seqs, own, slots)],
        [whole(rows, width), whole(own, width), whole(seqs, own, slots), whole(seqs, own, slots)],
        scratch=[pltpu.VMEM((rows, width), F32), pltpu.VMEM((own, rows), F32)],
        after=after,
    )


def project_back(d_projected, n_both, w_turned, w_sum, s, after=()):
    channels, length = d_projected.shape
    width = n_both[0].shape[1]
    tokens = length // 4

    def kernel(s_ref, d_ref, nh, nl, wh, wl, *refs):
        sum_refs, e_refs, dw_ref, ph, pl_ = refs[:-7], refs[-7:-3], refs[-3], refs[-2], refs[-1]
        ph[...], pl_[...] = halves(d_ref[...])
        part = dot((ph[...], pl_[...]), (nh[...], nl[...]), NN)
        dw_ref[...] = sum_refs[0][...] + part if sum_refs else part
        for i, e_ref in enumerate(e_refs):
            at = pl.ds(pl.multiple_of((s_ref[0] ^ i) * tokens, tokens), tokens)
            e_ref[...] = dot((ph[:, at], pl_[:, at]), (wh[...], wl[...]), TN)

    return call(
        kernel, "project_back", 12 * length * width * channels,
        4 * (2 * length * width + channels * (length + 3 * width)),
        [d_projected, *n_both, *w_turned, *w_sum],
        [whole(channels, length)] + [whole(length, width)] * 2 + [whole(channels, width)] * (2 + len(w_sum)),
        [shaped(tokens, width)] * 4 + [shaped(channels, width)],
        [whole(tokens, width)] * 4 + [whole(channels, width)],
        scratch=[pltpu.VMEM((channels, length), BF16)] * 2, scalars=[s.reshape(1)], after=after,
    )


def turn_back(turned, placed, w_out_part, after=()):
    channels, width = turned.shape
    own = w_out_part.shape[0]
    groups = lax.axis_size("batch")
    shards = width // own
    rows = own // groups
    wide = -(-(channels + 1) // 128) * 128

    def kernel(w_ref, p_ref, o_ref, out_ref, flat_ref):
        flat_ref[:channels] = w_ref[...]
        flat_ref[channels:] = jnp.zeros((wide - channels, width), F32)
        back = flat_ref[...].T
        for j in range(groups):
            for k in range(shards):
                at = (k * groups + j) * rows
                to = slice(k * rows, (k + 1) * rows)
                out_ref[j, to, : wide - 128] = back[at : at + rows, : wide - 128]
                out_ref[j, to, wide - 128 : wide] = back[at : at + rows, wide - 128 :] + p_ref[at : at + rows]
                out_ref[j, to, wide:] = o_ref[j * rows : (j + 1) * rows, k * own : (k + 1) * own]

    shape = (groups, shards * rows, wide + own)
    (out,) = call(
        kernel, "turn_back", 0, 8 * width * wide, [turned, placed, w_out_part],
        [whole(channels, width), whole(width, 128), whole(own, width)], [shaped(*shape)], [whole(*shape)],
        scratch=[pltpu.VMEM((wide, width), F32)], after=after,
    )
    return out


def finish(which, e_terms, x, d_residual, places, s, held, after=()):
    tokens, width = e_terms[0].shape
    seqs, slots, _ = places.shape

    def kernel(s_ref, e0, e1, e2, e3, x_ref, d_ref, at_ref, *refs):
        out_ref = refs[-1]
        e = (e0[...] + e1[...]) + (e2[...] + e3[...])
        n, inverse = normed(x_ref[0])
        along = jnp.mean(e * n, axis=-1, keepdims=True)
        here = lax.broadcasted_iota(jnp.int32, (slots, tokens), 1) + s_ref[0] * tokens
        pick = jnp.where(here == at_ref[0], 1.0, 0.0).astype(BF16)
        direct = chosen_rows(pick, halves(d_ref[...]), TN)
        out_ref[0] = (e - jnp.mean(e, axis=-1, keepdims=True) - n * along) * inverse + direct

    inputs = [*e_terms, x, d_residual, places, *held]
    one = pl.BlockSpec((1, tokens, width), lambda i, *_: (which, 0, 0))
    return pl.pallas_call(
        kernel,
        name="finish",
        out_shape=shaped(seqs, tokens, width),
        grid_spec=pltpu.PrefetchScalarGridSpec(
            num_scalar_prefetch=1,
            grid=(1,),
            in_specs=[whole(tokens, width)] * 4
            + [one, pl.BlockSpec((slots, width), lambda i, *_: (which, 0))]
            + [pl.BlockSpec((1, slots, 1), lambda i, *_: (which, 0, 0))]
            + [pl.BlockSpec(memory_space=pl.ANY)] * len(held),
            out_specs=one,
        ),
        input_output_aliases={len(inputs): 0} if held else {},
        compiler_params=pltpu.CompilerParams(vmem_limit_bytes=VMEM),
        cost_estimate=pl.CostEstimate(flops=10**6, bytes_accessed=10**6, transcendentals=0),
    )(s.reshape(1), *inputs)


def weight_grads(pieces, s, gain_one, gain_two, w_in, w_gate, w_up, own, units):
    rows, columns = pieces[0].shape
    start = columns - 2 * units
    shards = len(pieces)

    def kernel(s_ref, *refs):
        p_refs, refs = refs[:shards], refs[shards:]
        one_ref, two_ref, wi_ref, wg_ref, wu_ref, di_ref, dg_ref, du_ref, g1_ref, g2_ref, tap_ref = refs
        one, two = one_ref[...], two_ref[...]
        lane = 3 * own // 128 * 128
        tap_ref[...] = (p_refs[0][:, lane:start] + p_refs[1][:, lane:start]) + (
            p_refs[2][:, lane:start] + p_refs[3][:, lane:start]
        )
        for index in range(shards):

            @pl.when(s_ref[0] == index)
            def _(index=index):
                sum_one = jnp.zeros((rows, 1), F32)
                sum_two = jnp.zeros((rows, 1), F32)
                for d, p_ref in enumerate(p_refs):
                    k = index ^ d
                    for j in range(3):
                        at = slice((j * shards + k) * own, (j * shards + k + 1) * own)
                        part = p_ref[:, j * own : (j + 1) * own]
                        sum_one += jnp.sum(wi_ref[:, at] * part, axis=1, keepdims=True)
                        di_ref[:, at] = one * part
                    at = slice(k * units, (k + 1) * units)
                    for j, (w_ref, d_ref) in enumerate(((wg_ref, dg_ref), (wu_ref, du_ref))):
                        part = p_ref[:, start + j * units : start + (j + 1) * units]
                        sum_two += jnp.sum(w_ref[:, at] * part, axis=1, keepdims=True)
                        d_ref[:, at] = two * part
                g1_ref[...] = sum_one
                g2_ref[...] = sum_two

    inputs = [*pieces, gain_one[:, None], gain_two[:, None], w_in, w_gate, w_up]
    wide = start - 3 * own // 128 * 128
    outs = [w_in.shape, w_gate.shape, w_up.shape, (rows, 1), (rows, 1), (rows, wide)]
    return call(
        kernel, "weight_grads", 0, 0, inputs, [whole(*v.shape) for v in inputs],
        [shaped(*v) for v in outs], [whole(*v) for v in outs], scalars=[s.reshape(1)],
    )


def norm_pull(n, inverse, grad):
    along = jnp.mean(grad * n, axis=-1, keepdims=True)
    return (grad - jnp.mean(grad, axis=-1, keepdims=True) - n * along) * inverse


def together(*values):
    return lax.optimization_barrier(values)


def body(
    inputs,
    gain_one,
    w_in,
    conv_weight,
    kernel,
    w_out,
    gain_two,
    w_gate,
    w_up,
    w_down,
    mask_positions,
    mask_counts,
    grad_rows,
):
    shards = lax.axis_size("seq")
    groups = lax.axis_size("batch")
    s = lax.axis_index("seq")
    seqs, tokens, width = inputs.shape
    length = tokens * shards
    freqs = 2 * length
    own = width // shards
    rows = w_in.shape[0]
    units = w_gate.shape[1] // shards
    count = conv_weight.shape[1]
    extra = 3 * count // rows
    tables = phase_tables(freqs)

    slots = mask_positions.shape[1]
    pad = -slots % 128
    live = jnp.arange(slots, dtype=jnp.int32) < mask_counts[:, None]
    places = jnp.pad(jnp.where(live, mask_positions, -1), ((0, 0), (0, pad)), constant_values=-1)
    d_out = jnp.pad(jnp.where(live[:, :, None], grad_rows, 0.0), ((0, 0), (0, pad), (0, 0)))
    d_out = d_out.reshape(-1, width)
    places = places[:, :, None]

    w_pre = (gain_one[:, None] * w_in).reshape(rows, 3, shards, own).transpose(0, 2, 1, 3)
    w_pre = w_pre.reshape(rows, shards, 3 * own)
    carried = jnp.broadcast_to(conv_weight.reshape(rows, 1, extra), (rows, shards, extra))
    split = 3 * own + extra
    sent = columns_out(jnp.concatenate([w_pre, carried], axis=2), s)
    sent, x_now, kernel_now, places, d_out = together(sent, inputs, kernel, places, d_out)
    w_out_turned = w_out.reshape(rows, shards, own).transpose(1, 0, 2).reshape(shards * rows, own)
    w_pre = over_batch(jnp.concatenate([sent.reshape(shards * rows, split), w_out_turned], axis=1))
    w_pre = w_pre.reshape(groups, shards, rows, split + own)

    near = [swap(x_now, "seq", 1), swap(x_now, "seq", 2)]
    wide = kernel_now.reshape(2, -1, RADIX, own)
    mirror = [(i, groups - 1 - i) for i in range(groups)]
    folded = lax.ppermute(wide[:, ::-1, :4:-1], "batch", mirror)
    folded = fold_base(wide, folded)
    near, folded, w_gate_now, w_up_now = together(near, folded, w_gate, w_up)
    base = over_batch(folded)

    far = [swap(near[0][0], "seq", 2), swap(near[1][1], "seq", 1)]
    w_units = jnp.stack([gain_two[:, None] * w_gate_now, gain_two[:, None] * w_up_now], axis=1)
    w_units = w_units.reshape(rows, 2, shards, units).transpose(0, 2, 1, 3).reshape(rows, shards, 2 * units)
    w_turned = turn_in(w_pre, 3 * own)
    far, w_units, w_turned, w_pre, w_down_now = together(far, columns_out(w_units, s), w_turned, w_pre, w_down)
    w_units = over_batch(w_units.reshape(shards * rows, 2 * units))
    w_down_own = over_batch(w_down_now).reshape(units, width)

    w_out_own = w_pre[..., split:].transpose(0, 2, 1, 3).reshape(own, width)
    taps = w_pre[..., 3 * own : split].reshape(groups, shards, 3, count).transpose(2, 1, 0, 3)
    taps = lax.dynamic_index_in_dim(taps.reshape(3, 3, shards, own), s, axis=2, keepdims=False)
    taps = taps.transpose(1, 2, 0)

    def first_half(i, after=()):
        x_i, *n_i = arrange(i, (inputs, *near), far[i], s, after=after)
        return x_i, n_i, project(w_turned, n_i).reshape(3, own, length)

    x_0, n_0, p_0 = first_half(0)
    w_out_there, (gated_0, *mixed_0), x_0, n_0 = together(from_others(w_out_own), mix(p_0, taps, base, tables), x_0, n_0)
    x_1, n_1, p_1 = first_half(1, (gated_0,))
    there_0, (gated_1, *mixed_1), x_1, n_1 = together(from_others(gated_0), mix(p_1, taps, base, tables), x_1, n_1)
    n_one, projected = (n_0, n_1), (p_0, p_1)
    gating, long_conv, vals, spec = zip(mixed_0, mixed_1)
    w_out_pieces = (w_out_own, *w_out_there)

    residual_0 = add_mixer(x_0, (gated_0, *there_0), w_out_pieces, after=(gated_1,))
    w_units = split_units(w_units.reshape(groups, shards, rows, 2 * units), after=(residual_0,))
    hidden_0 = units_of(residual_0, w_units)
    w_down_own = split_down(w_down_own, after=(hidden_0[0],))
    down_0 = down_of(hidden_0, w_down_own, s)
    there_1, down_0, residual_0, w_units, w_down_own = together(
        from_others(gated_1), down_0, residual_0, w_units, w_down_own
    )

    lived = live_back(
        (residual_0,), x_1, (gated_1, *there_1), w_out_pieces, places, d_out, w_units, w_down_own, slots
    )
    live_rows, n_live, hidden, d_units, e_two = lived
    unit_part = unit_grads(n_live, d_units, hidden, d_out, shards)
    out_0 = [down_0[0], swap(down_0[1], "seq", 1), swap(down_0[2], "seq", 2)]
    live_rows, e_two, unit_part, out_0 = together(live_rows, e_two, unit_part, out_0)
    unit_sums = sum_over_batch(unit_part)

    e_two = [e_two[:slots], e_two[slots:]]
    residual_1 = add_mixer(x_1, (gated_1, *there_1), w_out_pieces, after=(unit_part,))
    e_there, residual_1 = together([swap(e, "seq", 1 + i) for i, e in enumerate(e_two)], residual_1)
    residual = (residual_0, residual_1)
    e_two = [e + there for e, there in zip(e_two, e_there)]
    down_1 = feed_forward(residual_1, w_units, w_down_own, s)
    e_there, down_1 = together([swap(e, "seq", 2 - i) for i, e in enumerate(e_two)], down_1)
    e_terms = [*e_two, *e_there]

    d_residual, w_out_part, d_gating, d_long = live_mix(live_rows, d_out, e_terms, w_out_own, gating, long_conv, places)
    *d_projected, kernel_part, taps_part = mix_back(
        places, d_gating, d_long, projected, taps, vals, spec, tables
    )
    taps_part = taps_part[:, :, :3]
    out_0 += [swap(down_0[3], "seq", 3)]
    out_1 = [down_1[0], swap(down_1[1], "seq", 1), swap(down_1[2], "seq", 2)]
    d_projected, kernel_part, taps_part, d_residual, w_out_part, out_0, out_1 = together(
        d_projected, kernel_part, taps_part, d_residual, w_out_part, out_0, out_1
    )

    e_0 = project_back(d_projected[0].reshape(3 * own, length), n_0, w_turned, (), s)
    out_1 += [swap(down_1[3], "seq", 3)]
    (*e_0, w_in_part), out_1, unit_sums, kernel_part = together(e_0, out_1, unit_sums, kernel_part)
    kernel_sum = sum_over_batch(kernel_part.reshape(groups, -1, 2 * own))

    e_1 = project_back(d_projected[1].reshape(3 * own, length), n_1, w_turned, (w_in_part,), s)
    placed = jnp.zeros((3, 3, shards, own), F32)
    taps_part = taps_part.transpose(2, 0, 1)[:, :, None]
    placed = lax.dynamic_update_slice(placed, taps_part, (0, 0, s, 0))
    placed = placed.reshape(3, shards, groups, count).transpose(1, 2, 0, 3).reshape(width, extra)
    free = 3 * own % 128
    placed = jnp.pad(placed, ((0, 0), (free, 128 - free - extra)))
    w_in_part = turn_back(e_1[4], placed, w_out_part)
    e_there = [swap(e_0[1], "seq", 1), swap(e_0[2], "seq", 2)]
    outputs = [
        added(out) + lax.dynamic_slice_in_dim(residual[i], s * tokens, tokens, axis=0)
        for i, out in enumerate((out_0, out_1))
    ]
    e_there, e_1, w_in_part = together(e_there, e_1[:4], w_in_part)
    w_in_sum = sum_over_batch(w_in_part)

    e_0 = [e_0[0], *e_there, swap(e_0[3], "seq", 3)]
    input_grad = finish(0, e_0, inputs, d_residual, places, s, ())
    outputs = jnp.stack(
        [
            added(out) + lax.dynamic_slice_in_dim(residual[i], s * tokens, tokens, axis=0)
            for i, out in enumerate((out_0, out_1))
        ]
    )
    kernel_sum = kernel_sum.reshape(FOLDED, -1, 2, own).transpose(2, 1, 0, 3)
    mirrored = lax.ppermute(kernel_sum[:, ::-1, 3:0:-1], "batch", mirror)
    e_1, w_in_sum, mirrored, outputs, input_grad = together(to_others(e_1), w_in_sum, mirrored, outputs, input_grad)

    w_back = jnp.concatenate([w_in_sum[:, :-own], unit_sums[:, : 2 * units]], axis=1)
    w_back = columns_there(w_back.reshape(shards, rows, -1), s)
    mirrored = jnp.stack([mirrored[0], -mirrored[1]])
    kernel_grad = jnp.concatenate([kernel_sum, mirrored], axis=2).reshape(kernel.shape)
    input_grad = finish(1, e_1, inputs, d_residual, places, s, (input_grad,))
    w_out_sum = w_in_sum[:, -own:].reshape(shards, rows, own).transpose(1, 0, 2).reshape(w_out.shape)
    w_down_sum = unit_sums[:, 2 * units :].reshape(w_down.shape)
    w_back, kernel_grad, input_grad, w_out_sum, w_down_sum = together(
        w_back, kernel_grad, input_grad, w_out_sum, w_down_sum
    )
    w_in_sum, w_gate_sum, w_up_sum, gain_one_sum, gain_two_sum, taps_sum = weight_grads(
        w_back, s, gain_one, gain_two, w_in, w_gate, w_up, own, units
    )
    taps_sum = taps_sum[:, free : free + extra].reshape(conv_weight.shape)

    return (
        outputs,
        input_grad,
        gain_one_sum.reshape(-1),
        w_in_sum,
        taps_sum,
        kernel_grad,
        w_out_sum,
        gain_two_sum.reshape(-1),
        w_gate_sum,
        w_up_sum,
        w_down_sum,
    )


def solution(mesh):
    split = ("seq", "batch")
    placed = (
        P("batch", "seq", None),
        P(split),
        P(split, None),
        P(None, split),
        P(None, "batch", "seq"),
        P(split, None),
        P(split),
        P(split, None),
        P(split, None),
        P(split, None),
        P("batch", None),
        P("batch"),
        P("batch", None, None),
    )
    return jax.shard_map(
        body,
        mesh=mesh,
        in_specs=placed,
        out_specs=(
            P("batch", "seq", None),
            P("batch", "seq", None),
            P(split),
            P(split, None),
            P(None, split),
            P(None, "batch", "seq"),
            P(split, None),
            P(split),
            P(split, None),
            P(split, None),
            P(split, None),
        ),
        check_vma=False,
    )
```

```python
import math

import jax
import jax.numpy as jnp
import numpy as np
from jax import lax
from jax.experimental import pallas as pl
from jax.experimental.pallas import tpu as pltpu
from jax.sharding import PartitionSpec as P

EPS = 1e-05
HIGH = lax.Precision.HIGH
RADIX = 8
FOLDED = 5
ROOT = math.sqrt(0.5)
VMEM = 56 * 1024 * 1024
COST = 20
NN = ((1,), (0,))
NT = ((1,), (1,))
TN = ((0,), (0,))
F32 = jnp.float32
BF16 = jnp.bfloat16


def contract(pattern, left_side, right_side):
    return jnp.einsum(pattern, left_side, right_side, precision=HIGH)


def swap(value, axis, distance):
    devices = lax.axis_size(axis)
    return lax.ppermute(value, axis, [(i, i ^ distance) for i in range(devices)])


def from_others(value):
    return [swap(value, "seq", d) for d in (1, 2, 3)]


def to_others(blocks):
    return [blocks[0]] + [swap(blocks[d], "seq", d) for d in (1, 2, 3)]


def to_all(value):
    return [value] + from_others(value)


def added(terms):
    return (terms[0] + terms[1]) + (terms[2] + terms[3])


def by_xor(pieces, index):
    count = len(pieces)
    out = []
    for k in range(count):
        chosen = pieces[k]
        for i in range(1, count):
            chosen = jnp.where(index == i, pieces[k ^ i], chosen)
        out.append(chosen)
    return out


def columns_out(shard, s):
    pieces = []
    for d in range(4):
        block = lax.dynamic_index_in_dim(shard, s ^ d, axis=1, keepdims=False)
        pieces.append(block if d == 0 else swap(block, "seq", d))
    return jnp.stack(by_xor(pieces, s))


def columns_there(own, s):
    pieces = []
    for d in range(4):
        block = lax.dynamic_index_in_dim(own, s ^ d, axis=0, keepdims=False)
        pieces.append(block if d == 0 else swap(block, "seq", d))
    return pieces


def over_batch(value):
    full = lax.all_gather(value, "batch", axis=0, tiled=True)
    return full.reshape((-1,) + value.shape)


def sum_over_batch(parts):
    flat = parts.reshape(-1, parts.shape[2])
    return lax.psum_scatter(flat, "batch", scatter_dimension=0, tiled=True)


def halves(value):
    high = value.astype(BF16)
    return high, (value - high.astype(F32)).astype(BF16)


def dot(left_side, right_side, dims):
    (a, b), (c, d) = left_side, right_side

    def product(x, y):
        return lax.dot_general(x, y, (dims, ((), ())), preferred_element_type=F32)

    return product(a, c) + (product(a, d) + product(b, c))


def chosen_rows(chosen, both, dims):
    high, low = both

    def product(x):
        return lax.dot_general(chosen, x, (dims, ((), ())), preferred_element_type=F32)

    return product(high) + product(low)


def normed(x):
    centered = x - jnp.mean(x, axis=-1, keepdims=True)
    inverse = lax.rsqrt(jnp.mean(centered * centered, axis=-1, keepdims=True) + EPS)
    return centered * inverse, inverse


def call(kernel, name, flops, moved, inputs, in_specs, outs, out_specs, grid=(1,), scratch=(), scalars=(), after=()):
    taken = len(scalars) + len(inputs)

    def run(*refs):
        kernel(*refs[:taken], *refs[taken + len(after) :])

    return pl.pallas_call(
        run,
        name=name,
        out_shape=tuple(outs),
        grid_spec=pltpu.PrefetchScalarGridSpec(
            num_scalar_prefetch=len(scalars),
            grid=grid,
            in_specs=list(in_specs) + [pl.BlockSpec(memory_space=pl.ANY)] * len(after),
            out_specs=tuple(out_specs),
            scratch_shapes=list(scratch),
        ),
        compiler_params=pltpu.CompilerParams(vmem_limit_bytes=VMEM),
        cost_estimate=pl.CostEstimate(flops=int(flops) // COST, bytes_accessed=int(moved) // COST, transcendentals=0),
    )(*scalars, *inputs, *after)


def shaped(*shape, dtype=F32):
    return jax.ShapeDtypeStruct(shape, dtype)


def whole(*shape):
    return pl.BlockSpec(shape, lambda *_: (0,) * len(shape))


def first(work):
    pl.when(pl.program_id(0) == 0)(work)


def fold_base(kernel, mirrored, after=()):
    _, turns, kept, own = mirrored.shape

    def run(k_ref, m_ref, out_ref):
        for phase in range(FOLDED):
            for part in range(2):
                value = k_ref[part, :, phase]
                if 0 < phase <= kept:
                    other = m_ref[part, :, phase - 1]
                    value = value + other if part == 0 else value - other
                out_ref[phase * turns : (phase + 1) * turns, part * own : (part + 1) * own] = value

    shape = (FOLDED * turns, 2 * own)
    (out,) = call(
        run, "fold_base", 0, 12 * shape[0] * shape[1], [kernel, mirrored],
        [whole(*kernel.shape), whole(*mirrored.shape)], [shaped(*shape)], [whole(*shape)], after=after,
    )
    return out


def turn_in(gathered, channels, split, after=()):
    groups, shards, rows, columns = gathered.shape
    width = groups * shards * rows
    own = columns - split
    wide = -(-channels // 128) * 128

    def kernel(w_ref, high_ref, low_ref, out_ref, flat_ref):
        flat_ref[:, channels // 128 * 128 :] = jnp.zeros((width, wide - channels // 128 * 128), F32)
        for k in range(shards):
            for j in range(groups):
                at = (k * groups + j) * rows
                flat_ref[at : at + rows, :channels] = w_ref[j, k, :, :channels]
                out_ref[j * rows : (j + 1) * rows, k * own : (k + 1) * own] = w_ref[j, k, :, split:]
        turned = flat_ref[...].T
        high_ref[...], low_ref[...] = halves(turned[:channels])

    return call(
        kernel, "turn_in", 0, 4 * 2 * width * wide, [gathered], [whole(*gathered.shape)],
        [shaped(channels, width, dtype=BF16)] * 2 + [shaped(groups * rows, width)],
        [whole(channels, width)] * 2 + [whole(groups * rows, width)],
        scratch=[pltpu.VMEM((width, wide), F32)], after=after,
    )


def split_units(gathered, after=()):
    groups, shards, rows, columns = gathered.shape
    width = groups * shards * rows

    def kernel(w_ref, high_ref, low_ref, flat_ref):
        for j in range(groups):
            flat_ref[j * rows : (j + 1) * rows] = w_ref[j, 0]
        high_ref[...], low_ref[...] = halves(flat_ref[...])

    part = pl.BlockSpec((groups * rows, columns), lambda i: (i, 0))
    return call(
        kernel, "split_units", 0, 8 * width * columns, [gathered],
        [pl.BlockSpec((groups, 1, rows, columns), lambda i: (0, i, 0, 0))],
        [shaped(width, columns, dtype=BF16)] * 2, [part, part], grid=(shards,),
        scratch=[pltpu.VMEM((groups * rows, columns), F32)], after=after,
    )


def split_down(weight, after=()):
    units, width = weight.shape

    def kernel(w_ref, high_ref, low_ref):
        high_ref[...], low_ref[...] = halves(w_ref[...])

    part = pl.BlockSpec((units // 2, width), lambda i: (i, 0))
    return call(
        kernel, "split_down", 0, 8 * units * width, [weight], [part],
        [shaped(units, width, dtype=BF16)] * 2, [part, part], grid=(2,), after=after,
    )


def arrange(which, near, far, s, after=()):
    _, tokens, width = near[0].shape
    length = 4 * tokens

    def kernel(s_ref, p0, p1, p2, p3, x_ref, high_ref, low_ref):
        for d, piece in enumerate((p0, p1, p2, p3)):

            @pl.when(pl.program_id(0) == d)
            def _(d=d, piece=piece):
                x = piece[...] if d == 3 else piece[0]
                x_ref[...] = x
                high_ref[...], low_ref[...] = halves(normed(x)[0])

    rows = pl.BlockSpec((tokens, width), lambda i, s_ref: (s_ref[0] ^ i, 0))
    return call(
        kernel, "arrange", 0, 12 * length * width, [*near, far],
        [pl.BlockSpec((1, tokens, width), lambda i, s_ref: (which, 0, 0))] * 3 + [whole(tokens, width)],
        [shaped(length, width), shaped(length, width, dtype=BF16), shaped(length, width, dtype=BF16)],
        [rows] * 3, grid=(4,), scalars=[s.reshape(1)], after=after,
    )


def project(w_turned, n_both, after=()):
    channels, width = w_turned[0].shape
    length = n_both[0].shape[0]
    tokens = length // 2

    def kernel(wh, wl, nh, nl, out_ref):
        out_ref[...] = dot((wh[...], wl[...]), (nh[...], nl[...]), NT)

    rows = pl.BlockSpec((tokens, width), lambda i: (i, 0))
    (out,) = call(
        kernel, "project", 6 * length * width * channels, 4 * (length * width + channels * (length + width)),
        [*w_turned, *n_both], [whole(channels, width)] * 2 + [rows] * 2,
        [shaped(channels, length)], [pl.BlockSpec((channels, tokens), lambda i: (0, i))], grid=(2,), after=after,
    )
    return out


def phase_tables(length):
    block = length // RADIX
    place = np.arange(block)[:, None]
    turn = np.arange(block)[None, :]
    tables = []
    for phase in range(FOLDED):
        angle = 2.0 * np.pi * ((RADIX * turn + phase) * place % length) / length
        cos, sin = np.cos(angle), np.sin(angle)
        tables.append(np.block([[cos, -sin], [sin, cos]]))
    table = np.stack(tables).astype(np.float32)
    high = table.astype(BF16)
    low = (table - high.astype(np.float32)).astype(BF16)
    return jnp.asarray(high), jnp.asarray(low)


def shift(value, step):
    length = value.shape[1]
    lane = lax.broadcasted_iota(jnp.int32, value.shape, 1)
    if step < 0:
        return jnp.where(lane == 0, 0.0, pltpu.roll(value, 1, 1))
    return jnp.where(lane == length - 1, 0.0, pltpu.roll(value, length - 1, 1))


def fold(value, phase, block):
    x0, x1, x2, x3 = [value[:, i * block : (i + 1) * block] for i in range(4)]
    if phase == 0:
        return (x0 + x2) + (x1 + x3)
    if phase == 4:
        return (x0 + x2) - (x1 + x3)
    if phase == 2:
        return jnp.concatenate([x0 - x2, x3 - x1], axis=1)
    slant, lean = (x1 - x3) * ROOT, (x1 + x3) * ROOT
    if phase == 1:
        return jnp.concatenate([x0 + slant, -x2 - lean], axis=1)
    return jnp.concatenate([x0 - slant, x2 - lean], axis=1)


def unfold(total_ref, value, phase, block):
    if phase == 0:
        terms = (value,) * 4
    elif phase == 4:
        terms = (value, -value, value, -value)
    else:
        real, imag = value[:, :block], value[:, block:]
        if phase == 2:
            terms = (real, -imag, -real, imag)
        elif phase == 1:
            terms = (real, ROOT * (real - imag), -imag, -ROOT * (real + imag))
        else:
            terms = (real, -ROOT * (real + imag), imag, ROOT * (real - imag))
    for i, term in enumerate(terms):
        cols = slice(i * block, (i + 1) * block)
        total_ref[:, cols] = term if phase == 0 else total_ref[:, cols] + term


def times(left_side, right_side, block, conj=False):
    a, b = left_side[:, :block], left_side[:, block:]
    c, d = right_side[:, :block], right_side[:, block:]
    if conj:
        d = -d
    return jnp.concatenate([a * c - b * d, a * d + b * c], axis=1)


def pair(phase):
    return 1.0 if phase in (0, 4) else 2.0


def depth(phase, block):
    return block if phase in (0, 4) else 2 * block


def mix(projected, taps, base, tables, after=()):
    own, length = projected.shape[1:]
    block = 2 * length // RADIX
    groups = base.shape[0]
    turns = block // groups
    if turns % 8:
        base = base.reshape(groups, FOLDED, turns, 2 * own)
        spectrum = pl.BlockSpec((groups, 1, turns, 2 * own), lambda i: (0, i, 0, 0))
    else:
        spectrum = pl.BlockSpec((groups, turns, 2 * own), lambda i: (0, i, 0))
    scale = 1.0 / math.sqrt(length)

    def kernel(p_ref, tap_ref, base_ref, th_ref, tl_ref, gated_ref, gating_ref, long_ref, vals_ref, spec_ref,
               mixed_ref, acc_ref, base_t):
        step = pl.program_id(0)

        @pl.when(step == 0)
        def _():
            for k in range(3):

                p = p_ref[k]
                tap = tap_ref[k]
                mixed = tap[:, 0:1] * shift(p, -1) + tap[:, 1:2] * p + tap[:, 2:3] * shift(p, 1)
                if k == 1:
                    gating_ref[...] = mixed
                else:
                    mixed_ref[k // 2 * own : (k // 2 + 1) * own] = mixed

        turned = base_ref[...].reshape(block, 2 * own).T
        base_t[:, :block] = turned[:own]
        base_t[:, block:] = turned[own:]

        for phase in range(FOLDED):

            @pl.when(step == phase)
            def _(phase=phase):
                deep = depth(phase, block)
                table = (th_ref[0, :deep], tl_ref[0, :deep])
                hats = dot(halves(fold(mixed_ref[...], phase, block)), table, NN)
                spec = base_t[...] + (pair(phase) * scale) * hats[:own]
                vals = hats[own:]
                spec_ref[0] = spec
                vals_ref[0] = vals
                unfold(acc_ref, dot(halves(times(spec, vals, block)), table, NT), phase, block)

        @pl.when(step == FOLDED - 1)
        def _():
            long_conv = acc_ref[...] * (0.5 / length)
            long_ref[...] = long_conv
            gated_ref[...] = gating_ref[...] * long_conv

    flat, hat = shaped(own, length), shaped(FOLDED, own, 2 * block)
    by_phase = lambda *shape: pl.BlockSpec((1,) + shape, lambda i, *_: (i,) + (0,) * len(shape))
    return call(
        kernel, "mix", 3 * 6 * own * 4 * length * length, 4 * own * length * 22,
        [projected, taps, base, *tables],
        [whole(3, own, length), whole(3, own, 3)]
        + [spectrum]
        + [by_phase(2 * block, 2 * block), by_phase(2 * block, 2 * block)],
        [flat, flat, flat, hat, hat],
        [whole(own, length)] * 3 + [by_phase(own, 2 * block)] * 2,
        grid=(FOLDED,),
        scratch=[
            pltpu.VMEM((2 * own, length), F32),
            pltpu.VMEM((own, length), F32),
            pltpu.VMEM((own, 2 * block), F32),
        ],
        after=after,
    )


def mix_back(places, d_gating, d_long, projected, taps, vals, spec, tables, after=()):
    seqs = len(projected)
    own, length = projected[0].shape[1:]
    block = vals[0].shape[2] // 2
    groups = lax.axis_size("batch")
    turns = block // groups
    slots = places.shape[1]
    scale = 1.0 / math.sqrt(length)

    def kernel(at_ref, dg_ref, dl_ref, tap_ref, *refs):
        p_refs, vals_refs, spec_refs, refs = refs[:seqs], refs[seqs : 2 * seqs], refs[2 * seqs : 3 * seqs], refs[3 * seqs :]
        th_ref, tl_ref, *refs = refs
        out_refs, (ker_ref, dtap_ref, long_ref, gating_ref, acc_ref) = refs[:seqs], refs[seqs:]
        step = pl.program_id(0)

        @pl.when(step == 0)
        def _():
            at = lax.broadcasted_iota(jnp.int32, (slots, length), 1)
            for i in range(seqs):
                pick = jnp.where(at == at_ref[i], 1.0, 0.0).astype(BF16)
                for source, target in ((dg_ref, gating_ref), (dl_ref, long_ref)):
                    high, low = halves(source[i])
                    target[i * own : (i + 1) * own] = lax.dot_general(
                        high, pick, (NN, ((), ())), preferred_element_type=F32
                    ) + lax.dot_general(low, pick, (NN, ((), ())), preferred_element_type=F32)

        for phase in range(FOLDED):

            @pl.when(step == phase)
            def _(phase=phase):
                deep = depth(phase, block)
                table = (th_ref[0, :deep], tl_ref[0, :deep])
                hats = dot(halves(fold(long_ref[...], phase, block)), table, NN) * (0.5 / length)
                both, kernel_sum = [], 0.0
                for i in range(seqs):
                    hat = hats[i * own : (i + 1) * own]
                    ker = times(hat, vals_refs[i][0], block, conj=True)
                    kernel_sum = kernel_sum + ker
                    both += [ker * (pair(phase) * scale), times(hat, spec_refs[i][0], block, conj=True)]
                turned = jnp.concatenate([kernel_sum[:, :block], kernel_sum[:, block:]], axis=0).T
                ker_ref[:, 0] = turned.reshape(groups, turns, 2 * own)
                unfold(acc_ref, dot(halves(jnp.concatenate(both, axis=0)), table, NT), phase, block)

        @pl.when(step == FOLDED - 1)
        def _():
            lane = lax.broadcasted_iota(jnp.int32, (own, 128), 1)
            for k in range(3):
                tap = tap_ref[k]
                sums = jnp.zeros((own, 128), F32)
                for i in range(seqs):
                    if k == 1:
                        grad = gating_ref[i * own : (i + 1) * own]
                    else:
                        at = 2 * i + k // 2
                        grad = acc_ref[at * own : (at + 1) * own]
                    p = p_refs[i][k]
                    out_refs[i][k] = tap[:, 0:1] * shift(grad, 1) + tap[:, 1:2] * grad + tap[:, 2:3] * shift(grad, -1)
                    for j, moved in enumerate((shift(p, -1), p, shift(p, 1))):
                        sums += jnp.where(lane == j, jnp.sum(moved * grad, axis=1, keepdims=True), 0.0)
                dtap_ref[k] = sums

    by_phase = lambda *shape: pl.BlockSpec((1,) + shape, lambda i: (i,) + (0,) * len(shape))
    flat = shaped(3, own, length)
    return call(
        kernel, "mix_back", seqs * 3 * 6 * own * 4 * length * length, seqs * 4 * own * length * 22,
        [places, d_gating, d_long, taps, *projected, *vals, *spec, *tables],
        [whole(seqs, slots, 1), whole(seqs, own, slots), whole(seqs, own, slots), whole(3, own, 3)]
        + [whole(3, own, length)] * seqs + [by_phase(own, 2 * block)] * (2 * seqs) + [by_phase(2 * block, 2 * block)] * 2,
        [flat] * seqs + [shaped(groups, FOLDED, turns, 2 * own), shaped(3, own, 128)],
        [whole(3, own, length)] * seqs
        + [pl.BlockSpec((groups, 1, turns, 2 * own), lambda i: (0, i, 0, 0)), whole(3, own, 128)],
        grid=(FOLDED,),
        scratch=[
            pltpu.VMEM((seqs * own, length), F32),
            pltpu.VMEM((seqs * own, length), F32),
            pltpu.VMEM((2 * seqs * own, length), F32),
        ],
        after=after,
    )


def add_mixer(x, gated, w_out, after=()):
    length, width = x.shape
    own = gated[0].shape[0]
    tokens = length // 2

    def kernel(x_ref, g0, g1, g2, g3, w0, w1, w2, w3, out_ref, wh, wl, gh, gl):
        @first
        def _():
            for d, ref in enumerate((w0, w1, w2, w3)):
                wh[d * own : (d + 1) * own], wl[d * own : (d + 1) * own] = halves(ref[...])

        for d, ref in enumerate((g0, g1, g2, g3)):
            gh[d * own : (d + 1) * own], gl[d * own : (d + 1) * own] = halves(ref[...])
        out_ref[...] = x_ref[...] + dot((gh[...], gl[...]), (wh[...], wl[...]), TN)

    rows = pl.BlockSpec((tokens, width), lambda i: (i, 0))
    (out,) = call(
        kernel, "add_mixer", 6 * length * width * width, 4 * (3 * length * width + width * width),
        [x, *gated, *w_out],
        [rows] + [pl.BlockSpec((own, tokens), lambda i: (0, i))] * 4 + [whole(own, width)] * 4,
        [shaped(length, width)], [rows], grid=(2,),
        scratch=[pltpu.VMEM((width, width), BF16)] * 2 + [pltpu.VMEM((width, tokens), BF16)] * 2,
        after=after,
    )
    return out


def gelu_parts(u):
    inner = math.sqrt(2.0 / math.pi) * (u + 0.044715 * (u * u * u))
    return 0.5 * (1.0 + jnp.tanh(inner))


def units_of(residual, w_units, after=()):
    length, width = residual.shape
    units = w_units[0].shape[1] // 2
    tokens = length // 4

    def kernel(r_ref, wh, wl, high_ref, low_ref):
        gate_up = []
        for i in range(2):
            rows = r_ref[i * tokens : (i + 1) * tokens]
            gate_up.append(dot(halves(normed(rows)[0]), (wh[...], wl[...]), NN))
        for i, v in enumerate(gate_up):
            at = slice(i * tokens, (i + 1) * tokens)
            high_ref[at], low_ref[at] = halves(v[:, :units] * gelu_parts(v[:, :units]) * v[:, units:])

    rows = lambda columns: pl.BlockSpec((2 * tokens, columns), lambda i: (i, 0))
    return call(
        kernel, "units_of", 12 * length * width * units, 4 * (2 * length * width + 2 * width * units),
        [residual, *w_units], [rows(width)] + [whole(width, 2 * units)] * 2,
        [shaped(length, units, dtype=BF16)] * 2, [rows(units)] * 2, grid=(2,), after=after,
    )


def down_of(hidden, w_down, s, after=()):
    length, units = hidden[0].shape
    width = w_down[0].shape[1]
    tokens = length // 4

    def kernel(s_ref, hh, hl, dh, dl, *out_refs):
        for i, out_ref in enumerate(out_refs):
            rows = pl.ds(pl.multiple_of((s_ref[0] ^ i) * tokens, tokens), tokens)
            out_ref[...] = dot((hh[rows], hl[rows]), (dh[...], dl[...]), NN)

    return call(
        kernel, "down_of", 6 * length * width * units, 4 * (2 * length * width + width * units),
        [*hidden, *w_down], [whole(length, units)] * 2 + [whole(units, width)] * 2,
        [shaped(tokens, width)] * 4, [whole(tokens, width)] * 4, scalars=[s.reshape(1)], after=after,
    )


def feed_forward(residual, w_units, w_down, s, after=()):
    length, width = residual.shape
    units = w_down[0].shape[0]
    tokens = length // 4

    def kernel(s_ref, r_ref, wh, wl, dh, dl, *out_refs):
        gate_up = []
        for i in range(4):
            rows = r_ref[pl.ds(pl.multiple_of((s_ref[0] ^ i) * tokens, tokens), tokens)]
            gate_up.append(dot(halves(normed(rows)[0]), (wh[...], wl[...]), NN))
        hidden = [halves(v[:, :units] * gelu_parts(v[:, :units]) * v[:, units:]) for v in gate_up]
        for both, out_ref in zip(hidden, out_refs):
            out_ref[...] = dot(both, (dh[...], dl[...]), NN)

    return call(
        kernel, "feed_forward", 18 * length * width * units, 4 * (2 * length * width + 3 * width * units),
        [residual, *w_units, *w_down],
        [whole(length, width)] + [whole(width, 2 * units)] * 2 + [whole(units, width)] * 2,
        [shaped(tokens, width)] * 4, [whole(tokens, width)] * 4,
        scalars=[s.reshape(1)], after=after,
    )


def chosen(at_ref, slots, length):
    lane = lax.broadcasted_iota(jnp.int32, (slots, length), 1)
    return jnp.where(lane == at_ref[...], 1.0, 0.0).astype(BF16)


def live_back(residual, x, gated, w_out, places, d_out, w_units, w_down, used, after=()):
    seqs = 1 + len(residual)
    length, width = x.shape
    own = gated[0].shape[0]
    slots = places.shape[1]
    units = w_down[0].shape[0]
    rows = seqs * slots

    def kernel(*refs):
        r_refs, refs = refs[: seqs - 1], refs[seqs - 1 :]
        x_ref, g_refs, w_refs, refs = refs[0], refs[1:5], refs[5:9], refs[9:]
        at_ref, o_ref, wh, wl, dh, dl, live_ref, n_ref, hid_ref, du_ref, e_ref = refs
        for i, ref in enumerate((*r_refs, x_ref)):
            pick = chosen(at_ref.at[i], slots, length)
            live_ref[i * slots : (i + 1) * slots] = chosen_rows(pick, halves(ref[...]), NN)
        mixed = []
        for ref in g_refs:
            parts = [lax.dot_general(v, pick, (NT, ((), ())), preferred_element_type=F32) for v in halves(ref[...])]
            mixed.append(parts[0] + parts[1])
        weight = jnp.concatenate([ref[...] for ref in w_refs], axis=0)
        live_ref[rows - slots :] += dot(halves(jnp.concatenate(mixed, axis=0)), halves(weight), TN)
        n = normed(live_ref[...])[0]
        n_ref[...] = n
        gate_up = dot(halves(n), (wh[...], wl[...]), NN)
        d_hidden = dot(halves(o_ref[...]), (dh[...], dl[...]), NT)
        gate, up = gate_up[:, :units], gate_up[:, units:]
        half = gelu_parts(gate)
        slope = half + gate * 2.0 * half * (1.0 - half) * math.sqrt(2.0 / math.pi) * (1.0 + 0.134145 * (gate * gate))
        hid_ref[...] = gate * half * up
        d_units = jnp.concatenate([d_hidden * up * slope, d_hidden * (gate * half)], axis=1)
        du_ref[...] = d_units
        e = dot(halves(d_units), (wh[...], wl[...]), NT)
        for i in range(seqs):
            e_ref[i * used : (i + 1) * used] = e[i * slots : i * slots + used]

    return call(
        kernel, "live_back", 30 * rows * width * units, 4 * (2 * length * width + 4 * width * units),
        [*residual, x, *gated, *w_out, places, d_out, *w_units, *w_down],
        [whole(length, width)] * seqs + [whole(own, length)] * 4 + [whole(own, width)] * 4
        + [whole(seqs, slots, 1), whole(rows, width)] + [whole(width, 2 * units)] * 2 + [whole(units, width)] * 2,
        [shaped(rows, width), shaped(rows, width), shaped(rows, units), shaped(rows, 2 * units), shaped(seqs * used, width)],
        [whole(rows, width), whole(rows, width), whole(rows, units), whole(rows, 2 * units), whole(seqs * used, width)],
        after=after,
    )


def unit_grads(normed_live, d_units, hidden, d_out, shards, after=()):
    slots, width = normed_live.shape
    units = hidden.shape[1]
    groups = lax.axis_size("batch")
    rows = width // groups // shards
    down = units // groups

    def kernel(n_ref, u_ref, h_ref, o_ref, out_ref):
        @pl.when(pl.program_id(0) < 2)
        def _():
            part = dot(halves(n_ref[...]), halves(u_ref[...]), TN)
            for j in range(groups):
                for k in range(shards):
                    at = (k * groups + j) * rows
                    out_ref[j, k * rows : (k + 1) * rows] = part[at : at + rows]

        @pl.when(pl.program_id(0) == 2)
        def _():
            part = dot(halves(h_ref[...]), halves(o_ref[...]), TN)
            for j in range(groups):
                out_ref[j] = part[j * down : (j + 1) * down]

    (out,) = call(
        kernel, "unit_grads", 18 * slots * width * units, 4 * 3 * width * units,
        [normed_live, d_units, hidden, d_out],
        [
            whole(slots, width),
            pl.BlockSpec((slots, units), lambda i: (0, jnp.minimum(i, 1))),
            whole(slots, units),
            whole(slots, width),
        ],
        [shaped(groups, shards * rows, 2 * units + width)],
        [pl.BlockSpec((groups, shards * rows, width), lambda i: (0, 0, i))],
        grid=(3,), after=after,
    )
    return out


def live_mix(live, d_out, e_terms, w_out, gating, long_conv, places, after=()):
    seqs = len(gating)
    own, length = gating[0].shape
    rows, width = live.shape
    slots = rows // seqs
    used = e_terms[0].shape[0]

    def kernel(live_ref, o_ref, *refs):
        e_refs, w_ref, refs = refs[: 2 * seqs], refs[2 * seqs], refs[2 * seqs + 1 :]
        g_refs, l_refs, refs = refs[:seqs], refs[seqs : 2 * seqs], refs[2 * seqs :]
        at_ref, res_ref, dw_ref, dg_ref, dl_ref, e_all, pick_ref = refs
        e_all[...] = jnp.zeros((rows, width), F32)
        for i in range(seqs):
            e_all[i * slots : i * slots + used] = e_refs[i][...] + e_refs[seqs + i][...]
        n, inverse = normed(live_ref[...])
        e = e_all[...]
        along = jnp.mean(e * n, axis=-1, keepdims=True)
        res_ref[...] = o_ref[...] + (e - jnp.mean(e, axis=-1, keepdims=True) - n * along) * inverse
        d_res = halves(res_ref[...])
        d_gated = dot(halves(w_ref[...]), d_res, NT)
        for i in range(seqs):
            pick = chosen(at_ref.at[i], slots, length)
            at = slice(i * slots, (i + 1) * slots)
            gate = [lax.dot_general(v, pick, (NT, ((), ())), preferred_element_type=F32) for v in halves(g_refs[i][...])]
            lng = [lax.dot_general(v, pick, (NT, ((), ())), preferred_element_type=F32) for v in halves(l_refs[i][...])]
            gate, lng = gate[0] + gate[1], lng[0] + lng[1]
            dg_ref[i] = d_gated[:, at] * lng
            dl_ref[i] = d_gated[:, at] * gate
            pick_ref[:, at] = gate * lng
        dw_ref[...] = dot(halves(pick_ref[...]), d_res, NN)

    return call(
        kernel, "live_mix", 20 * rows * width * own, 4 * (4 * own * length + 4 * rows * width),
        [live, d_out, *e_terms, w_out, *gating, *long_conv, places],
        [whole(rows, width)] * 2 + [whole(used, width)] * (2 * seqs) + [whole(own, width)]
        + [whole(own, length)] * (2 * seqs) + [whole(seqs, slots, 1)],
        [shaped(rows, width), shaped(own, width), shaped(seqs, own, slots), shaped(seqs, own, slots)],
        [whole(rows, width), whole(own, width), whole(seqs, own, slots), whole(seqs, own, slots)],
        scratch=[pltpu.VMEM((rows, width), F32), pltpu.VMEM((own, rows), F32)],
        after=after,
    )


def project_back(d_projected, n_both, w_turned, w_sum, s, after=()):
    channels, length = d_projected.shape
    width = n_both[0].shape[1]
    tokens = length // 4

    def kernel(s_ref, d_ref, nh, nl, wh, wl, *refs):
        sum_refs, e_refs, dw_ref, ph, pl_ = refs[:-7], refs[-7:-3], refs[-3], refs[-2], refs[-1]
        ph[...], pl_[...] = halves(d_ref[...])
        part = dot((ph[...], pl_[...]), (nh[...], nl[...]), NN)
        dw_ref[...] = sum_refs[0][...] + part if sum_refs else part
        for i, e_ref in enumerate(e_refs):
            at = pl.ds(pl.multiple_of((s_ref[0] ^ i) * tokens, tokens), tokens)
            e_ref[...] = dot((ph[:, at], pl_[:, at]), (wh[...], wl[...]), TN)

    return call(
        kernel, "project_back", 12 * length * width * channels,
        4 * (2 * length * width + channels * (length + 3 * width)),
        [d_projected, *n_both, *w_turned, *w_sum],
        [whole(channels, length)] + [whole(length, width)] * 2 + [whole(channels, width)] * (2 + len(w_sum)),
        [shaped(tokens, width)] * 4 + [shaped(channels, width)],
        [whole(tokens, width)] * 4 + [whole(channels, width)],
        scratch=[pltpu.VMEM((channels, length), BF16)] * 2, scalars=[s.reshape(1)], after=after,
    )


def turn_back(turned, placed, w_out_part, after=()):
    channels, width = turned.shape
    own = w_out_part.shape[0]
    groups = lax.axis_size("batch")
    shards = width // own
    rows = own // groups
    wide = -(-(channels + 1) // 128) * 128

    def kernel(w_ref, p_ref, o_ref, out_ref, flat_ref):
        flat_ref[:channels] = w_ref[...]
        flat_ref[channels:] = jnp.zeros((wide - channels, width), F32)
        back = flat_ref[...].T
        for j in range(groups):
            for k in range(shards):
                at = (k * groups + j) * rows
                to = slice(k * rows, (k + 1) * rows)
                out_ref[j, to, : wide - 128] = back[at : at + rows, : wide - 128]
                out_ref[j, to, wide - 128 : wide] = back[at : at + rows, wide - 128 :] + p_ref[at : at + rows]
                out_ref[j, to, wide:] = o_ref[j * rows : (j + 1) * rows, k * own : (k + 1) * own]

    shape = (groups, shards * rows, wide + own)
    (out,) = call(
        kernel, "turn_back", 0, 8 * width * wide, [turned, placed, w_out_part],
        [whole(channels, width), whole(width, 128), whole(own, width)], [shaped(*shape)], [whole(*shape)],
        scratch=[pltpu.VMEM((wide, width), F32)], after=after,
    )
    return out


def finish(which, e_terms, x, d_residual, places, s, held, after=()):
    tokens, width = e_terms[0].shape
    seqs, slots, _ = places.shape

    def kernel(s_ref, e0, e1, e2, e3, x_ref, d_ref, at_ref, *refs):
        out_ref = refs[-1]
        e = (e0[...] + e1[...]) + (e2[...] + e3[...])
        n, inverse = normed(x_ref[0])
        along = jnp.mean(e * n, axis=-1, keepdims=True)
        here = lax.broadcasted_iota(jnp.int32, (slots, tokens), 1) + s_ref[0] * tokens
        pick = jnp.where(here == at_ref[0], 1.0, 0.0).astype(BF16)
        direct = chosen_rows(pick, halves(d_ref[...]), TN)
        out_ref[0] = (e - jnp.mean(e, axis=-1, keepdims=True) - n * along) * inverse + direct

    inputs = [*e_terms, x, d_residual, places, *held]
    one = pl.BlockSpec((1, tokens, width), lambda i, *_: (which, 0, 0))
    return pl.pallas_call(
        kernel,
        name="finish",
        out_shape=shaped(seqs, tokens, width),
        grid_spec=pltpu.PrefetchScalarGridSpec(
            num_scalar_prefetch=1,
            grid=(1,),
            in_specs=[whole(tokens, width)] * 4
            + [one, pl.BlockSpec((slots, width), lambda i, *_: (which, 0))]
            + [pl.BlockSpec((1, slots, 1), lambda i, *_: (which, 0, 0))]
            + [pl.BlockSpec(memory_space=pl.ANY)] * len(held),
            out_specs=one,
        ),
        input_output_aliases={len(inputs): 0} if held else {},
        compiler_params=pltpu.CompilerParams(vmem_limit_bytes=VMEM),
        cost_estimate=pl.CostEstimate(flops=10**6, bytes_accessed=10**6, transcendentals=0),
    )(s.reshape(1), *inputs)


def lanes_summed(value):
    return lax.dot_general(
        jnp.ones((8, value.shape[1]), F32), value, (NT, ((), ())),
        precision=lax.Precision.HIGHEST, preferred_element_type=F32,
    )


def weight_grads(pieces, s, gain_one, gain_two, w_in, w_gate, w_up, own, units):
    rows, columns = pieces[0].shape
    start = columns - 2 * units
    shards = len(pieces)

    def kernel(s_ref, *refs):
        p_refs, refs = refs[:shards], refs[shards:]
        one_ref, two_ref, wi_ref, wg_ref, wu_ref, di_ref, dg_ref, du_ref, g1_ref, g2_ref, tap_ref = refs
        one, two = one_ref[...], two_ref[...]
        lane = 3 * own // 128 * 128
        tap_ref[...] = (p_refs[0][:, lane:start] + p_refs[1][:, lane:start]) + (
            p_refs[2][:, lane:start] + p_refs[3][:, lane:start]
        )
        for index in range(shards):

            @pl.when(s_ref[0] == index)
            def _(index=index):
                sum_one = jnp.zeros((8, rows), F32)
                sum_two = jnp.zeros((8, rows), F32)
                for d, p_ref in enumerate(p_refs):
                    k = index ^ d
                    for j in range(3):
                        at = slice((j * shards + k) * own, (j * shards + k + 1) * own)
                        part = p_ref[:, j * own : (j + 1) * own]
                        sum_one += lanes_summed(wi_ref[:, at] * part)
                        di_ref[:, at] = one * part
                    at = slice(k * units, (k + 1) * units)
                    for j, (w_ref, d_ref) in enumerate(((wg_ref, dg_ref), (wu_ref, du_ref))):
                        part = p_ref[:, start + j * units : start + (j + 1) * units]
                        sum_two += lanes_summed(w_ref[:, at] * part)
                        d_ref[:, at] = two * part
                g1_ref[...] = sum_one
                g2_ref[...] = sum_two

    inputs = [*pieces, gain_one[:, None], gain_two[:, None], w_in, w_gate, w_up]
    wide = start - 3 * own // 128 * 128
    outs = [w_in.shape, w_gate.shape, w_up.shape, (8, rows), (8, rows), (rows, wide)]
    return call(
        kernel, "weight_grads", 0, 0, inputs, [whole(*v.shape) for v in inputs],
        [shaped(*v) for v in outs], [whole(*v) for v in outs], scalars=[s.reshape(1)],
    )


def norm_pull(n, inverse, grad):
    along = jnp.mean(grad * n, axis=-1, keepdims=True)
    return (grad - jnp.mean(grad, axis=-1, keepdims=True) - n * along) * inverse


def together(*values):
    return lax.optimization_barrier(values)


def body(
    inputs,
    gain_one,
    w_in,
    conv_weight,
    kernel,
    w_out,
    gain_two,
    w_gate,
    w_up,
    w_down,
    mask_positions,
    mask_counts,
    grad_rows,
):
    shards = lax.axis_size("seq")
    groups = lax.axis_size("batch")
    s = lax.axis_index("seq")
    seqs, tokens, width = inputs.shape
    length = tokens * shards
    freqs = 2 * length
    own = width // shards
    rows = w_in.shape[0]
    units = w_gate.shape[1] // shards
    count = conv_weight.shape[1]
    extra = 3 * count // rows
    tables = phase_tables(freqs)

    slots = mask_positions.shape[1]
    pad = -slots % 128
    live = jnp.arange(slots, dtype=jnp.int32) < mask_counts[:, None]
    places = jnp.pad(jnp.where(live, mask_positions, -1), ((0, 0), (0, pad)), constant_values=-1)
    d_out = jnp.pad(jnp.where(live[:, :, None], grad_rows, 0.0), ((0, 0), (0, pad), (0, 0)))
    d_out = d_out.reshape(-1, width)
    places = places[:, :, None]

    w_pre = (gain_one[:, None] * w_in).reshape(rows, 3, shards, own).transpose(0, 2, 1, 3)
    w_pre = w_pre.reshape(rows, shards, 3 * own)
    carried = jnp.broadcast_to(conv_weight.reshape(rows, 1, extra), (rows, shards, extra))
    split = 3 * own + extra
    sent = columns_out(jnp.concatenate([w_pre, carried], axis=2), s)
    sent, x_now, kernel_now, places, d_out = together(sent, inputs, kernel, places, d_out)
    w_out_turned = w_out.reshape(rows, shards, own).transpose(1, 0, 2).reshape(shards * rows, own)
    w_pre = over_batch(jnp.concatenate([sent.reshape(shards * rows, split), w_out_turned], axis=1))
    w_pre = w_pre.reshape(groups, shards, rows, split + own)

    near = [swap(x_now, "seq", 1), swap(x_now, "seq", 2)]
    wide = kernel_now.reshape(2, -1, RADIX, own)
    mirror = [(i, groups - 1 - i) for i in range(groups)]
    folded = lax.ppermute(wide[:, ::-1, :4:-1], "batch", mirror)
    folded = fold_base(wide, folded)
    near, folded, w_gate_now, w_up_now = together(near, folded, w_gate, w_up)
    base = over_batch(folded)

    far = [swap(near[0][0], "seq", 2), swap(near[1][1], "seq", 1)]
    w_units = jnp.stack([gain_two[:, None] * w_gate_now, gain_two[:, None] * w_up_now], axis=1)
    w_units = w_units.reshape(rows, 2, shards, units).transpose(0, 2, 1, 3).reshape(rows, shards, 2 * units)
    *w_turned, w_out_own = turn_in(w_pre, 3 * own, split)
    taps = w_pre[..., 3 * own : split]
    far, w_units, w_turned, w_out_own, taps, w_down_now = together(
        far, columns_out(w_units, s), w_turned, w_out_own, taps, w_down
    )
    w_units = over_batch(w_units.reshape(shards * rows, 2 * units))
    w_down_own = over_batch(w_down_now).reshape(units, width)

    taps = taps.reshape(groups, shards, 3, count).transpose(2, 1, 0, 3)
    taps = lax.dynamic_index_in_dim(taps.reshape(3, 3, shards, own), s, axis=2, keepdims=False)
    taps = taps.transpose(1, 2, 0)

    def first_half(i, after=()):
        x_i, *n_i = arrange(i, (inputs, *near), far[i], s, after=after)
        return x_i, n_i, project(w_turned, n_i).reshape(3, own, length)

    x_0, n_0, p_0 = first_half(0)
    w_out_there, (gated_0, *mixed_0), x_0, n_0 = together(from_others(w_out_own), mix(p_0, taps, base, tables), x_0, n_0)
    x_1, n_1, p_1 = first_half(1, (gated_0,))
    there_0, (gated_1, *mixed_1), x_1, n_1 = together(from_others(gated_0), mix(p_1, taps, base, tables), x_1, n_1)
    n_one, projected = (n_0, n_1), (p_0, p_1)
    gating, long_conv, vals, spec = zip(mixed_0, mixed_1)
    w_out_pieces = (w_out_own, *w_out_there)

    residual_0 = add_mixer(x_0, (gated_0, *there_0), w_out_pieces, after=(gated_1,))
    w_units = split_units(w_units.reshape(groups, shards, rows, 2 * units), after=(residual_0,))
    hidden_0 = units_of(residual_0, w_units)
    w_down_own = split_down(w_down_own, after=(hidden_0[0],))
    down_0 = down_of(hidden_0, w_down_own, s)
    there_1, down_0, residual_0, w_units, w_down_own = together(
        from_others(gated_1), down_0, residual_0, w_units, w_down_own
    )

    lived = live_back(
        (residual_0,), x_1, (gated_1, *there_1), w_out_pieces, places, d_out, w_units, w_down_own, slots
    )
    live_rows, n_live, hidden, d_units, e_two = lived
    unit_part = unit_grads(n_live, d_units, hidden, d_out, shards)
    out_0 = [down_0[0], swap(down_0[1], "seq", 1), swap(down_0[2], "seq", 2)]
    live_rows, e_two, unit_part, out_0 = together(live_rows, e_two, unit_part, out_0)
    unit_sums = sum_over_batch(unit_part)

    e_two = [e_two[:slots], e_two[slots:]]
    residual_1 = add_mixer(x_1, (gated_1, *there_1), w_out_pieces, after=(unit_part,))
    e_there, residual_1 = together([swap(e, "seq", 1 + i) for i, e in enumerate(e_two)], residual_1)
    residual = (residual_0, residual_1)
    e_two = [e + there for e, there in zip(e_two, e_there)]
    down_1 = feed_forward(residual_1, w_units, w_down_own, s)
    e_there, down_1 = together([swap(e, "seq", 2 - i) for i, e in enumerate(e_two)], down_1)
    e_terms = [*e_two, *e_there]

    d_residual, w_out_part, d_gating, d_long = live_mix(live_rows, d_out, e_terms, w_out_own, gating, long_conv, places)
    *d_projected, kernel_part, taps_part = mix_back(
        places, d_gating, d_long, projected, taps, vals, spec, tables
    )
    taps_part = taps_part[:, :, :3]
    out_0 += [swap(down_0[3], "seq", 3)]
    out_1 = [down_1[0], swap(down_1[1], "seq", 1), swap(down_1[2], "seq", 2)]
    d_projected, kernel_part, taps_part, d_residual, w_out_part, out_0, out_1 = together(
        d_projected, kernel_part, taps_part, d_residual, w_out_part, out_0, out_1
    )

    e_0 = project_back(d_projected[0].reshape(3 * own, length), n_0, w_turned, (), s)
    out_1 += [swap(down_1[3], "seq", 3)]
    (*e_0, w_in_part), out_1, unit_sums, kernel_part = together(e_0, out_1, unit_sums, kernel_part)
    kernel_sum = sum_over_batch(kernel_part.reshape(groups, -1, 2 * own))

    e_1 = project_back(d_projected[1].reshape(3 * own, length), n_1, w_turned, (w_in_part,), s)
    placed = jnp.zeros((3, 3, shards, own), F32)
    taps_part = taps_part.transpose(2, 0, 1)[:, :, None]
    placed = lax.dynamic_update_slice(placed, taps_part, (0, 0, s, 0))
    placed = placed.reshape(3, shards, groups, count).transpose(1, 2, 0, 3).reshape(width, extra)
    free = 3 * own % 128
    placed = jnp.pad(placed, ((0, 0), (free, 128 - free - extra)))
    w_in_part = turn_back(e_1[4], placed, w_out_part)
    e_there = [swap(e_0[1], "seq", 1), swap(e_0[2], "seq", 2)]
    outputs = [
        added(out) + lax.dynamic_slice_in_dim(residual[i], s * tokens, tokens, axis=0)
        for i, out in enumerate((out_0, out_1))
    ]
    e_there, e_1, w_in_part = together(e_there, e_1[:4], w_in_part)
    w_in_sum = sum_over_batch(w_in_part)

    e_0 = [e_0[0], *e_there, swap(e_0[3], "seq", 3)]
    input_grad = finish(0, e_0, inputs, d_residual, places, s, ())
    outputs = jnp.stack(
        [
            added(out) + lax.dynamic_slice_in_dim(residual[i], s * tokens, tokens, axis=0)
            for i, out in enumerate((out_0, out_1))
        ]
    )
    kernel_sum = kernel_sum.reshape(FOLDED, -1, 2, own).transpose(2, 1, 0, 3)
    mirrored = lax.ppermute(kernel_sum[:, ::-1, 3:0:-1], "batch", mirror)
    e_1, w_in_sum, mirrored, outputs, input_grad = together(to_others(e_1), w_in_sum, mirrored, outputs, input_grad)

    w_back = jnp.concatenate([w_in_sum[:, :-own], unit_sums[:, : 2 * units]], axis=1)
    w_back = columns_there(w_back.reshape(shards, rows, -1), s)
    mirrored = jnp.stack([mirrored[0], -mirrored[1]])
    kernel_grad = jnp.concatenate([kernel_sum, mirrored], axis=2).reshape(kernel.shape)
    input_grad = finish(1, e_1, inputs, d_residual, places, s, (input_grad,))
    w_out_sum = w_in_sum[:, -own:].reshape(shards, rows, own).transpose(1, 0, 2).reshape(w_out.shape)
    w_down_sum = unit_sums[:, 2 * units :].reshape(w_down.shape)
    w_back, kernel_grad, input_grad, w_out_sum, w_down_sum = together(
        w_back, kernel_grad, input_grad, w_out_sum, w_down_sum
    )
    w_in_sum, w_gate_sum, w_up_sum, gain_one_sum, gain_two_sum, taps_sum = weight_grads(
        w_back, s, gain_one, gain_two, w_in, w_gate, w_up, own, units
    )
    taps_sum = taps_sum[:, free : free + extra].reshape(conv_weight.shape)

    return (
        outputs,
        input_grad,
        gain_one_sum[0],
        w_in_sum,
        taps_sum,
        kernel_grad,
        w_out_sum,
        gain_two_sum[0],
        w_gate_sum,
        w_up_sum,
        w_down_sum,
    )


def solution(mesh):
    split = ("seq", "batch")
    placed = (
        P("batch", "seq", None),
        P(split),
        P(split, None),
        P(None, split),
        P(None, "batch", "seq"),
        P(split, None),
        P(split),
        P(split, None),
        P(split, None),
        P(split, None),
        P("batch", None),
        P("batch"),
        P("batch", None, None),
    )
    return jax.shard_map(
        body,
        mesh=mesh,
        in_specs=placed,
        out_specs=(
            P("batch", "seq", None),
            P("batch", "seq", None),
            P(split),
            P(split, None),
            P(None, split),
            P(None, "batch", "seq"),
            P(split, None),
            P(split),
            P(split, None),
            P(split, None),
            P(split, None),
        ),
        check_vma=False,
    )
```

```python
import math

import jax
import jax.numpy as jnp
import numpy as np
from jax import lax
from jax.experimental import pallas as pl
from jax.experimental.pallas import tpu as pltpu
from jax.sharding import PartitionSpec as P

EPS = 1e-05
HIGH = lax.Precision.HIGH
RADIX = 8
FOLDED = 5
ROOT = math.sqrt(0.5)
VMEM = 56 * 1024 * 1024
COST = 20
NN = ((1,), (0,))
NT = ((1,), (1,))
TN = ((0,), (0,))
F32 = jnp.float32
BF16 = jnp.bfloat16


def contract(pattern, left_side, right_side):
    return jnp.einsum(pattern, left_side, right_side, precision=HIGH)


def swap(value, axis, distance):
    devices = lax.axis_size(axis)
    return lax.ppermute(value, axis, [(i, i ^ distance) for i in range(devices)])


def from_others(value):
    return [swap(value, "seq", d) for d in (1, 2, 3)]


def to_others(blocks):
    return [blocks[0]] + [swap(blocks[d], "seq", d) for d in (1, 2, 3)]


def to_all(value):
    return [value] + from_others(value)


def added(terms):
    return (terms[0] + terms[1]) + (terms[2] + terms[3])


def by_xor(pieces, index):
    count = len(pieces)
    out = []
    for k in range(count):
        chosen = pieces[k]
        for i in range(1, count):
            chosen = jnp.where(index == i, pieces[k ^ i], chosen)
        out.append(chosen)
    return out


def columns_out(shard, s):
    pieces = []
    for d in range(4):
        block = lax.dynamic_index_in_dim(shard, s ^ d, axis=1, keepdims=False)
        pieces.append(block if d == 0 else swap(block, "seq", d))
    return jnp.stack(by_xor(pieces, s))


def columns_there(own, s):
    pieces = []
    for d in range(4):
        block = lax.dynamic_index_in_dim(own, s ^ d, axis=0, keepdims=False)
        pieces.append(block if d == 0 else swap(block, "seq", d))
    return pieces


def over_batch(value):
    full = lax.all_gather(value, "batch", axis=0, tiled=True)
    return full.reshape((-1,) + value.shape)


def sum_over_batch(parts):
    flat = parts.reshape(-1, parts.shape[2])
    return lax.psum_scatter(flat, "batch", scatter_dimension=0, tiled=True)


def halves(value):
    high = value.astype(BF16)
    return high, (value - high.astype(F32)).astype(BF16)


def dot(left_side, right_side, dims):
    (a, b), (c, d) = left_side, right_side

    def product(x, y):
        return lax.dot_general(x, y, (dims, ((), ())), preferred_element_type=F32)

    return product(a, c) + (product(a, d) + product(b, c))


def chosen_rows(chosen, both, dims):
    high, low = both

    def product(x):
        return lax.dot_general(chosen, x, (dims, ((), ())), preferred_element_type=F32)

    return product(high) + product(low)


def normed(x):
    centered = x - jnp.mean(x, axis=-1, keepdims=True)
    inverse = lax.rsqrt(jnp.mean(centered * centered, axis=-1, keepdims=True) + EPS)
    return centered * inverse, inverse


def call(kernel, name, flops, moved, inputs, in_specs, outs, out_specs, grid=(1,), scratch=(), scalars=(), after=()):
    taken = len(scalars) + len(inputs)

    def run(*refs):
        kernel(*refs[:taken], *refs[taken + len(after) :])

    return pl.pallas_call(
        run,
        name=name,
        out_shape=tuple(outs),
        grid_spec=pltpu.PrefetchScalarGridSpec(
            num_scalar_prefetch=len(scalars),
            grid=grid,
            in_specs=list(in_specs) + [pl.BlockSpec(memory_space=pl.ANY)] * len(after),
            out_specs=tuple(out_specs),
            scratch_shapes=list(scratch),
        ),
        compiler_params=pltpu.CompilerParams(vmem_limit_bytes=VMEM),
        cost_estimate=pl.CostEstimate(flops=int(flops) // COST, bytes_accessed=int(moved) // COST, transcendentals=0),
    )(*scalars, *inputs, *after)


def shaped(*shape, dtype=F32):
    return jax.ShapeDtypeStruct(shape, dtype)


def whole(*shape):
    return pl.BlockSpec(shape, lambda *_: (0,) * len(shape))


def first(work):
    pl.when(pl.program_id(0) == 0)(work)


def fold_base(kernel, mirrored, after=()):
    _, turns, kept, own = mirrored.shape

    def run(k_ref, m_ref, out_ref):
        for phase in range(FOLDED):
            for part in range(2):
                value = k_ref[part, :, phase]
                if 0 < phase <= kept:
                    other = m_ref[part, :, phase - 1]
                    value = value + other if part == 0 else value - other
                out_ref[phase * turns : (phase + 1) * turns, part * own : (part + 1) * own] = value

    shape = (FOLDED * turns, 2 * own)
    (out,) = call(
        run, "fold_base", 0, 12 * shape[0] * shape[1], [kernel, mirrored],
        [whole(*kernel.shape), whole(*mirrored.shape)], [shaped(*shape)], [whole(*shape)], after=after,
    )
    return out


def turn_in(gathered, channels, split, after=()):
    groups, shards, rows, columns = gathered.shape
    width = groups * shards * rows
    own = columns - split
    wide = -(-channels // 128) * 128

    def kernel(w_ref, high_ref, low_ref, out_ref, flat_ref):
        flat_ref[:, channels // 128 * 128 :] = jnp.zeros((width, wide - channels // 128 * 128), F32)
        for k in range(shards):
            for j in range(groups):
                at = (k * groups + j) * rows
                flat_ref[at : at + rows, :channels] = w_ref[j, k, :, :channels]
                out_ref[j * rows : (j + 1) * rows, k * own : (k + 1) * own] = w_ref[j, k, :, split:]
        turned = flat_ref[...].T
        high_ref[...], low_ref[...] = halves(turned[:channels])

    return call(
        kernel, "turn_in", 0, 4 * 2 * width * wide, [gathered], [whole(*gathered.shape)],
        [shaped(channels, width, dtype=BF16)] * 2 + [shaped(groups * rows, width)],
        [whole(channels, width)] * 2 + [whole(groups * rows, width)],
        scratch=[pltpu.VMEM((width, wide), F32)], after=after,
    )


def split_units(gathered, after=()):
    groups, shards, rows, columns = gathered.shape
    width = groups * shards * rows

    def kernel(w_ref, high_ref, low_ref, flat_ref):
        for j in range(groups):
            flat_ref[j * rows : (j + 1) * rows] = w_ref[j, 0]
        high_ref[...], low_ref[...] = halves(flat_ref[...])

    part = pl.BlockSpec((groups * rows, columns), lambda i: (i, 0))
    return call(
        kernel, "split_units", 0, 8 * width * columns, [gathered],
        [pl.BlockSpec((groups, 1, rows, columns), lambda i: (0, i, 0, 0))],
        [shaped(width, columns, dtype=BF16)] * 2, [part, part], grid=(shards,),
        scratch=[pltpu.VMEM((groups * rows, columns), F32)], after=after,
    )


def split_down(weight, after=()):
    units, width = weight.shape

    def kernel(w_ref, high_ref, low_ref):
        high_ref[...], low_ref[...] = halves(w_ref[...])

    part = pl.BlockSpec((units // 2, width), lambda i: (i, 0))
    return call(
        kernel, "split_down", 0, 8 * units * width, [weight], [part],
        [shaped(units, width, dtype=BF16)] * 2, [part, part], grid=(2,), after=after,
    )


def arrange(which, near, far, s, after=()):
    _, tokens, width = near[0].shape
    length = 4 * tokens

    def kernel(s_ref, p0, p1, p2, p3, x_ref, high_ref, low_ref):
        for d, piece in enumerate((p0, p1, p2, p3)):

            @pl.when(pl.program_id(0) == d)
            def _(d=d, piece=piece):
                x = piece[...] if d == 3 else piece[0]
                x_ref[...] = x
                high_ref[...], low_ref[...] = halves(normed(x)[0])

    rows = pl.BlockSpec((tokens, width), lambda i, s_ref: (s_ref[0] ^ i, 0))
    return call(
        kernel, "arrange", 0, 12 * length * width, [*near, far],
        [pl.BlockSpec((1, tokens, width), lambda i, s_ref: (which, 0, 0))] * 3 + [whole(tokens, width)],
        [shaped(length, width), shaped(length, width, dtype=BF16), shaped(length, width, dtype=BF16)],
        [rows] * 3, grid=(4,), scalars=[s.reshape(1)], after=after,
    )


def project(w_turned, n_both, after=()):
    channels, width = w_turned[0].shape
    length = n_both[0].shape[0]
    tokens = length // 2

    def kernel(wh, wl, nh, nl, out_ref):
        out_ref[...] = dot((wh[...], wl[...]), (nh[...], nl[...]), NT)

    rows = pl.BlockSpec((tokens, width), lambda i: (i, 0))
    (out,) = call(
        kernel, "project", 6 * length * width * channels, 4 * (length * width + channels * (length + width)),
        [*w_turned, *n_both], [whole(channels, width)] * 2 + [rows] * 2,
        [shaped(channels, length)], [pl.BlockSpec((channels, tokens), lambda i: (0, i))], grid=(2,), after=after,
    )
    return out


def phase_tables(length):
    block = length // RADIX
    place = np.arange(block)[:, None]
    turn = np.arange(block)[None, :]
    tables = []
    for phase in range(FOLDED):
        angle = 2.0 * np.pi * ((RADIX * turn + phase) * place % length) / length
        cos, sin = np.cos(angle), np.sin(angle)
        tables.append(np.block([[cos, -sin], [sin, cos]]))
    table = np.stack(tables).astype(np.float32)
    high = table.astype(BF16)
    low = (table - high.astype(np.float32)).astype(BF16)
    return jnp.asarray(high), jnp.asarray(low)


def shift(value, step):
    length = value.shape[1]
    lane = lax.broadcasted_iota(jnp.int32, value.shape, 1)
    if step < 0:
        return jnp.where(lane == 0, 0.0, pltpu.roll(value, 1, 1))
    return jnp.where(lane == length - 1, 0.0, pltpu.roll(value, length - 1, 1))


def fold(value, phase, block):
    x0, x1, x2, x3 = [value[:, i * block : (i + 1) * block] for i in range(4)]
    if phase == 0:
        return (x0 + x2) + (x1 + x3)
    if phase == 4:
        return (x0 + x2) - (x1 + x3)
    if phase == 2:
        return jnp.concatenate([x0 - x2, x3 - x1], axis=1)
    slant, lean = (x1 - x3) * ROOT, (x1 + x3) * ROOT
    if phase == 1:
        return jnp.concatenate([x0 + slant, -x2 - lean], axis=1)
    return jnp.concatenate([x0 - slant, x2 - lean], axis=1)


def unfold(total_ref, value, phase, block):
    if phase == 0:
        terms = (value,) * 4
    elif phase == 4:
        terms = (value, -value, value, -value)
    else:
        real, imag = value[:, :block], value[:, block:]
        if phase == 2:
            terms = (real, -imag, -real, imag)
        elif phase == 1:
            terms = (real, ROOT * (real - imag), -imag, -ROOT * (real + imag))
        else:
            terms = (real, -ROOT * (real + imag), imag, ROOT * (real - imag))
    for i, term in enumerate(terms):
        cols = slice(i * block, (i + 1) * block)
        total_ref[:, cols] = term if phase == 0 else total_ref[:, cols] + term


def times(left_side, right_side, block, conj=False):
    a, b = left_side[:, :block], left_side[:, block:]
    c, d = right_side[:, :block], right_side[:, block:]
    if conj:
        d = -d
    return jnp.concatenate([a * c - b * d, a * d + b * c], axis=1)


def pair(phase):
    return 1.0 if phase in (0, 4) else 2.0


def depth(phase, block):
    return block if phase in (0, 4) else 2 * block


def mix(projected, taps, base, tables, after=()):
    own, length = projected.shape[1:]
    block = 2 * length // RADIX
    groups = base.shape[0]
    turns = block // groups
    if turns % 8:
        base = base.reshape(groups, FOLDED, turns, 2 * own)
        spectrum = pl.BlockSpec((groups, 1, turns, 2 * own), lambda i: (0, i, 0, 0))
    else:
        spectrum = pl.BlockSpec((groups, turns, 2 * own), lambda i: (0, i, 0))
    scale = 1.0 / math.sqrt(length)

    def kernel(p_ref, tap_ref, base_ref, th_ref, tl_ref, gated_ref, gating_ref, long_ref, vals_ref, spec_ref,
               mixed_ref, acc_ref, base_t):
        step = pl.program_id(0)

        @pl.when(step == 0)
        def _():
            for k in range(3):

                p = p_ref[k]
                tap = tap_ref[k]
                mixed = tap[:, 0:1] * shift(p, -1) + tap[:, 1:2] * p + tap[:, 2:3] * shift(p, 1)
                if k == 1:
                    gating_ref[...] = mixed
                else:
                    mixed_ref[k // 2 * own : (k // 2 + 1) * own] = mixed

        turned = base_ref[...].reshape(block, 2 * own).T
        base_t[:, :block] = turned[:own]
        base_t[:, block:] = turned[own:]

        for phase in range(FOLDED):

            @pl.when(step == phase)
            def _(phase=phase):
                deep = depth(phase, block)
                table = (th_ref[0, :deep], tl_ref[0, :deep])
                hats = dot(halves(fold(mixed_ref[...], phase, block)), table, NN)
                spec = base_t[...] + (pair(phase) * scale) * hats[:own]
                vals = hats[own:]
                spec_ref[0] = spec
                vals_ref[0] = vals
                unfold(acc_ref, dot(halves(times(spec, vals, block)), table, NT), phase, block)

        @pl.when(step == FOLDED - 1)
        def _():
            long_conv = acc_ref[...] * (0.5 / length)
            long_ref[...] = long_conv
            gated_ref[...] = gating_ref[...] * long_conv

    flat, hat = shaped(own, length), shaped(FOLDED, own, 2 * block)
    by_phase = lambda *shape: pl.BlockSpec((1,) + shape, lambda i, *_: (i,) + (0,) * len(shape))
    return call(
        kernel, "mix", 3 * 6 * own * 4 * length * length, 4 * own * length * 22,
        [projected, taps, base, *tables],
        [whole(3, own, length), whole(3, own, 3)]
        + [spectrum]
        + [by_phase(2 * block, 2 * block), by_phase(2 * block, 2 * block)],
        [flat, flat, flat, hat, hat],
        [whole(own, length)] * 3 + [by_phase(own, 2 * block)] * 2,
        grid=(FOLDED,),
        scratch=[
            pltpu.VMEM((2 * own, length), F32),
            pltpu.VMEM((own, length), F32),
            pltpu.VMEM((own, 2 * block), F32),
        ],
        after=after,
    )


def mix_back(places, d_gating, d_long, projected, taps, vals, spec, tables, after=()):
    seqs = len(projected)
    own, length = projected[0].shape[1:]
    block = vals[0].shape[2] // 2
    groups = lax.axis_size("batch")
    turns = block // groups
    slots = places.shape[1]
    scale = 1.0 / math.sqrt(length)

    def kernel(at_ref, dg_ref, dl_ref, tap_ref, *refs):
        p_refs, vals_refs, spec_refs, refs = refs[:seqs], refs[seqs : 2 * seqs], refs[2 * seqs : 3 * seqs], refs[3 * seqs :]
        th_ref, tl_ref, *refs = refs
        out_refs, (ker_ref, dtap_ref, long_ref, gating_ref, acc_ref) = refs[:seqs], refs[seqs:]
        step = pl.program_id(0)

        @pl.when(step == 0)
        def _():
            at = lax.broadcasted_iota(jnp.int32, (slots, length), 1)
            for i in range(seqs):
                pick = jnp.where(at == at_ref[i], 1.0, 0.0).astype(BF16)
                for source, target in ((dg_ref, gating_ref), (dl_ref, long_ref)):
                    high, low = halves(source[i])
                    target[i * own : (i + 1) * own] = lax.dot_general(
                        high, pick, (NN, ((), ())), preferred_element_type=F32
                    ) + lax.dot_general(low, pick, (NN, ((), ())), preferred_element_type=F32)

        for phase in range(FOLDED):

            @pl.when(step == phase)
            def _(phase=phase):
                deep = depth(phase, block)
                table = (th_ref[0, :deep], tl_ref[0, :deep])
                hats = dot(halves(fold(long_ref[...], phase, block)), table, NN) * (0.5 / length)
                both, kernel_sum = [], 0.0
                for i in range(seqs):
                    hat = hats[i * own : (i + 1) * own]
                    ker = times(hat, vals_refs[i][0], block, conj=True)
                    kernel_sum = kernel_sum + ker
                    both += [ker * (pair(phase) * scale), times(hat, spec_refs[i][0], block, conj=True)]
                turned = jnp.concatenate([kernel_sum[:, :block], kernel_sum[:, block:]], axis=0).T
                ker_ref[:, 0] = turned.reshape(groups, turns, 2 * own)
                unfold(acc_ref, dot(halves(jnp.concatenate(both, axis=0)), table, NT), phase, block)

        @pl.when(step == FOLDED - 1)
        def _():
            lane = lax.broadcasted_iota(jnp.int32, (own, 128), 1)
            for k in range(3):
                tap = tap_ref[k]
                sums = jnp.zeros((own, 128), F32)
                for i in range(seqs):
                    if k == 1:
                        grad = gating_ref[i * own : (i + 1) * own]
                    else:
                        at = 2 * i + k // 2
                        grad = acc_ref[at * own : (at + 1) * own]
                    p = p_refs[i][k]
                    out_refs[i][k] = tap[:, 0:1] * shift(grad, 1) + tap[:, 1:2] * grad + tap[:, 2:3] * shift(grad, -1)
                    for j, moved in enumerate((shift(p, -1), p, shift(p, 1))):
                        sums += jnp.where(lane == j, jnp.sum(moved * grad, axis=1, keepdims=True), 0.0)
                dtap_ref[k] = sums

    by_phase = lambda *shape: pl.BlockSpec((1,) + shape, lambda i: (i,) + (0,) * len(shape))
    flat = shaped(3, own, length)
    return call(
        kernel, "mix_back", seqs * 3 * 6 * own * 4 * length * length, seqs * 4 * own * length * 22,
        [places, d_gating, d_long, taps, *projected, *vals, *spec, *tables],
        [whole(seqs, slots, 1), whole(seqs, own, slots), whole(seqs, own, slots), whole(3, own, 3)]
        + [whole(3, own, length)] * seqs + [by_phase(own, 2 * block)] * (2 * seqs) + [by_phase(2 * block, 2 * block)] * 2,
        [flat] * seqs + [shaped(groups, FOLDED, turns, 2 * own), shaped(3, own, 128)],
        [whole(3, own, length)] * seqs
        + [pl.BlockSpec((groups, 1, turns, 2 * own), lambda i: (0, i, 0, 0)), whole(3, own, 128)],
        grid=(FOLDED,),
        scratch=[
            pltpu.VMEM((seqs * own, length), F32),
            pltpu.VMEM((seqs * own, length), F32),
            pltpu.VMEM((2 * seqs * own, length), F32),
        ],
        after=after,
    )


def add_mixer(x, gated, w_out, after=()):
    length, width = x.shape
    own = gated[0].shape[0]
    tokens = length // 2

    def kernel(x_ref, g0, g1, g2, g3, w0, w1, w2, w3, out_ref, wh, wl, gh, gl):
        @first
        def _():
            for d, ref in enumerate((w0, w1, w2, w3)):
                wh[d * own : (d + 1) * own], wl[d * own : (d + 1) * own] = halves(ref[...])

        for d, ref in enumerate((g0, g1, g2, g3)):
            gh[d * own : (d + 1) * own], gl[d * own : (d + 1) * own] = halves(ref[...])
        out_ref[...] = x_ref[...] + dot((gh[...], gl[...]), (wh[...], wl[...]), TN)

    rows = pl.BlockSpec((tokens, width), lambda i: (i, 0))
    (out,) = call(
        kernel, "add_mixer", 6 * length * width * width, 4 * (3 * length * width + width * width),
        [x, *gated, *w_out],
        [rows] + [pl.BlockSpec((own, tokens), lambda i: (0, i))] * 4 + [whole(own, width)] * 4,
        [shaped(length, width)], [rows], grid=(2,),
        scratch=[pltpu.VMEM((width, width), BF16)] * 2 + [pltpu.VMEM((width, tokens), BF16)] * 2,
        after=after,
    )
    return out


def gelu_parts(u):
    inner = math.sqrt(2.0 / math.pi) * (u + 0.044715 * (u * u * u))
    return 0.5 * (1.0 + jnp.tanh(inner))


def units_of(residual, w_units, after=()):
    length, width = residual.shape
    units = w_units[0].shape[1] // 2
    tokens = length // 4

    def kernel(r_ref, wh, wl, high_ref, low_ref):
        gate_up = []
        for i in range(2):
            rows = r_ref[i * tokens : (i + 1) * tokens]
            gate_up.append(dot(halves(normed(rows)[0]), (wh[...], wl[...]), NN))
        for i, v in enumerate(gate_up):
            at = slice(i * tokens, (i + 1) * tokens)
            high_ref[at], low_ref[at] = halves(v[:, :units] * gelu_parts(v[:, :units]) * v[:, units:])

    rows = lambda columns: pl.BlockSpec((2 * tokens, columns), lambda i: (i, 0))
    return call(
        kernel, "units_of", 12 * length * width * units, 4 * (2 * length * width + 2 * width * units),
        [residual, *w_units], [rows(width)] + [whole(width, 2 * units)] * 2,
        [shaped(length, units, dtype=BF16)] * 2, [rows(units)] * 2, grid=(2,), after=after,
    )


def down_of(hidden, w_down, s, after=()):
    length, units = hidden[0].shape
    width = w_down[0].shape[1]
    tokens = length // 4

    def kernel(s_ref, hh, hl, dh, dl, *out_refs):
        for i, out_ref in enumerate(out_refs):
            rows = pl.ds(pl.multiple_of((s_ref[0] ^ i) * tokens, tokens), tokens)
            out_ref[...] = dot((hh[rows], hl[rows]), (dh[...], dl[...]), NN)

    return call(
        kernel, "down_of", 6 * length * width * units, 4 * (2 * length * width + width * units),
        [*hidden, *w_down], [whole(length, units)] * 2 + [whole(units, width)] * 2,
        [shaped(tokens, width)] * 4, [whole(tokens, width)] * 4, scalars=[s.reshape(1)], after=after,
    )


def feed_forward(residual, w_units, w_down, s, after=()):
    length, width = residual.shape
    units = w_down[0].shape[0]
    tokens = length // 4

    def kernel(s_ref, r_ref, wh, wl, dh, dl, *out_refs):
        gate_up = []
        for i in range(4):
            rows = r_ref[pl.ds(pl.multiple_of((s_ref[0] ^ i) * tokens, tokens), tokens)]
            gate_up.append(dot(halves(normed(rows)[0]), (wh[...], wl[...]), NN))
        hidden = [halves(v[:, :units] * gelu_parts(v[:, :units]) * v[:, units:]) for v in gate_up]
        for both, out_ref in zip(hidden, out_refs):
            out_ref[...] = dot(both, (dh[...], dl[...]), NN)

    return call(
        kernel, "feed_forward", 18 * length * width * units, 4 * (2 * length * width + 3 * width * units),
        [residual, *w_units, *w_down],
        [whole(length, width)] + [whole(width, 2 * units)] * 2 + [whole(units, width)] * 2,
        [shaped(tokens, width)] * 4, [whole(tokens, width)] * 4,
        scalars=[s.reshape(1)], after=after,
    )


def chosen(at_ref, slots, length):
    lane = lax.broadcasted_iota(jnp.int32, (slots, length), 1)
    return jnp.where(lane == at_ref[...], 1.0, 0.0).astype(BF16)


def live_back(residual, x, gated, w_out, places, d_out, w_units, w_down, used, after=()):
    seqs = 1 + len(residual)
    length, width = x.shape
    own = gated[0].shape[0]
    slots = places.shape[1]
    units = w_down[0].shape[0]
    rows = seqs * slots

    def kernel(*refs):
        r_refs, refs = refs[: seqs - 1], refs[seqs - 1 :]
        x_ref, g_refs, w_refs, refs = refs[0], refs[1:5], refs[5:9], refs[9:]
        at_ref, o_ref, wh, wl, dh, dl, live_ref, n_ref, hid_ref, du_ref, e_ref = refs
        for i, ref in enumerate((*r_refs, x_ref)):
            pick = chosen(at_ref.at[i], slots, length)
            live_ref[i * slots : (i + 1) * slots] = chosen_rows(pick, halves(ref[...]), NN)
        mixed = []
        for ref in g_refs:
            parts = [lax.dot_general(v, pick, (NT, ((), ())), preferred_element_type=F32) for v in halves(ref[...])]
            mixed.append(parts[0] + parts[1])
        weight = jnp.concatenate([ref[...] for ref in w_refs], axis=0)
        live_ref[rows - slots :] += dot(halves(jnp.concatenate(mixed, axis=0)), halves(weight), TN)
        n = normed(live_ref[...])[0]
        n_ref[...] = n
        gate_up = dot(halves(n), (wh[...], wl[...]), NN)
        d_hidden = dot(halves(o_ref[...]), (dh[...], dl[...]), NT)
        gate, up = gate_up[:, :units], gate_up[:, units:]
        half = gelu_parts(gate)
        slope = half + gate * 2.0 * half * (1.0 - half) * math.sqrt(2.0 / math.pi) * (1.0 + 0.134145 * (gate * gate))
        hid_ref[...] = gate * half * up
        d_units = jnp.concatenate([d_hidden * up * slope, d_hidden * (gate * half)], axis=1)
        du_ref[...] = d_units
        e = dot(halves(d_units), (wh[...], wl[...]), NT)
        for i in range(seqs):
            e_ref[i * used : (i + 1) * used] = e[i * slots : i * slots + used]

    return call(
        kernel, "live_back", 30 * rows * width * units, 4 * (2 * length * width + 4 * width * units),
        [*residual, x, *gated, *w_out, places, d_out, *w_units, *w_down],
        [whole(length, width)] * seqs + [whole(own, length)] * 4 + [whole(own, width)] * 4
        + [whole(seqs, slots, 1), whole(rows, width)] + [whole(width, 2 * units)] * 2 + [whole(units, width)] * 2,
        [shaped(rows, width), shaped(rows, width), shaped(rows, units), shaped(rows, 2 * units), shaped(seqs * used, width)],
        [whole(rows, width), whole(rows, width), whole(rows, units), whole(rows, 2 * units), whole(seqs * used, width)],
        after=after,
    )


def unit_grads(normed_live, d_units, hidden, d_out, shards, after=()):
    slots, width = normed_live.shape
    units = hidden.shape[1]
    groups = lax.axis_size("batch")
    rows = width // groups // shards
    down = units // groups

    def kernel(n_ref, u_ref, h_ref, o_ref, out_ref):
        @pl.when(pl.program_id(0) < 2)
        def _():
            part = dot(halves(n_ref[...]), halves(u_ref[...]), TN)
            for j in range(groups):
                for k in range(shards):
                    at = (k * groups + j) * rows
                    out_ref[j, k * rows : (k + 1) * rows] = part[at : at + rows]

        @pl.when(pl.program_id(0) == 2)
        def _():
            part = dot(halves(h_ref[...]), halves(o_ref[...]), TN)
            for j in range(groups):
                out_ref[j] = part[j * down : (j + 1) * down]

    (out,) = call(
        kernel, "unit_grads", 18 * slots * width * units, 4 * 3 * width * units,
        [normed_live, d_units, hidden, d_out],
        [
            whole(slots, width),
            pl.BlockSpec((slots, units), lambda i: (0, jnp.minimum(i, 1))),
            whole(slots, units),
            whole(slots, width),
        ],
        [shaped(groups, shards * rows, 2 * units + width)],
        [pl.BlockSpec((groups, shards * rows, width), lambda i: (0, 0, i))],
        grid=(3,), after=after,
    )
    return out


def live_mix(live, d_out, e_terms, w_out, gating, long_conv, places, after=()):
    seqs = len(gating)
    own, length = gating[0].shape
    rows, width = live.shape
    slots = rows // seqs
    used = e_terms[0].shape[0]

    def kernel(live_ref, o_ref, *refs):
        e_refs, w_ref, refs = refs[: 2 * seqs], refs[2 * seqs], refs[2 * seqs + 1 :]
        g_refs, l_refs, refs = refs[:seqs], refs[seqs : 2 * seqs], refs[2 * seqs :]
        at_ref, res_ref, dw_ref, dg_ref, dl_ref, e_all, pick_ref = refs
        e_all[...] = jnp.zeros((rows, width), F32)
        for i in range(seqs):
            e_all[i * slots : i * slots + used] = e_refs[i][...] + e_refs[seqs + i][...]
        n, inverse = normed(live_ref[...])
        e = e_all[...]
        along = jnp.mean(e * n, axis=-1, keepdims=True)
        res_ref[...] = o_ref[...] + (e - jnp.mean(e, axis=-1, keepdims=True) - n * along) * inverse
        d_res = halves(res_ref[...])
        d_gated = dot(halves(w_ref[...]), d_res, NT)
        for i in range(seqs):
            pick = chosen(at_ref.at[i], slots, length)
            at = slice(i * slots, (i + 1) * slots)
            gate = [lax.dot_general(v, pick, (NT, ((), ())), preferred_element_type=F32) for v in halves(g_refs[i][...])]
            lng = [lax.dot_general(v, pick, (NT, ((), ())), preferred_element_type=F32) for v in halves(l_refs[i][...])]
            gate, lng = gate[0] + gate[1], lng[0] + lng[1]
            dg_ref[i] = d_gated[:, at] * lng
            dl_ref[i] = d_gated[:, at] * gate
            pick_ref[:, at] = gate * lng
        dw_ref[...] = dot(halves(pick_ref[...]), d_res, NN)

    return call(
        kernel, "live_mix", 20 * rows * width * own, 4 * (4 * own * length + 4 * rows * width),
        [live, d_out, *e_terms, w_out, *gating, *long_conv, places],
        [whole(rows, width)] * 2 + [whole(used, width)] * (2 * seqs) + [whole(own, width)]
        + [whole(own, length)] * (2 * seqs) + [whole(seqs, slots, 1)],
        [shaped(rows, width), shaped(own, width), shaped(seqs, own, slots), shaped(seqs, own, slots)],
        [whole(rows, width), whole(own, width), whole(seqs, own, slots), whole(seqs, own, slots)],
        scratch=[pltpu.VMEM((rows, width), F32), pltpu.VMEM((own, rows), F32)],
        after=after,
    )


def project_back(d_projected, n_both, w_turned, w_sum, s, after=()):
    channels, length = d_projected.shape
    width = n_both[0].shape[1]
    tokens = length // 4

    def kernel(s_ref, d_ref, nh, nl, wh, wl, *refs):
        sum_refs, e_refs, dw_ref, ph, pl_ = refs[:-7], refs[-7:-3], refs[-3], refs[-2], refs[-1]
        ph[...], pl_[...] = halves(d_ref[...])
        part = dot((ph[...], pl_[...]), (nh[...], nl[...]), NN)
        dw_ref[...] = sum_refs[0][...] + part if sum_refs else part
        for i, e_ref in enumerate(e_refs):
            at = pl.ds(pl.multiple_of((s_ref[0] ^ i) * tokens, tokens), tokens)
            e_ref[...] = dot((ph[:, at], pl_[:, at]), (wh[...], wl[...]), TN)

    return call(
        kernel, "project_back", 12 * length * width * channels,
        4 * (2 * length * width + channels * (length + 3 * width)),
        [d_projected, *n_both, *w_turned, *w_sum],
        [whole(channels, length)] + [whole(length, width)] * 2 + [whole(channels, width)] * (2 + len(w_sum)),
        [shaped(tokens, width)] * 4 + [shaped(channels, width)],
        [whole(tokens, width)] * 4 + [whole(channels, width)],
        scratch=[pltpu.VMEM((channels, length), BF16)] * 2, scalars=[s.reshape(1)], after=after,
    )


def turn_back(turned, placed, w_out_part, after=()):
    channels, width = turned.shape
    own = w_out_part.shape[0]
    groups = lax.axis_size("batch")
    shards = width // own
    rows = own // groups
    wide = -(-(channels + 1) // 128) * 128

    def kernel(w_ref, p_ref, o_ref, out_ref, flat_ref):
        flat_ref[:channels] = w_ref[...]
        flat_ref[channels:] = jnp.zeros((wide - channels, width), F32)
        back = flat_ref[...].T
        for j in range(groups):
            for k in range(shards):
                at = (k * groups + j) * rows
                to = slice(k * rows, (k + 1) * rows)
                out_ref[j, to, : wide - 128] = back[at : at + rows, : wide - 128]
                out_ref[j, to, wide - 128 : wide] = back[at : at + rows, wide - 128 :] + p_ref[at : at + rows]
                out_ref[j, to, wide:] = o_ref[j * rows : (j + 1) * rows, k * own : (k + 1) * own]

    shape = (groups, shards * rows, wide + own)
    (out,) = call(
        kernel, "turn_back", 0, 8 * width * wide, [turned, placed, w_out_part],
        [whole(channels, width), whole(width, 128), whole(own, width)], [shaped(*shape)], [whole(*shape)],
        scratch=[pltpu.VMEM((wide, width), F32)], after=after,
    )
    return out


def finish(which, e_terms, x, d_residual, places, s, held, after=()):
    tokens, width = e_terms[0].shape
    seqs, slots, _ = places.shape

    def kernel(s_ref, e0, e1, e2, e3, x_ref, d_ref, at_ref, *refs):
        out_ref = refs[-1]
        e = (e0[...] + e1[...]) + (e2[...] + e3[...])
        n, inverse = normed(x_ref[0])
        along = jnp.mean(e * n, axis=-1, keepdims=True)
        here = lax.broadcasted_iota(jnp.int32, (slots, tokens), 1) + s_ref[0] * tokens
        pick = jnp.where(here == at_ref[0], 1.0, 0.0).astype(BF16)
        direct = chosen_rows(pick, halves(d_ref[...]), TN)
        out_ref[0] = (e - jnp.mean(e, axis=-1, keepdims=True) - n * along) * inverse + direct

    inputs = [*e_terms, x, d_residual, places, *held]
    one = pl.BlockSpec((1, tokens, width), lambda i, *_: (which, 0, 0))
    return pl.pallas_call(
        kernel,
        name="finish",
        out_shape=shaped(seqs, tokens, width),
        grid_spec=pltpu.PrefetchScalarGridSpec(
            num_scalar_prefetch=1,
            grid=(1,),
            in_specs=[whole(tokens, width)] * 4
            + [one, pl.BlockSpec((slots, width), lambda i, *_: (which, 0))]
            + [pl.BlockSpec((1, slots, 1), lambda i, *_: (which, 0, 0))]
            + [pl.BlockSpec(memory_space=pl.ANY)] * len(held),
            out_specs=one,
        ),
        input_output_aliases={len(inputs): 0} if held else {},
        compiler_params=pltpu.CompilerParams(vmem_limit_bytes=VMEM),
        cost_estimate=pl.CostEstimate(flops=10**6, bytes_accessed=10**6, transcendentals=0),
    )(s.reshape(1), *inputs)


def lanes_summed(value):
    return lax.dot_general(
        jnp.ones((8, value.shape[1]), F32), value, (NT, ((), ())),
        precision=lax.Precision.HIGHEST, preferred_element_type=F32,
    )


def weight_grads(pieces, s, gain_one, gain_two, w_in, w_gate, w_up, own, units):
    rows, columns = pieces[0].shape
    start = columns - 2 * units
    shards = len(pieces)

    def kernel(s_ref, *refs):
        p_refs, refs = refs[:shards], refs[shards:]
        one_ref, two_ref, wi_ref, wg_ref, wu_ref, di_ref, dg_ref, du_ref, g1_ref, g2_ref, tap_ref = refs
        one, two = one_ref[...], two_ref[...]
        lane = 3 * own // 128 * 128
        tap_ref[...] = (p_refs[0][:, lane:start] + p_refs[1][:, lane:start]) + (
            p_refs[2][:, lane:start] + p_refs[3][:, lane:start]
        )
        for index in range(shards):

            @pl.when(s_ref[0] == index)
            def _(index=index):
                sum_one = jnp.zeros((8, rows), F32)
                sum_two = jnp.zeros((8, rows), F32)
                for d, p_ref in enumerate(p_refs):
                    k = index ^ d
                    for j in range(3):
                        at = slice((j * shards + k) * own, (j * shards + k + 1) * own)
                        part = p_ref[:, j * own : (j + 1) * own]
                        sum_one += lanes_summed(wi_ref[:, at] * part)
                        di_ref[:, at] = one * part
                    at = slice(k * units, (k + 1) * units)
                    for j, (w_ref, d_ref) in enumerate(((wg_ref, dg_ref), (wu_ref, du_ref))):
                        part = p_ref[:, start + j * units : start + (j + 1) * units]
                        sum_two += lanes_summed(w_ref[:, at] * part)
                        d_ref[:, at] = two * part
                g1_ref[...] = sum_one
                g2_ref[...] = sum_two

    inputs = [*pieces, gain_one[:, None], gain_two[:, None], w_in, w_gate, w_up]
    wide = start - 3 * own // 128 * 128
    outs = [w_in.shape, w_gate.shape, w_up.shape, (8, rows), (8, rows), (rows, wide)]
    return call(
        kernel, "weight_grads", 0, 0, inputs, [whole(*v.shape) for v in inputs],
        [shaped(*v) for v in outs], [whole(*v) for v in outs], scalars=[s.reshape(1)],
    )


def norm_pull(n, inverse, grad):
    along = jnp.mean(grad * n, axis=-1, keepdims=True)
    return (grad - jnp.mean(grad, axis=-1, keepdims=True) - n * along) * inverse


def together(*values):
    return lax.optimization_barrier(values)


def body(
    inputs,
    gain_one,
    w_in,
    conv_weight,
    kernel,
    w_out,
    gain_two,
    w_gate,
    w_up,
    w_down,
    mask_positions,
    mask_counts,
    grad_rows,
):
    shards = lax.axis_size("seq")
    groups = lax.axis_size("batch")
    s = lax.axis_index("seq")
    seqs, tokens, width = inputs.shape
    length = tokens * shards
    freqs = 2 * length
    own = width // shards
    rows = w_in.shape[0]
    units = w_gate.shape[1] // shards
    count = conv_weight.shape[1]
    extra = 3 * count // rows
    tables = phase_tables(freqs)

    slots = mask_positions.shape[1]
    pad = -slots % 128
    live = jnp.arange(slots, dtype=jnp.int32) < mask_counts[:, None]
    places = jnp.pad(jnp.where(live, mask_positions, -1), ((0, 0), (0, pad)), constant_values=-1)
    d_out = jnp.pad(jnp.where(live[:, :, None], grad_rows, 0.0), ((0, 0), (0, pad), (0, 0)))
    d_out = d_out.reshape(-1, width)
    places = places[:, :, None]

    w_pre = (gain_one[:, None] * w_in).reshape(rows, 3, shards, own).transpose(0, 2, 1, 3)
    w_pre = w_pre.reshape(rows, shards, 3 * own)
    carried = jnp.broadcast_to(conv_weight.reshape(rows, 1, extra), (rows, shards, extra))
    split = 3 * own + extra
    sent = columns_out(jnp.concatenate([w_pre, carried], axis=2), s)
    sent, x_now, kernel_now, places, d_out = together(sent, inputs, kernel, places, d_out)
    w_out_turned = w_out.reshape(rows, shards, own).transpose(1, 0, 2).reshape(shards * rows, own)
    w_pre = over_batch(jnp.concatenate([sent.reshape(shards * rows, split), w_out_turned], axis=1))
    w_pre = w_pre.reshape(groups, shards, rows, split + own)

    near = [swap(x_now, "seq", 1), swap(x_now, "seq", 2)]
    wide = kernel_now.reshape(2, -1, RADIX, own)
    mirror = [(i, groups - 1 - i) for i in range(groups)]
    folded = lax.ppermute(wide[:, ::-1, :4:-1], "batch", mirror)
    folded = fold_base(wide, folded)
    near, folded, w_gate_now, w_up_now = together(near, folded, w_gate, w_up)
    base = over_batch(folded)

    from_one, from_two, w_gate_now, w_up_now = together(near[0][0], near[1][1], w_gate_now, w_up_now)
    far = [swap(from_one, "seq", 2), swap(from_two, "seq", 1)]
    w_units = jnp.stack([gain_two[:, None] * w_gate_now, gain_two[:, None] * w_up_now], axis=1)
    w_units = w_units.reshape(rows, 2, shards, units).transpose(0, 2, 1, 3).reshape(rows, shards, 2 * units)
    *w_turned, w_out_own = turn_in(w_pre, 3 * own, split)
    taps = w_pre[..., 3 * own : split]
    far, w_units, w_turned, w_out_own, taps, w_down_now = together(
        far, columns_out(w_units, s), w_turned, w_out_own, taps, w_down
    )
    w_units = over_batch(w_units.reshape(shards * rows, 2 * units))
    w_down_own = over_batch(w_down_now).reshape(units, width)

    taps = taps.reshape(groups, shards, 3, count).transpose(2, 1, 0, 3)
    taps = lax.dynamic_index_in_dim(taps.reshape(3, 3, shards, own), s, axis=2, keepdims=False)
    taps = taps.transpose(1, 2, 0)

    def first_half(i, after=()):
        x_i, *n_i = arrange(i, (inputs, *near), far[i], s, after=after)
        return x_i, n_i, project(w_turned, n_i).reshape(3, own, length)

    x_0, n_0, p_0 = first_half(0)
    w_out_there, (gated_0, *mixed_0), x_0, n_0 = together(from_others(w_out_own), mix(p_0, taps, base, tables), x_0, n_0)
    x_1, n_1, p_1 = first_half(1, (gated_0,))
    there_0, (gated_1, *mixed_1), x_1, n_1 = together(from_others(gated_0), mix(p_1, taps, base, tables), x_1, n_1)
    n_one, projected = (n_0, n_1), (p_0, p_1)
    gating, long_conv, vals, spec = zip(mixed_0, mixed_1)
    w_out_pieces = (w_out_own, *w_out_there)

    residual_0 = add_mixer(x_0, (gated_0, *there_0), w_out_pieces, after=(gated_1,))
    w_units = split_units(w_units.reshape(groups, shards, rows, 2 * units), after=(residual_0,))
    hidden_0 = units_of(residual_0, w_units)
    w_down_own = split_down(w_down_own, after=(hidden_0[0],))
    down_0 = down_of(hidden_0, w_down_own, s)
    there_1, down_0, residual_0, w_units, w_down_own = together(
        from_others(gated_1), down_0, residual_0, w_units, w_down_own
    )

    lived = live_back(
        (residual_0,), x_1, (gated_1, *there_1), w_out_pieces, places, d_out, w_units, w_down_own, slots
    )
    live_rows, n_live, hidden, d_units, e_two = lived
    unit_part = unit_grads(n_live, d_units, hidden, d_out, shards)
    out_0 = [down_0[0], swap(down_0[1], "seq", 1), swap(down_0[2], "seq", 2)]
    live_rows, e_two, unit_part, out_0 = together(live_rows, e_two, unit_part, out_0)
    unit_sums = sum_over_batch(unit_part)

    e_two = [e_two[:slots], e_two[slots:]]
    residual_1 = add_mixer(x_1, (gated_1, *there_1), w_out_pieces, after=(unit_part,))
    e_there, residual_1 = together([swap(e, "seq", 1 + i) for i, e in enumerate(e_two)], residual_1)
    residual = (residual_0, residual_1)
    e_two = [e + there for e, there in zip(e_two, e_there)]
    down_1 = feed_forward(residual_1, w_units, w_down_own, s)
    e_there, down_1 = together([swap(e, "seq", 2 - i) for i, e in enumerate(e_two)], down_1)
    e_terms = [*e_two, *e_there]

    d_residual, w_out_part, d_gating, d_long = live_mix(live_rows, d_out, e_terms, w_out_own, gating, long_conv, places)
    *d_projected, kernel_part, taps_part = mix_back(
        places, d_gating, d_long, projected, taps, vals, spec, tables
    )
    taps_part = taps_part[:, :, :3]
    out_0 += [swap(down_0[3], "seq", 3)]
    out_1 = [down_1[0], swap(down_1[1], "seq", 1), swap(down_1[2], "seq", 2)]
    d_projected, kernel_part, taps_part, d_residual, w_out_part, out_0, out_1 = together(
        d_projected, kernel_part, taps_part, d_residual, w_out_part, out_0, out_1
    )

    e_0 = project_back(d_projected[0].reshape(3 * own, length), n_0, w_turned, (), s)
    out_1 += [swap(down_1[3], "seq", 3)]
    (*e_0, w_in_part), out_1, unit_sums, kernel_part = together(e_0, out_1, unit_sums, kernel_part)
    kernel_sum = sum_over_batch(kernel_part.reshape(groups, -1, 2 * own))

    e_1 = project_back(d_projected[1].reshape(3 * own, length), n_1, w_turned, (w_in_part,), s)
    placed = jnp.zeros((3, 3, shards, own), F32)
    taps_part = taps_part.transpose(2, 0, 1)[:, :, None]
    placed = lax.dynamic_update_slice(placed, taps_part, (0, 0, s, 0))
    placed = placed.reshape(3, shards, groups, count).transpose(1, 2, 0, 3).reshape(width, extra)
    free = 3 * own % 128
    placed = jnp.pad(placed, ((0, 0), (free, 128 - free - extra)))
    w_in_part = turn_back(e_1[4], placed, w_out_part)
    e_there = [swap(e_0[1], "seq", 1), swap(e_0[2], "seq", 2)]
    outputs = [
        added(out) + lax.dynamic_slice_in_dim(residual[i], s * tokens, tokens, axis=0)
        for i, out in enumerate((out_0, out_1))
    ]
    e_there, e_1, w_in_part = together(e_there, e_1[:4], w_in_part)
    w_in_sum = sum_over_batch(w_in_part)

    e_0 = [e_0[0], *e_there, swap(e_0[3], "seq", 3)]
    input_grad = finish(0, e_0, inputs, d_residual, places, s, ())
    outputs = jnp.stack(
        [
            added(out) + lax.dynamic_slice_in_dim(residual[i], s * tokens, tokens, axis=0)
            for i, out in enumerate((out_0, out_1))
        ]
    )
    kernel_sum = kernel_sum.reshape(FOLDED, -1, 2, own).transpose(2, 1, 0, 3)
    mirrored = lax.ppermute(kernel_sum[:, ::-1, 3:0:-1], "batch", mirror)
    e_1, w_in_sum, mirrored, outputs, input_grad = together(to_others(e_1), w_in_sum, mirrored, outputs, input_grad)

    w_back = jnp.concatenate([w_in_sum[:, :-own], unit_sums[:, : 2 * units]], axis=1)
    w_back = columns_there(w_back.reshape(shards, rows, -1), s)
    mirrored = jnp.stack([mirrored[0], -mirrored[1]])
    kernel_grad = jnp.concatenate([kernel_sum, mirrored], axis=2).reshape(kernel.shape)
    input_grad = finish(1, e_1, inputs, d_residual, places, s, (input_grad,))
    w_out_sum = w_in_sum[:, -own:].reshape(shards, rows, own).transpose(1, 0, 2).reshape(w_out.shape)
    w_down_sum = unit_sums[:, 2 * units :].reshape(w_down.shape)
    w_back, kernel_grad, input_grad, w_out_sum, w_down_sum = together(
        w_back, kernel_grad, input_grad, w_out_sum, w_down_sum
    )
    w_in_sum, w_gate_sum, w_up_sum, gain_one_sum, gain_two_sum, taps_sum = weight_grads(
        w_back, s, gain_one, gain_two, w_in, w_gate, w_up, own, units
    )
    taps_sum = taps_sum[:, free : free + extra].reshape(conv_weight.shape)

    return (
        outputs,
        input_grad,
        gain_one_sum[0],
        w_in_sum,
        taps_sum,
        kernel_grad,
        w_out_sum,
        gain_two_sum[0],
        w_gate_sum,
        w_up_sum,
        w_down_sum,
    )


def solution(mesh):
    split = ("seq", "batch")
    placed = (
        P("batch", "seq", None),
        P(split),
        P(split, None),
        P(None, split),
        P(None, "batch", "seq"),
        P(split, None),
        P(split),
        P(split, None),
        P(split, None),
        P(split, None),
        P("batch", None),
        P("batch"),
        P("batch", None, None),
    )
    return jax.shard_map(
        body,
        mesh=mesh,
        in_specs=placed,
        out_specs=(
            P("batch", "seq", None),
            P("batch", "seq", None),
            P(split),
            P(split, None),
            P(None, split),
            P(None, "batch", "seq"),
            P(split, None),
            P(split),
            P(split, None),
            P(split, None),
            P(split, None),
        ),
        check_vma=False,
    )
```

```python
import math

import jax
import jax.numpy as jnp
import numpy as np
from jax import lax
from jax.experimental import pallas as pl
from jax.experimental.pallas import tpu as pltpu
from jax.sharding import PartitionSpec as P

EPS = 1e-05
HIGH = lax.Precision.HIGH
RADIX = 8
FOLDED = 5
ROOT = math.sqrt(0.5)
VMEM = 56 * 1024 * 1024
COST = 20
NN = ((1,), (0,))
NT = ((1,), (1,))
TN = ((0,), (0,))
F32 = jnp.float32
BF16 = jnp.bfloat16


def contract(pattern, left_side, right_side):
    return jnp.einsum(pattern, left_side, right_side, precision=HIGH)


def swap(value, axis, distance):
    devices = lax.axis_size(axis)
    return lax.ppermute(value, axis, [(i, i ^ distance) for i in range(devices)])


def from_others(value):
    return [swap(value, "seq", d) for d in (1, 2, 3)]


def to_others(blocks):
    return [blocks[0]] + [swap(blocks[d], "seq", d) for d in (1, 2, 3)]


def to_all(value):
    return [value] + from_others(value)


def added(terms):
    return (terms[0] + terms[1]) + (terms[2] + terms[3])


def by_xor(pieces, index):
    count = len(pieces)
    out = []
    for k in range(count):
        chosen = pieces[k]
        for i in range(1, count):
            chosen = jnp.where(index == i, pieces[k ^ i], chosen)
        out.append(chosen)
    return out


def columns_out(shard, s):
    pieces = []
    for d in range(4):
        block = lax.dynamic_index_in_dim(shard, s ^ d, axis=1, keepdims=False)
        pieces.append(block if d == 0 else swap(block, "seq", d))
    return jnp.stack(by_xor(pieces, s))


def columns_there(own, s):
    pieces = []
    for d in range(4):
        block = lax.dynamic_index_in_dim(own, s ^ d, axis=0, keepdims=False)
        pieces.append(block if d == 0 else swap(block, "seq", d))
    return pieces


def over_batch(value):
    full = lax.all_gather(value, "batch", axis=0, tiled=True)
    return full.reshape((-1,) + value.shape)


def sum_over_batch(parts):
    flat = parts.reshape(-1, parts.shape[2])
    return lax.psum_scatter(flat, "batch", scatter_dimension=0, tiled=True)


def halves(value):
    high = value.astype(BF16)
    return high, (value - high.astype(F32)).astype(BF16)


def dot(left_side, right_side, dims):
    (a, b), (c, d) = left_side, right_side

    def product(x, y):
        return lax.dot_general(x, y, (dims, ((), ())), preferred_element_type=F32)

    return product(a, c) + (product(a, d) + product(b, c))


def chosen_rows(chosen, both, dims):
    high, low = both

    def product(x):
        return lax.dot_general(chosen, x, (dims, ((), ())), preferred_element_type=F32)

    return product(high) + product(low)


def normed(x):
    centered = x - jnp.mean(x, axis=-1, keepdims=True)
    inverse = lax.rsqrt(jnp.mean(centered * centered, axis=-1, keepdims=True) + EPS)
    return centered * inverse, inverse


def call(kernel, name, flops, moved, inputs, in_specs, outs, out_specs, grid=(1,), scratch=(), scalars=(), after=()):
    taken = len(scalars) + len(inputs)

    def run(*refs):
        kernel(*refs[:taken], *refs[taken + len(after) :])

    return pl.pallas_call(
        run,
        name=name,
        out_shape=tuple(outs),
        grid_spec=pltpu.PrefetchScalarGridSpec(
            num_scalar_prefetch=len(scalars),
            grid=grid,
            in_specs=list(in_specs) + [pl.BlockSpec(memory_space=pl.ANY)] * len(after),
            out_specs=tuple(out_specs),
            scratch_shapes=list(scratch),
        ),
        compiler_params=pltpu.CompilerParams(vmem_limit_bytes=VMEM),
        cost_estimate=pl.CostEstimate(flops=int(flops) // COST, bytes_accessed=int(moved) // COST, transcendentals=0),
    )(*scalars, *inputs, *after)


def shaped(*shape, dtype=F32):
    return jax.ShapeDtypeStruct(shape, dtype)


def whole(*shape):
    return pl.BlockSpec(shape, lambda *_: (0,) * len(shape))


def first(work):
    pl.when(pl.program_id(0) == 0)(work)


def fold_base(kernel, mirrored, after=()):
    _, turns, kept, own = mirrored.shape

    def run(k_ref, m_ref, out_ref):
        for phase in range(FOLDED):
            for part in range(2):
                value = k_ref[part, :, phase]
                if 0 < phase <= kept:
                    other = m_ref[part, :, phase - 1]
                    value = value + other if part == 0 else value - other
                out_ref[phase * turns : (phase + 1) * turns, part * own : (part + 1) * own] = value

    shape = (FOLDED * turns, 2 * own)
    (out,) = call(
        run, "fold_base", 0, 12 * shape[0] * shape[1], [kernel, mirrored],
        [whole(*kernel.shape), whole(*mirrored.shape)], [shaped(*shape)], [whole(*shape)], after=after,
    )
    return out


def turn_in(gathered, channels, split, after=()):
    groups, shards, rows, columns = gathered.shape
    width = groups * shards * rows
    own = columns - split
    wide = -(-channels // 128) * 128

    def kernel(w_ref, high_ref, low_ref, out_ref, flat_ref):
        flat_ref[:, channels // 128 * 128 :] = jnp.zeros((width, wide - channels // 128 * 128), F32)
        for k in range(shards):
            for j in range(groups):
                at = (k * groups + j) * rows
                flat_ref[at : at + rows, :channels] = w_ref[j, k, :, :channels]
                out_ref[j * rows : (j + 1) * rows, k * own : (k + 1) * own] = w_ref[j, k, :, split:]
        turned = flat_ref[...].T
        high_ref[...], low_ref[...] = halves(turned[:channels])

    return call(
        kernel, "turn_in", 0, 4 * 2 * width * wide, [gathered], [whole(*gathered.shape)],
        [shaped(channels, width, dtype=BF16)] * 2 + [shaped(groups * rows, width)],
        [whole(channels, width)] * 2 + [whole(groups * rows, width)],
        scratch=[pltpu.VMEM((width, wide), F32)], after=after,
    )


def split_units(gathered, after=()):
    groups, shards, rows, columns = gathered.shape
    width = groups * shards * rows

    def kernel(w_ref, high_ref, low_ref, flat_ref):
        for j in range(groups):
            flat_ref[j * rows : (j + 1) * rows] = w_ref[j, 0]
        high_ref[...], low_ref[...] = halves(flat_ref[...])

    part = pl.BlockSpec((groups * rows, columns), lambda i: (i, 0))
    return call(
        kernel, "split_units", 0, 8 * width * columns, [gathered],
        [pl.BlockSpec((groups, 1, rows, columns), lambda i: (0, i, 0, 0))],
        [shaped(width, columns, dtype=BF16)] * 2, [part, part], grid=(shards,),
        scratch=[pltpu.VMEM((groups * rows, columns), F32)], after=after,
    )


def split_down(weight, after=()):
    units, width = weight.shape

    def kernel(w_ref, high_ref, low_ref):
        high_ref[...], low_ref[...] = halves(w_ref[...])

    part = pl.BlockSpec((units // 2, width), lambda i: (i, 0))
    return call(
        kernel, "split_down", 0, 8 * units * width, [weight], [part],
        [shaped(units, width, dtype=BF16)] * 2, [part, part], grid=(2,), after=after,
    )


def arrange(which, near, far, s, after=()):
    _, tokens, width = near[0].shape
    length = 4 * tokens

    def kernel(s_ref, p0, p1, p2, p3, x_ref, high_ref, low_ref):
        for d, piece in enumerate((p0, p1, p2, p3)):

            @pl.when(pl.program_id(0) == d)
            def _(d=d, piece=piece):
                x = piece[...] if d == 3 else piece[0]
                x_ref[...] = x
                high_ref[...], low_ref[...] = halves(normed(x)[0])

    rows = pl.BlockSpec((tokens, width), lambda i, s_ref: (s_ref[0] ^ i, 0))
    return call(
        kernel, "arrange", 0, 12 * length * width, [*near, far],
        [pl.BlockSpec((1, tokens, width), lambda i, s_ref: (which, 0, 0))] * 3 + [whole(tokens, width)],
        [shaped(length, width), shaped(length, width, dtype=BF16), shaped(length, width, dtype=BF16)],
        [rows] * 3, grid=(4,), scalars=[s.reshape(1)], after=after,
    )


def project(w_turned, n_both, after=()):
    channels, width = w_turned[0].shape
    length = n_both[0].shape[0]
    tokens = length // 2

    def kernel(wh, wl, nh, nl, out_ref):
        out_ref[...] = dot((wh[...], wl[...]), (nh[...], nl[...]), NT)

    rows = pl.BlockSpec((tokens, width), lambda i: (i, 0))
    (out,) = call(
        kernel, "project", 6 * length * width * channels, 4 * (length * width + channels * (length + width)),
        [*w_turned, *n_both], [whole(channels, width)] * 2 + [rows] * 2,
        [shaped(channels, length)], [pl.BlockSpec((channels, tokens), lambda i: (0, i))], grid=(2,), after=after,
    )
    return out


def phase_tables(length):
    block = length // RADIX
    place = np.arange(block)[:, None]
    turn = np.arange(block)[None, :]
    tables = []
    for phase in range(FOLDED):
        angle = 2.0 * np.pi * ((RADIX * turn + phase) * place % length) / length
        cos, sin = np.cos(angle), np.sin(angle)
        tables.append(np.block([[cos, -sin], [sin, cos]]))
    table = np.stack(tables).astype(np.float32)
    high = table.astype(BF16)
    low = (table - high.astype(np.float32)).astype(BF16)
    return jnp.asarray(high), jnp.asarray(low)


def shift(value, step):
    length = value.shape[1]
    lane = lax.broadcasted_iota(jnp.int32, value.shape, 1)
    if step < 0:
        return jnp.where(lane == 0, 0.0, pltpu.roll(value, 1, 1))
    return jnp.where(lane == length - 1, 0.0, pltpu.roll(value, length - 1, 1))


def fold(value, phase, block):
    x0, x1, x2, x3 = [value[:, i * block : (i + 1) * block] for i in range(4)]
    if phase == 0:
        return (x0 + x2) + (x1 + x3)
    if phase == 4:
        return (x0 + x2) - (x1 + x3)
    if phase == 2:
        return jnp.concatenate([x0 - x2, x3 - x1], axis=1)
    slant, lean = (x1 - x3) * ROOT, (x1 + x3) * ROOT
    if phase == 1:
        return jnp.concatenate([x0 + slant, -x2 - lean], axis=1)
    return jnp.concatenate([x0 - slant, x2 - lean], axis=1)


def unfold(total_ref, value, phase, block):
    if phase == 0:
        terms = (value,) * 4
    elif phase == 4:
        terms = (value, -value, value, -value)
    else:
        real, imag = value[:, :block], value[:, block:]
        if phase == 2:
            terms = (real, -imag, -real, imag)
        elif phase == 1:
            terms = (real, ROOT * (real - imag), -imag, -ROOT * (real + imag))
        else:
            terms = (real, -ROOT * (real + imag), imag, ROOT * (real - imag))
    for i, term in enumerate(terms):
        cols = slice(i * block, (i + 1) * block)
        total_ref[:, cols] = term if phase == 0 else total_ref[:, cols] + term


def times(left_side, right_side, block, conj=False):
    a, b = left_side[:, :block], left_side[:, block:]
    c, d = right_side[:, :block], right_side[:, block:]
    if conj:
        d = -d
    return jnp.concatenate([a * c - b * d, a * d + b * c], axis=1)


def pair(phase):
    return 1.0 if phase in (0, 4) else 2.0


def depth(phase, block):
    return block if phase in (0, 4) else 2 * block


def mix(projected, taps, base, tables, after=()):
    own, length = projected.shape[1:]
    block = 2 * length // RADIX
    groups = base.shape[0]
    turns = block // groups
    if turns % 8:
        base = base.reshape(groups, FOLDED, turns, 2 * own)
        spectrum = pl.BlockSpec((groups, 1, turns, 2 * own), lambda i: (0, i, 0, 0))
    else:
        spectrum = pl.BlockSpec((groups, turns, 2 * own), lambda i: (0, i, 0))
    scale = 1.0 / math.sqrt(length)

    def kernel(p_ref, tap_ref, base_ref, th_ref, tl_ref, gated_ref, gating_ref, long_ref, vals_ref, spec_ref,
               mixed_ref, acc_ref, base_t):
        step = pl.program_id(0)

        @pl.when(step == 0)
        def _():
            for k in range(3):

                p = p_ref[k]
                tap = tap_ref[k]
                mixed = tap[:, 0:1] * shift(p, -1) + tap[:, 1:2] * p + tap[:, 2:3] * shift(p, 1)
                if k == 1:
                    gating_ref[...] = mixed
                else:
                    mixed_ref[k // 2 * own : (k // 2 + 1) * own] = mixed

        turned = base_ref[...].reshape(block, 2 * own).T
        base_t[:, :block] = turned[:own]
        base_t[:, block:] = turned[own:]

        for phase in range(FOLDED):

            @pl.when(step == phase)
            def _(phase=phase):
                deep = depth(phase, block)
                table = (th_ref[0, :deep], tl_ref[0, :deep])
                hats = dot(halves(fold(mixed_ref[...], phase, block)), table, NN)
                spec = base_t[...] + (pair(phase) * scale) * hats[:own]
                vals = hats[own:]
                spec_ref[0] = spec
                vals_ref[0] = vals
                unfold(acc_ref, dot(halves(times(spec, vals, block)), table, NT), phase, block)

        @pl.when(step == FOLDED - 1)
        def _():
            long_conv = acc_ref[...] * (0.5 / length)
            long_ref[...] = long_conv
            gated_ref[...] = gating_ref[...] * long_conv

    flat, hat = shaped(own, length), shaped(FOLDED, own, 2 * block)
    by_phase = lambda *shape: pl.BlockSpec((1,) + shape, lambda i, *_: (i,) + (0,) * len(shape))
    return call(
        kernel, "mix", 3 * 6 * own * 4 * length * length, 4 * own * length * 22,
        [projected, taps, base, *tables],
        [whole(3, own, length), whole(3, own, 3)]
        + [spectrum]
        + [by_phase(2 * block, 2 * block), by_phase(2 * block, 2 * block)],
        [flat, flat, flat, hat, hat],
        [whole(own, length)] * 3 + [by_phase(own, 2 * block)] * 2,
        grid=(FOLDED,),
        scratch=[
            pltpu.VMEM((2 * own, length), F32),
            pltpu.VMEM((own, length), F32),
            pltpu.VMEM((own, 2 * block), F32),
        ],
        after=after,
    )


def mix_back(places, d_gating, d_long, projected, taps, vals, spec, tables, after=()):
    seqs = len(projected)
    own, length = projected[0].shape[1:]
    block = vals[0].shape[2] // 2
    groups = lax.axis_size("batch")
    turns = block // groups
    slots = places.shape[1]
    scale = 1.0 / math.sqrt(length)

    def kernel(at_ref, dg_ref, dl_ref, tap_ref, *refs):
        p_refs, vals_refs, spec_refs, refs = refs[:seqs], refs[seqs : 2 * seqs], refs[2 * seqs : 3 * seqs], refs[3 * seqs :]
        th_ref, tl_ref, *refs = refs
        out_refs, (ker_ref, dtap_ref, long_ref, gating_ref, acc_ref) = refs[:seqs], refs[seqs:]
        step = pl.program_id(0)

        @pl.when(step == 0)
        def _():
            at = lax.broadcasted_iota(jnp.int32, (slots, length), 1)
            for i in range(seqs):
                pick = jnp.where(at == at_ref[i], 1.0, 0.0).astype(BF16)
                for source, target in ((dg_ref, gating_ref), (dl_ref, long_ref)):
                    high, low = halves(source[i])
                    target[i * own : (i + 1) * own] = lax.dot_general(
                        high, pick, (NN, ((), ())), preferred_element_type=F32
                    ) + lax.dot_general(low, pick, (NN, ((), ())), preferred_element_type=F32)

        for phase in range(FOLDED):

            @pl.when(step == phase)
            def _(phase=phase):
                deep = depth(phase, block)
                table = (th_ref[0, :deep], tl_ref[0, :deep])
                hats = dot(halves(fold(long_ref[...], phase, block)), table, NN) * (0.5 / length)
                both, kernel_sum = [], 0.0
                for i in range(seqs):
                    hat = hats[i * own : (i + 1) * own]
                    ker = times(hat, vals_refs[i][0], block, conj=True)
                    kernel_sum = kernel_sum + ker
                    both += [ker * (pair(phase) * scale), times(hat, spec_refs[i][0], block, conj=True)]
                turned = jnp.concatenate([kernel_sum[:, :block], kernel_sum[:, block:]], axis=0).T
                ker_ref[:, 0] = turned.reshape(groups, turns, 2 * own)
                unfold(acc_ref, dot(halves(jnp.concatenate(both, axis=0)), table, NT), phase, block)

        @pl.when(step == FOLDED - 1)
        def _():
            lane = lax.broadcasted_iota(jnp.int32, (own, 128), 1)
            for k in range(3):
                tap = tap_ref[k]
                sums = jnp.zeros((own, 128), F32)
                for i in range(seqs):
                    if k == 1:
                        grad = gating_ref[i * own : (i + 1) * own]
                    else:
                        at = 2 * i + k // 2
                        grad = acc_ref[at * own : (at + 1) * own]
                    p = p_refs[i][k]
                    out_refs[i][k] = tap[:, 0:1] * shift(grad, 1) + tap[:, 1:2] * grad + tap[:, 2:3] * shift(grad, -1)
                    for j, moved in enumerate((shift(p, -1), p, shift(p, 1))):
                        sums += jnp.where(lane == j, jnp.sum(moved * grad, axis=1, keepdims=True), 0.0)
                dtap_ref[k] = sums

    by_phase = lambda *shape: pl.BlockSpec((1,) + shape, lambda i: (i,) + (0,) * len(shape))
    flat = shaped(3, own, length)
    return call(
        kernel, "mix_back", seqs * 3 * 6 * own * 4 * length * length, seqs * 4 * own * length * 22,
        [places, d_gating, d_long, taps, *projected, *vals, *spec, *tables],
        [whole(seqs, slots, 1), whole(seqs, own, slots), whole(seqs, own, slots), whole(3, own, 3)]
        + [whole(3, own, length)] * seqs + [by_phase(own, 2 * block)] * (2 * seqs) + [by_phase(2 * block, 2 * block)] * 2,
        [flat] * seqs + [shaped(groups, FOLDED, turns, 2 * own), shaped(3, own, 128)],
        [whole(3, own, length)] * seqs
        + [pl.BlockSpec((groups, 1, turns, 2 * own), lambda i: (0, i, 0, 0)), whole(3, own, 128)],
        grid=(FOLDED,),
        scratch=[
            pltpu.VMEM((seqs * own, length), F32),
            pltpu.VMEM((seqs * own, length), F32),
            pltpu.VMEM((2 * seqs * own, length), F32),
        ],
        after=after,
    )


def add_mixer(x, gated, w_out, after=()):
    length, width = x.shape
    own = gated[0].shape[0]
    tokens = length // 2

    def kernel(x_ref, g0, g1, g2, g3, w0, w1, w2, w3, out_ref, wh, wl, gh, gl):
        @first
        def _():
            for d, ref in enumerate((w0, w1, w2, w3)):
                wh[d * own : (d + 1) * own], wl[d * own : (d + 1) * own] = halves(ref[...])

        for d, ref in enumerate((g0, g1, g2, g3)):
            gh[d * own : (d + 1) * own], gl[d * own : (d + 1) * own] = halves(ref[...])
        out_ref[...] = x_ref[...] + dot((gh[...], gl[...]), (wh[...], wl[...]), TN)

    rows = pl.BlockSpec((tokens, width), lambda i: (i, 0))
    (out,) = call(
        kernel, "add_mixer", 6 * length * width * width, 4 * (3 * length * width + width * width),
        [x, *gated, *w_out],
        [rows] + [pl.BlockSpec((own, tokens), lambda i: (0, i))] * 4 + [whole(own, width)] * 4,
        [shaped(length, width)], [rows], grid=(2,),
        scratch=[pltpu.VMEM((width, width), BF16)] * 2 + [pltpu.VMEM((width, tokens), BF16)] * 2,
        after=after,
    )
    return out


def gelu_parts(u):
    inner = math.sqrt(2.0 / math.pi) * (u + 0.044715 * (u * u * u))
    return 0.5 * (1.0 + jnp.tanh(inner))


def units_of(residual, w_units, after=()):
    length, width = residual.shape
    units = w_units[0].shape[1] // 2
    tokens = length // 4

    def kernel(r_ref, wh, wl, high_ref, low_ref):
        gate_up = []
        for i in range(2):
            rows = r_ref[i * tokens : (i + 1) * tokens]
            gate_up.append(dot(halves(normed(rows)[0]), (wh[...], wl[...]), NN))
        for i, v in enumerate(gate_up):
            at = slice(i * tokens, (i + 1) * tokens)
            high_ref[at], low_ref[at] = halves(v[:, :units] * gelu_parts(v[:, :units]) * v[:, units:])

    rows = lambda columns: pl.BlockSpec((2 * tokens, columns), lambda i: (i, 0))
    return call(
        kernel, "units_of", 12 * length * width * units, 4 * (2 * length * width + 2 * width * units),
        [residual, *w_units], [rows(width)] + [whole(width, 2 * units)] * 2,
        [shaped(length, units, dtype=BF16)] * 2, [rows(units)] * 2, grid=(2,), after=after,
    )


def down_of(hidden, w_down, s, after=()):
    length, units = hidden[0].shape
    width = w_down[0].shape[1]
    tokens = length // 4

    def kernel(s_ref, hh, hl, dh, dl, *out_refs):
        for i, out_ref in enumerate(out_refs):
            rows = pl.ds(pl.multiple_of((s_ref[0] ^ i) * tokens, tokens), tokens)
            out_ref[...] = dot((hh[rows], hl[rows]), (dh[...], dl[...]), NN)

    return call(
        kernel, "down_of", 6 * length * width * units, 4 * (2 * length * width + width * units),
        [*hidden, *w_down], [whole(length, units)] * 2 + [whole(units, width)] * 2,
        [shaped(tokens, width)] * 4, [whole(tokens, width)] * 4, scalars=[s.reshape(1)], after=after,
    )


def feed_forward(residual, w_units, w_down, s, after=()):
    length, width = residual.shape
    units = w_down[0].shape[0]
    tokens = length // 4

    def kernel(s_ref, r_ref, wh, wl, dh, dl, *out_refs):
        gate_up = []
        for i in range(4):
            rows = r_ref[pl.ds(pl.multiple_of((s_ref[0] ^ i) * tokens, tokens), tokens)]
            gate_up.append(dot(halves(normed(rows)[0]), (wh[...], wl[...]), NN))
        hidden = [halves(v[:, :units] * gelu_parts(v[:, :units]) * v[:, units:]) for v in gate_up]
        for both, out_ref in zip(hidden, out_refs):
            out_ref[...] = dot(both, (dh[...], dl[...]), NN)

    return call(
        kernel, "feed_forward", 18 * length * width * units, 4 * (2 * length * width + 3 * width * units),
        [residual, *w_units, *w_down],
        [whole(length, width)] + [whole(width, 2 * units)] * 2 + [whole(units, width)] * 2,
        [shaped(tokens, width)] * 4, [whole(tokens, width)] * 4,
        scalars=[s.reshape(1)], after=after,
    )


def chosen(at_ref, slots, length):
    lane = lax.broadcasted_iota(jnp.int32, (slots, length), 1)
    return jnp.where(lane == at_ref[...], 1.0, 0.0).astype(BF16)


def live_back(residual, x, gated, w_out, places, d_out, w_units, w_down, after=()):
    seqs = 1 + len(residual)
    length, width = x.shape
    own = gated[0].shape[0]
    slots = places.shape[1]
    units = w_down[0].shape[0]
    rows = seqs * slots

    def kernel(*refs):
        r_refs, refs = refs[: seqs - 1], refs[seqs - 1 :]
        x_ref, g_refs, w_refs, refs = refs[0], refs[1:5], refs[5:9], refs[9:]
        at_ref, o_ref, wh, wl, dh, dl, live_ref, n_ref, hid_ref, du_ref = refs
        for i, ref in enumerate((*r_refs, x_ref)):
            pick = chosen(at_ref.at[i], slots, length)
            live_ref[i * slots : (i + 1) * slots] = chosen_rows(pick, halves(ref[...]), NN)
        mixed = []
        for ref in g_refs:
            parts = [lax.dot_general(v, pick, (NT, ((), ())), preferred_element_type=F32) for v in halves(ref[...])]
            mixed.append(parts[0] + parts[1])
        weight = jnp.concatenate([ref[...] for ref in w_refs], axis=0)
        live_ref[rows - slots :] += dot(halves(jnp.concatenate(mixed, axis=0)), halves(weight), TN)
        n = normed(live_ref[...])[0]
        n_ref[...] = n
        gate_up = dot(halves(n), (wh[...], wl[...]), NN)
        d_hidden = dot(halves(o_ref[...]), (dh[...], dl[...]), NT)
        gate, up = gate_up[:, :units], gate_up[:, units:]
        half = gelu_parts(gate)
        slope = half + gate * 2.0 * half * (1.0 - half) * math.sqrt(2.0 / math.pi) * (1.0 + 0.134145 * (gate * gate))
        hid_ref[...] = gate * half * up
        d_units = jnp.concatenate([d_hidden * up * slope, d_hidden * (gate * half)], axis=1)
        du_ref[...] = d_units

    return call(
        kernel, "live_back", 30 * rows * width * units, 4 * (2 * length * width + 4 * width * units),
        [*residual, x, *gated, *w_out, places, d_out, *w_units, *w_down],
        [whole(length, width)] * seqs + [whole(own, length)] * 4 + [whole(own, width)] * 4
        + [whole(seqs, slots, 1), whole(rows, width)] + [whole(width, 2 * units)] * 2 + [whole(units, width)] * 2,
        [shaped(rows, width), shaped(rows, width), shaped(rows, units), shaped(rows, 2 * units)],
        [whole(rows, width), whole(rows, width), whole(rows, units), whole(rows, 2 * units)],
        after=after,
    )


def through_units(d_units, w_units, seqs, used, after=()):
    rows = d_units.shape[0]
    width, wide = w_units[0].shape
    slots = rows // seqs

    def kernel(u_ref, wh, wl, *out_refs):
        e = dot(halves(u_ref[...]), (wh[...], wl[...]), NT)
        for i, out_ref in enumerate(out_refs):
            out_ref[...] = e[i * slots : i * slots + used]

    return call(
        kernel, "through_units", 6 * rows * width * wide, 4 * (rows * wide + width * wide),
        [d_units, *w_units], [whole(rows, wide)] + [whole(width, wide)] * 2,
        [shaped(used, width)] * seqs, [whole(used, width)] * seqs, after=after,
    )


def unit_grads(normed_live, d_units, hidden, d_out, shards, after=()):
    slots, width = normed_live.shape
    units = hidden.shape[1]
    groups = lax.axis_size("batch")
    rows = width // groups // shards
    down = units // groups

    def kernel(n_ref, u_ref, h_ref, o_ref, out_ref):
        @pl.when(pl.program_id(0) < 2)
        def _():
            part = dot(halves(n_ref[...]), halves(u_ref[...]), TN)
            for j in range(groups):
                for k in range(shards):
                    at = (k * groups + j) * rows
                    out_ref[j, k * rows : (k + 1) * rows] = part[at : at + rows]

        @pl.when(pl.program_id(0) == 2)
        def _():
            part = dot(halves(h_ref[...]), halves(o_ref[...]), TN)
            for j in range(groups):
                out_ref[j] = part[j * down : (j + 1) * down]

    (out,) = call(
        kernel, "unit_grads", 18 * slots * width * units, 4 * 3 * width * units,
        [normed_live, d_units, hidden, d_out],
        [
            whole(slots, width),
            pl.BlockSpec((slots, units), lambda i: (0, jnp.minimum(i, 1))),
            whole(slots, units),
            whole(slots, width),
        ],
        [shaped(groups, shards * rows, 2 * units + width)],
        [pl.BlockSpec((groups, shards * rows, width), lambda i: (0, 0, i))],
        grid=(3,), after=after,
    )
    return out


def live_mix(live, d_out, e_terms, w_out, gating, long_conv, places, after=()):
    seqs = len(gating)
    own, length = gating[0].shape
    rows, width = live.shape
    slots = rows // seqs
    used = e_terms[0].shape[0]

    def kernel(live_ref, o_ref, *refs):
        e_refs, w_ref, refs = refs[: 2 * seqs], refs[2 * seqs], refs[2 * seqs + 1 :]
        g_refs, l_refs, refs = refs[:seqs], refs[seqs : 2 * seqs], refs[2 * seqs :]
        at_ref, res_ref, dw_ref, dg_ref, dl_ref, e_all, pick_ref = refs
        e_all[...] = jnp.zeros((rows, width), F32)
        for i in range(seqs):
            e_all[i * slots : i * slots + used] = e_refs[i][...] + e_refs[seqs + i][...]
        n, inverse = normed(live_ref[...])
        e = e_all[...]
        along = jnp.mean(e * n, axis=-1, keepdims=True)
        res_ref[...] = o_ref[...] + (e - jnp.mean(e, axis=-1, keepdims=True) - n * along) * inverse
        d_res = halves(res_ref[...])
        d_gated = dot(halves(w_ref[...]), d_res, NT)
        for i in range(seqs):
            pick = chosen(at_ref.at[i], slots, length)
            at = slice(i * slots, (i + 1) * slots)
            gate = [lax.dot_general(v, pick, (NT, ((), ())), preferred_element_type=F32) for v in halves(g_refs[i][...])]
            lng = [lax.dot_general(v, pick, (NT, ((), ())), preferred_element_type=F32) for v in halves(l_refs[i][...])]
            gate, lng = gate[0] + gate[1], lng[0] + lng[1]
            dg_ref[i] = d_gated[:, at] * lng
            dl_ref[i] = d_gated[:, at] * gate
            pick_ref[:, at] = gate * lng
        dw_ref[...] = dot(halves(pick_ref[...]), d_res, NN)

    return call(
        kernel, "live_mix", 20 * rows * width * own, 4 * (4 * own * length + 4 * rows * width),
        [live, d_out, *e_terms, w_out, *gating, *long_conv, places],
        [whole(rows, width)] * 2 + [whole(used, width)] * (2 * seqs) + [whole(own, width)]
        + [whole(own, length)] * (2 * seqs) + [whole(seqs, slots, 1)],
        [shaped(rows, width), shaped(own, width), shaped(seqs, own, slots), shaped(seqs, own, slots)],
        [whole(rows, width), whole(own, width), whole(seqs, own, slots), whole(seqs, own, slots)],
        scratch=[pltpu.VMEM((rows, width), F32), pltpu.VMEM((own, rows), F32)],
        after=after,
    )


def project_back(d_projected, n_both, w_turned, w_sum, s, after=()):
    channels, length = d_projected.shape
    width = n_both[0].shape[1]
    tokens = length // 4

    def kernel(s_ref, d_ref, nh, nl, wh, wl, *refs):
        sum_refs, e_refs, dw_ref, ph, pl_ = refs[:-7], refs[-7:-3], refs[-3], refs[-2], refs[-1]
        ph[...], pl_[...] = halves(d_ref[...])
        part = dot((ph[...], pl_[...]), (nh[...], nl[...]), NN)
        dw_ref[...] = sum_refs[0][...] + part if sum_refs else part
        for i, e_ref in enumerate(e_refs):
            at = pl.ds(pl.multiple_of((s_ref[0] ^ i) * tokens, tokens), tokens)
            e_ref[...] = dot((ph[:, at], pl_[:, at]), (wh[...], wl[...]), TN)

    return call(
        kernel, "project_back", 12 * length * width * channels,
        4 * (2 * length * width + channels * (length + 3 * width)),
        [d_projected, *n_both, *w_turned, *w_sum],
        [whole(channels, length)] + [whole(length, width)] * 2 + [whole(channels, width)] * (2 + len(w_sum)),
        [shaped(tokens, width)] * 4 + [shaped(channels, width)],
        [whole(tokens, width)] * 4 + [whole(channels, width)],
        scratch=[pltpu.VMEM((channels, length), BF16)] * 2, scalars=[s.reshape(1)], after=after,
    )


def turn_back(turned, placed, w_out_part, after=()):
    channels, width = turned.shape
    own = w_out_part.shape[0]
    groups = lax.axis_size("batch")
    shards = width // own
    rows = own // groups
    wide = -(-(channels + 1) // 128) * 128

    def kernel(w_ref, p_ref, o_ref, out_ref, flat_ref):
        flat_ref[:channels] = w_ref[...]
        flat_ref[channels:] = jnp.zeros((wide - channels, width), F32)
        back = flat_ref[...].T
        for j in range(groups):
            for k in range(shards):
                at = (k * groups + j) * rows
                to = slice(k * rows, (k + 1) * rows)
                out_ref[j, to, : wide - 128] = back[at : at + rows, : wide - 128]
                out_ref[j, to, wide - 128 : wide] = back[at : at + rows, wide - 128 :] + p_ref[at : at + rows]
                out_ref[j, to, wide:] = o_ref[j * rows : (j + 1) * rows, k * own : (k + 1) * own]

    shape = (groups, shards * rows, wide + own)
    (out,) = call(
        kernel, "turn_back", 0, 8 * width * wide, [turned, placed, w_out_part],
        [whole(channels, width), whole(width, 128), whole(own, width)], [shaped(*shape)], [whole(*shape)],
        scratch=[pltpu.VMEM((wide, width), F32)], after=after,
    )
    return out


def finish(which, e_terms, x, d_residual, places, s, held, after=()):
    tokens, width = e_terms[0].shape
    seqs, slots, _ = places.shape

    def kernel(s_ref, e0, e1, e2, e3, x_ref, d_ref, at_ref, *refs):
        out_ref = refs[-1]
        e = (e0[...] + e1[...]) + (e2[...] + e3[...])
        n, inverse = normed(x_ref[0])
        along = jnp.mean(e * n, axis=-1, keepdims=True)
        here = lax.broadcasted_iota(jnp.int32, (slots, tokens), 1) + s_ref[0] * tokens
        pick = jnp.where(here == at_ref[0], 1.0, 0.0).astype(BF16)
        direct = chosen_rows(pick, halves(d_ref[...]), TN)
        out_ref[0] = (e - jnp.mean(e, axis=-1, keepdims=True) - n * along) * inverse + direct

    inputs = [*e_terms, x, d_residual, places, *held]
    one = pl.BlockSpec((1, tokens, width), lambda i, *_: (which, 0, 0))
    return pl.pallas_call(
        kernel,
        name="finish",
        out_shape=shaped(seqs, tokens, width),
        grid_spec=pltpu.PrefetchScalarGridSpec(
            num_scalar_prefetch=1,
            grid=(1,),
            in_specs=[whole(tokens, width)] * 4
            + [one, pl.BlockSpec((slots, width), lambda i, *_: (which, 0))]
            + [pl.BlockSpec((1, slots, 1), lambda i, *_: (which, 0, 0))]
            + [pl.BlockSpec(memory_space=pl.ANY)] * len(held),
            out_specs=one,
        ),
        input_output_aliases={len(inputs): 0} if held else {},
        compiler_params=pltpu.CompilerParams(vmem_limit_bytes=VMEM),
        cost_estimate=pl.CostEstimate(flops=10**6, bytes_accessed=10**6, transcendentals=0),
    )(s.reshape(1), *inputs)


def lanes_summed(value):
    return lax.dot_general(
        jnp.ones((8, value.shape[1]), F32), value, (NT, ((), ())),
        precision=lax.Precision.HIGHEST, preferred_element_type=F32,
    )


def weight_grads(pieces, s, gain_one, gain_two, w_in, w_gate, w_up, own, units):
    rows, columns = pieces[0].shape
    start = columns - 2 * units
    shards = len(pieces)

    def kernel(s_ref, *refs):
        p_refs, refs = refs[:shards], refs[shards:]
        one_ref, two_ref, wi_ref, wg_ref, wu_ref, di_ref, dg_ref, du_ref, g1_ref, g2_ref, tap_ref = refs
        one, two = one_ref[...], two_ref[...]
        lane = 3 * own // 128 * 128
        tap_ref[...] = (p_refs[0][:, lane:start] + p_refs[1][:, lane:start]) + (
            p_refs[2][:, lane:start] + p_refs[3][:, lane:start]
        )
        for index in range(shards):

            @pl.when(s_ref[0] == index)
            def _(index=index):
                sum_one = jnp.zeros((8, rows), F32)
                sum_two = jnp.zeros((8, rows), F32)
                for d, p_ref in enumerate(p_refs):
                    k = index ^ d
                    for j in range(3):
                        at = slice((j * shards + k) * own, (j * shards + k + 1) * own)
                        part = p_ref[:, j * own : (j + 1) * own]
                        sum_one += lanes_summed(wi_ref[:, at] * part)
                        di_ref[:, at] = one * part
                    at = slice(k * units, (k + 1) * units)
                    for j, (w_ref, d_ref) in enumerate(((wg_ref, dg_ref), (wu_ref, du_ref))):
                        part = p_ref[:, start + j * units : start + (j + 1) * units]
                        sum_two += lanes_summed(w_ref[:, at] * part)
                        d_ref[:, at] = two * part
                g1_ref[...] = sum_one
                g2_ref[...] = sum_two

    inputs = [*pieces, gain_one[:, None], gain_two[:, None], w_in, w_gate, w_up]
    wide = start - 3 * own // 128 * 128
    outs = [w_in.shape, w_gate.shape, w_up.shape, (8, rows), (8, rows), (rows, wide)]
    return call(
        kernel, "weight_grads", 0, 0, inputs, [whole(*v.shape) for v in inputs],
        [shaped(*v) for v in outs], [whole(*v) for v in outs], scalars=[s.reshape(1)],
    )


def norm_pull(n, inverse, grad):
    along = jnp.mean(grad * n, axis=-1, keepdims=True)
    return (grad - jnp.mean(grad, axis=-1, keepdims=True) - n * along) * inverse


def together(*values):
    return lax.optimization_barrier(values)


def body(
    inputs,
    gain_one,
    w_in,
    conv_weight,
    kernel,
    w_out,
    gain_two,
    w_gate,
    w_up,
    w_down,
    mask_positions,
    mask_counts,
    grad_rows,
):
    shards = lax.axis_size("seq")
    groups = lax.axis_size("batch")
    s = lax.axis_index("seq")
    seqs, tokens, width = inputs.shape
    length = tokens * shards
    freqs = 2 * length
    own = width // shards
    rows = w_in.shape[0]
    units = w_gate.shape[1] // shards
    count = conv_weight.shape[1]
    extra = 3 * count // rows
    tables = phase_tables(freqs)

    slots = mask_positions.shape[1]
    pad = -slots % 128
    live = jnp.arange(slots, dtype=jnp.int32) < mask_counts[:, None]
    places = jnp.pad(jnp.where(live, mask_positions, -1), ((0, 0), (0, pad)), constant_values=-1)
    d_out = jnp.pad(jnp.where(live[:, :, None], grad_rows, 0.0), ((0, 0), (0, pad), (0, 0)))
    d_out = d_out.reshape(-1, width)
    places = places[:, :, None]

    w_pre = (gain_one[:, None] * w_in).reshape(rows, 3, shards, own).transpose(0, 2, 1, 3)
    w_pre = w_pre.reshape(rows, shards, 3 * own)
    carried = jnp.broadcast_to(conv_weight.reshape(rows, 1, extra), (rows, shards, extra))
    split = 3 * own + extra
    sent = columns_out(jnp.concatenate([w_pre, carried], axis=2), s)
    sent, x_now, kernel_now, places, d_out = together(sent, inputs, kernel, places, d_out)
    w_out_turned = w_out.reshape(rows, shards, own).transpose(1, 0, 2).reshape(shards * rows, own)
    w_pre = over_batch(jnp.concatenate([sent.reshape(shards * rows, split), w_out_turned], axis=1))
    w_pre = w_pre.reshape(groups, shards, rows, split + own)

    near = [swap(x_now, "seq", 1), swap(x_now, "seq", 2)]
    wide = kernel_now.reshape(2, -1, RADIX, own)
    mirror = [(i, groups - 1 - i) for i in range(groups)]
    folded = lax.ppermute(wide[:, ::-1, :4:-1], "batch", mirror)
    folded = fold_base(wide, folded)
    near, folded, w_gate_now, w_up_now = together(near, folded, w_gate, w_up)
    base = over_batch(folded)

    from_one, from_two, w_gate_now, w_up_now = together(near[0][0], near[1][1], w_gate_now, w_up_now)
    far = [swap(from_one, "seq", 2), swap(from_two, "seq", 1)]
    w_units = jnp.stack([gain_two[:, None] * w_gate_now, gain_two[:, None] * w_up_now], axis=1)
    w_units = w_units.reshape(rows, 2, shards, units).transpose(0, 2, 1, 3).reshape(rows, shards, 2 * units)
    *w_turned, w_out_own = turn_in(w_pre, 3 * own, split)
    taps = w_pre[..., 3 * own : split]
    far, w_units, w_turned, w_out_own, taps, w_down_now = together(
        far, columns_out(w_units, s), w_turned, w_out_own, taps, w_down
    )
    w_units = over_batch(w_units.reshape(shards * rows, 2 * units))
    w_down_own = over_batch(w_down_now).reshape(units, width)

    taps = taps.reshape(groups, shards, 3, count).transpose(2, 1, 0, 3)
    taps = lax.dynamic_index_in_dim(taps.reshape(3, 3, shards, own), s, axis=2, keepdims=False)
    taps = taps.transpose(1, 2, 0)

    def first_half(i, after=()):
        x_i, *n_i = arrange(i, (inputs, *near), far[i], s, after=after)
        return x_i, n_i, project(w_turned, n_i).reshape(3, own, length)

    x_0, n_0, p_0 = first_half(0)
    w_out_there, (gated_0, *mixed_0), x_0, n_0 = together(from_others(w_out_own), mix(p_0, taps, base, tables), x_0, n_0)
    x_1, n_1, p_1 = first_half(1, (gated_0,))
    there_0, (gated_1, *mixed_1), x_1, n_1 = together(from_others(gated_0), mix(p_1, taps, base, tables), x_1, n_1)
    n_one, projected = (n_0, n_1), (p_0, p_1)
    gating, long_conv, vals, spec = zip(mixed_0, mixed_1)
    w_out_pieces = (w_out_own, *w_out_there)

    residual_0 = add_mixer(x_0, (gated_0, *there_0), w_out_pieces, after=(gated_1,))
    w_units = split_units(w_units.reshape(groups, shards, rows, 2 * units), after=(residual_0,))
    hidden_0 = units_of(residual_0, w_units)
    w_down_own = split_down(w_down_own, after=(hidden_0[0],))
    down_0 = down_of(hidden_0, w_down_own, s)
    there_1, down_0, residual_0, w_units, w_down_own = together(
        from_others(gated_1), down_0, residual_0, w_units, w_down_own
    )

    lived = live_back(
        (residual_0,), x_1, (gated_1, *there_1), w_out_pieces, places, d_out, w_units, w_down_own
    )
    live_rows, n_live, hidden, d_units = lived
    unit_part = unit_grads(n_live, d_units, hidden, d_out, shards)
    out_0 = [down_0[0], swap(down_0[1], "seq", 1), swap(down_0[2], "seq", 2)]
    live_rows, d_units, unit_part, out_0 = together(live_rows, d_units, unit_part, out_0)
    unit_sums = sum_over_batch(unit_part)

    e_two = through_units(d_units, w_units, seqs, slots, after=(unit_part,))
    residual_1 = add_mixer(x_1, (gated_1, *there_1), w_out_pieces, after=(e_two[0],))
    e_there, residual_1 = together([swap(e, "seq", 1 + i) for i, e in enumerate(e_two)], residual_1)
    residual = (residual_0, residual_1)
    e_two = [e + there for e, there in zip(e_two, e_there)]
    down_1 = feed_forward(residual_1, w_units, w_down_own, s)
    e_there, down_1 = together([swap(e, "seq", 2 - i) for i, e in enumerate(e_two)], down_1)
    e_terms = [*e_two, *e_there]

    d_residual, w_out_part, d_gating, d_long = live_mix(live_rows, d_out, e_terms, w_out_own, gating, long_conv, places)
    *d_projected, kernel_part, taps_part = mix_back(
        places, d_gating, d_long, projected, taps, vals, spec, tables
    )
    taps_part = taps_part[:, :, :3]
    out_0 += [swap(down_0[3], "seq", 3)]
    out_1 = [down_1[0], swap(down_1[1], "seq", 1), swap(down_1[2], "seq", 2)]
    d_projected, kernel_part, taps_part, d_residual, w_out_part, out_0, out_1 = together(
        d_projected, kernel_part, taps_part, d_residual, w_out_part, out_0, out_1
    )

    e_0 = project_back(d_projected[0].reshape(3 * own, length), n_0, w_turned, (), s)
    out_1 += [swap(down_1[3], "seq", 3)]
    (*e_0, w_in_part), out_1, unit_sums, kernel_part = together(e_0, out_1, unit_sums, kernel_part)
    kernel_sum = sum_over_batch(kernel_part.reshape(groups, -1, 2 * own))

    e_1 = project_back(d_projected[1].reshape(3 * own, length), n_1, w_turned, (w_in_part,), s)
    placed = jnp.zeros((3, 3, shards, own), F32)
    taps_part = taps_part.transpose(2, 0, 1)[:, :, None]
    placed = lax.dynamic_update_slice(placed, taps_part, (0, 0, s, 0))
    placed = placed.reshape(3, shards, groups, count).transpose(1, 2, 0, 3).reshape(width, extra)
    free = 3 * own % 128
    placed = jnp.pad(placed, ((0, 0), (free, 128 - free - extra)))
    w_in_part = turn_back(e_1[4], placed, w_out_part)
    e_there = [swap(e_0[1], "seq", 1), swap(e_0[2], "seq", 2)]
    outputs = [
        added(out) + lax.dynamic_slice_in_dim(residual[i], s * tokens, tokens, axis=0)
        for i, out in enumerate((out_0, out_1))
    ]
    e_there, e_1, w_in_part = together(e_there, e_1[:4], w_in_part)
    w_in_sum = sum_over_batch(w_in_part)

    e_0 = [e_0[0], *e_there, swap(e_0[3], "seq", 3)]
    input_grad = finish(0, e_0, inputs, d_residual, places, s, ())
    outputs = jnp.stack(
        [
            added(out) + lax.dynamic_slice_in_dim(residual[i], s * tokens, tokens, axis=0)
            for i, out in enumerate((out_0, out_1))
        ]
    )
    kernel_sum = kernel_sum.reshape(FOLDED, -1, 2, own).transpose(2, 1, 0, 3)
    mirrored = lax.ppermute(kernel_sum[:, ::-1, 3:0:-1], "batch", mirror)
    e_1, w_in_sum, mirrored, outputs, input_grad = together(to_others(e_1), w_in_sum, mirrored, outputs, input_grad)

    w_back = jnp.concatenate([w_in_sum[:, :-own], unit_sums[:, : 2 * units]], axis=1)
    w_back = columns_there(w_back.reshape(shards, rows, -1), s)
    mirrored = jnp.stack([mirrored[0], -mirrored[1]])
    kernel_grad = jnp.concatenate([kernel_sum, mirrored], axis=2).reshape(kernel.shape)
    input_grad = finish(1, e_1, inputs, d_residual, places, s, (input_grad,))
    w_out_sum = w_in_sum[:, -own:].reshape(shards, rows, own).transpose(1, 0, 2).reshape(w_out.shape)
    w_down_sum = unit_sums[:, 2 * units :].reshape(w_down.shape)
    w_back, kernel_grad, input_grad, w_out_sum, w_down_sum = together(
        w_back, kernel_grad, input_grad, w_out_sum, w_down_sum
    )
    w_in_sum, w_gate_sum, w_up_sum, gain_one_sum, gain_two_sum, taps_sum = weight_grads(
        w_back, s, gain_one, gain_two, w_in, w_gate, w_up, own, units
    )
    taps_sum = taps_sum[:, free : free + extra].reshape(conv_weight.shape)

    return (
        outputs,
        input_grad,
        gain_one_sum[0],
        w_in_sum,
        taps_sum,
        kernel_grad,
        w_out_sum,
        gain_two_sum[0],
        w_gate_sum,
        w_up_sum,
        w_down_sum,
    )


def solution(mesh):
    split = ("seq", "batch")
    placed = (
        P("batch", "seq", None),
        P(split),
        P(split, None),
        P(None, split),
        P(None, "batch", "seq"),
        P(split, None),
        P(split),
        P(split, None),
        P(split, None),
        P(split, None),
        P("batch", None),
        P("batch"),
        P("batch", None, None),
    )
    return jax.shard_map(
        body,
        mesh=mesh,
        in_specs=placed,
        out_specs=(
            P("batch", "seq", None),
            P("batch", "seq", None),
            P(split),
            P(split, None),
            P(None, split),
            P(None, "batch", "seq"),
            P(split, None),
            P(split),
            P(split, None),
            P(split, None),
            P(split, None),
        ),
        check_vma=False,
    )
```
